32 devices in a mesh: dp: 4 (over y, core), tensor: 8 (over z, x).
Axes of the slice: x: 2, y: 2, z: 4, core: 2. Of those that a mesh axis runs over, the one named last changes fastest.
Arguments:
- inputs: bfloat16 [3, 4, 1024, 1024], P(None, 'dp', 'tensor'), may hold values from -6 to 6
- doc_starts: int32 [3, 4, 4], P(None, 'dp'), may hold values from 0 to 1023, as said below
- w_qkv: bfloat16 [3, 1024, 1024], P(None, 'dp', 'tensor'), may hold values from -0.1875 to 0.1875
- w_out: bfloat16 [1024, 1024], P('tensor', 'dp'), may hold values from -0.1875 to 0.1875
- w_up: bfloat16 [1024, 4096], P('dp', 'tensor'), may hold values from -0.1875 to 0.1875
- w_down: bfloat16 [4096, 1024], P('tensor', 'dp'), may hold values from -0.09375 to 0.09375
- norm_gains: bfloat16 [4, 1024], P(None, 'dp'), may hold values from 0.25 to 1.75
- norm_biases: bfloat16 [4, 1024], P(None, 'dp'), may hold values from -3 to 3
- cotangent: bfloat16 [3, 4, 1024, 1024], P(None, 'dp', 'tensor'), may hold values from -6 to 6
Outputs:
- outputs: bfloat16 [3, 4, 1024, 1024], P(None, 'dp', 'tensor')
- inputs_grad: float32 [3, 4, 1024, 1024], P(None, 'dp', 'tensor')
- qkv_grad: float32 [3, 1024, 1024], P(None, 'dp', 'tensor')
- out_grad: float32 [1024, 1024], P('tensor', 'dp')
- up_grad: float32 [1024, 4096], P('dp', 'tensor')
- down_grad: float32 [4096, 1024], P('tensor', 'dp')
- gains_grad: float32 [4, 1024], P(None, 'dp')
- biases_grad: float32 [4, 1024], P(None, 'dp')
The draws below stay inside these ranges and needn't reach their ends.
Inputs may be any that keep to these rules, and one draw needn't show every extreme that they name: `doc_starts`: each row's 4 document starts rise strictly and the first is 0; one document of each row, which one is drawn, begins before token 128 and has its last token at 896 or later; every other document has fewer than 128 tokens; in every draw some row has a document that starts at token 1023.
All inputs are finite; a program needn't handle non-finite values.
Results may differ from the reference program's by a relative error of at most 0.014.
Values may be sent and summed in bfloat16 or wider, within the bound.
No kernel may reach another device: no remote copies, remote signals or barrier semaphores. Data moves between devices by JAX's collectives and lax.ppermute only.
A program may use at most 192 MiB of HBM per device.

```python
import math
import jax
import jax.numpy as jnp
from jax import lax

D = 1024
H = 16
HD = 64
FF = 4096
LEN = 1024
MICRO = 3
NDOC = 4
ROWS = 4
SHARD = 128


def draw_doc_starts(key, part):
    key = jax.random.fold_in(key, 11)
    row_count = MICRO * ROWS

    def one_row(row_key, first_row):
        pick_key, lower_key, upper_key, other_key = jax.random.split(row_key, 4)
        chosen_any = jax.random.randint(pick_key, (), 0, NDOC)
        chosen_first = jax.random.randint(other_key, (), 0, NDOC - 1)
        chosen = jnp.where(first_row, chosen_first, chosen_any)
        lower = jnp.sort(jax.random.permutation(lower_key, SHARD - 1)[:NDOC - 1]) + 1
        upper = jnp.sort(jax.random.permutation(upper_key, SHARD - 1)[:NDOC - 1]) + (LEN - SHARD + 1)
        slot_index = jnp.arange(NDOC - 1)
        upper = jnp.where(first_row & (slot_index == NDOC - 2), LEN - 1, upper)
        boundaries = jnp.where(slot_index < chosen, lower, upper).astype(jnp.int32)
        return jnp.concatenate([jnp.zeros((1,), jnp.int32), boundaries])
    first_flags = jnp.arange(row_count) == 0
    all_rows = jax.vmap(one_row)(jax.random.split(key, row_count), first_flags)
    return all_rows.reshape(MICRO, ROWS, NDOC)


def block_scale(stream_key, extent, cuts, low, largest):
    def one(dim, parts):
        heights = jax.random.uniform(jax.random.fold_in(jax.random.fold_in(stream_key, 6), dim), (parts,), jnp.float32, low / len(cuts), largest / len(cuts))
        return jnp.repeat(jnp.exp(heights), extent[dim] // parts).reshape((-1,) + (1,) * (len(extent) - dim - 1))

    factor_of = one(*cuts[0])
    for cut in cuts[1:]:
        factor_of = factor_of * one(*cut)
    return factor_of


def gaussian(own_key, shape, spread, limit, pieces=(), kind=jnp.bfloat16):
    level = block_scale(own_key, shape, pieces, -0.22, 0.18) if pieces else 1.0
    values = jax.random.normal(own_key, shape, jnp.float32) * spread * level
    return jnp.minimum(jnp.maximum(values, -limit), limit).astype(kind)


def setup_inputs(seed: int = 0) -> dict:
    key_list = jax.random.split(jax.random.key(seed), 10)
    return {
        "inputs": gaussian(key_list[0], (MICRO, ROWS, LEN, D), 1.0, 6.0, ((1, 4), (2, 8))),
        "doc_starts": draw_doc_starts(jax.random.fold_in(key_list[9], 71), 0),
        "w_qkv": gaussian(key_list[2], (3, D, H * HD), D ** -0.5, 0.1875, ((1, 4), (2, 8))),
        "w_out": gaussian(key_list[3], (H * HD, D), (H * HD) ** -0.5, 0.1875, ((0, 8), (1, 4))),
        "w_up": gaussian(key_list[4], (D, FF), D ** -0.5, 0.1875, ((0, 4), (1, 8))),
        "w_down": gaussian(key_list[5], (FF, D), FF ** -0.5, 0.09375, ((0, 8), (1, 4))),
        "norm_gains": jnp.clip(1.0 + 0.15 * jax.random.normal(key_list[6], (4, D), jnp.float32), 0.25, 1.75).astype(jnp.bfloat16),
        "norm_biases": gaussian(key_list[7], (4, D), 0.5, 3.0, ((1, 4),)),
        "cotangent": gaussian(key_list[8], (MICRO, ROWS, LEN, D), 1.0, 6.0, ((1, 4), (2, 8))),
    }


@jax.custom_vjp
def low(v):
    return lax.optimization_barrier(v.astype(jnp.bfloat16)).astype(jnp.float32)

@jax.custom_vjp
def low_back(v):
    return v

def low_keep(v):
    return (low(v), None)

def low_pass(kept, grad):
    return (grad,)

def back_keep(v):
    return (v, None)

def back_low(kept, grad):
    return (low(grad),)
low.defvjp(low_keep, low_pass)
low_back.defvjp(back_keep, back_low)
EPSILON = 1e-05

def layer_norm(values, gain, shift):
    average = lax.optimization_barrier(jnp.mean(values, axis=-1, keepdims=True))
    centred = values - average
    variance = lax.optimization_barrier(jnp.mean(centred * centred, axis=-1, keepdims=True))
    return centred * lax.rsqrt(variance + EPSILON) * gain + shift

def rotate(values, angles):
    half_dim = values.shape[-1] // 2
    lower_half = values[..., :half_dim]
    upper_half = values[..., half_dim:]
    cosines = jnp.cos(angles)
    sine_part = jnp.sin(angles)
    return jnp.concatenate([lower_half * cosines - upper_half * sine_part, upper_half * cosines + lower_half * sine_part], axis=-1)

def doc_layout(starts, length):
    token_index = jnp.arange(length, dtype=jnp.int32)
    inside = token_index[:, None] >= starts[None, :]
    segment = lax.optimization_barrier(jnp.sum(inside.astype(jnp.int32), axis=1))
    begins = lax.optimization_barrier(jnp.max(jnp.where(inside, starts[None, :], 0), axis=1))
    return (segment, token_index - begins)

def rotary_angles(position, head_dim):
    frequency = jnp.exp(jnp.arange(head_dim // 2, dtype=jnp.float32) * (-2.0 * math.log(10000.0) / head_dim))
    return position.astype(jnp.float32)[..., None] * frequency

def block_forward(parameters, sequence, starts):
    w_qkv, w_out, w_up, w_down, gain_rows, shift_rows = parameters
    highest = lax.Precision.HIGHEST
    length = sequence.shape[0]
    segment, position = doc_layout(starts, length)
    angles = rotary_angles(position, HD)
    normed1 = low(layer_norm(sequence, gain_rows[0], shift_rows[0]))
    projected = low_back(jnp.einsum('td,cde->cte', normed1, w_qkv, precision=highest))
    projected = projected.reshape(3, length, H, HD).transpose(0, 2, 1, 3)
    queries = low(rotate(projected[0], angles))
    key_rows = low(rotate(projected[1], angles))
    values = low(projected[2])
    block_len = min(512, length)
    score_scale = 1.0 / math.sqrt(HD)

    def attend(number):
        offset = number * block_len
        q_block = lax.dynamic_slice_in_dim(queries, offset, block_len, 1)
        query_pos = offset + jnp.arange(block_len, dtype=jnp.int32)
        query_seg = lax.dynamic_slice_in_dim(segment, offset, block_len, 0)
        key_pos = jnp.arange(length, dtype=jnp.int32)
        allowed = (key_pos[None, :] <= query_pos[:, None]) & (segment[None, :] == query_seg[:, None])
        scores = low_back(score_scale * jnp.einsum('hqe,hke->hqk', q_block, key_rows, precision=highest))
        scores = jnp.where(allowed[None], scores, -1e+30)
        probs = low(jax.nn.softmax(scores, axis=-1))
        return low_back(low(jnp.einsum('hqk,hke->hqe', probs, values, precision=highest)))
    blocks = lax.map(jax.checkpoint(attend), jnp.arange(length // block_len, dtype=jnp.int32))
    attended = blocks.transpose(0, 2, 1, 3).reshape(length, H * HD)
    branch1 = low_back(jnp.dot(attended, w_out, precision=highest))
    hidden = sequence + layer_norm(branch1, gain_rows[1], shift_rows[1])
    normed2 = low(layer_norm(hidden, gain_rows[2], shift_rows[2]))
    up_act = low_back(jnp.dot(normed2, w_up, precision=highest))
    activated = low(jax.nn.gelu(up_act, approximate=True))
    branch2 = low_back(jnp.dot(activated, w_down, precision=highest))
    return hidden + layer_norm(branch2, gain_rows[3], shift_rows[3])

def reference(inputs, doc_starts, w_qkv, w_out, w_up, w_down, norm_gains, norm_biases, cotangent):
    parameters = tuple((item.astype(jnp.float32) for item in (w_qkv, w_out, w_up, w_down, norm_gains, norm_biases)))

    def one_sequence(running, item):
        sequence, starts, upstream = item
        result, pull_back = jax.vjp(lambda params_in, seq_in: block_forward(params_in, seq_in, starts), parameters, sequence.astype(jnp.float32))
        grad_params, grad_seq = pull_back(upstream.astype(jnp.float32))
        running = jax.tree.map(jnp.add, running, grad_params)
        return (running, (result.astype(jnp.bfloat16), grad_seq))
    zeros_init = jax.tree.map(jnp.zeros_like, parameters)
    running, (results, grads_in) = lax.scan(one_sequence, zeros_init, (inputs.reshape(MICRO * ROWS, LEN, D), doc_starts.reshape(MICRO * ROWS, NDOC), cotangent.reshape(MICRO * ROWS, LEN, D)))
    shape_full = (MICRO, ROWS, LEN, D)
    return (results.reshape(shape_full), grads_in.reshape(shape_full), running[0], running[1], running[2], running[3], running[4], running[5])
```

```python
import math

import jax
import jax.numpy as jnp
from jax import lax
from jax.sharding import Mesh, PartitionSpec as P

HD = 64
EPSILON = 1e-05
F32 = jnp.float32
BF16 = jnp.bfloat16
CHIPS = ("y", "z", "x")
SEQ = ("z", "x")
SWAP = [(0, 1), (1, 0)]


def ln_forward(values, gain, shift):
    average = jnp.mean(values, axis=-1, keepdims=True)
    centred = values - average
    variance = jnp.mean(centred * centred, axis=-1, keepdims=True)
    scale = lax.rsqrt(variance + EPSILON)
    xhat = centred * scale
    return xhat * gain + shift, xhat, scale


def ln_backward(grad, xhat, scale, gain):
    e = grad * gain
    dv = scale * (
        e - jnp.mean(e, axis=-1, keepdims=True) - xhat * jnp.mean(e * xhat, axis=-1, keepdims=True)
    )
    return dv, jnp.sum(grad * xhat, axis=0), jnp.sum(grad, axis=0)


def rotate(values, cosines, sines):
    half_dim = values.shape[-1] // 2
    lower = values[..., :half_dim]
    upper = values[..., half_dim:]
    return jnp.concatenate(
        [lower * cosines - upper * sines, upper * cosines + lower * sines], axis=-1
    )


def doc_layout(starts, token_index):
    inside = token_index[:, None] >= starts[None, :]
    segment = jnp.sum(inside.astype(jnp.int32), axis=1)
    begins = jnp.max(jnp.where(inside, starts[None, :], 0), axis=1)
    return segment, token_index - begins


def angles_of(position):
    frequency = jnp.exp(
        jnp.arange(HD // 2, dtype=F32) * (-2.0 * math.log(10000.0) / HD)
    )
    angles = position.astype(F32)[..., None] * frequency
    return jnp.cos(angles), jnp.sin(angles)


def block_mask(segment, offset, block_len, key_len):
    query_pos = jnp.arange(offset, offset + block_len, dtype=jnp.int32)
    key_pos = jnp.arange(key_len, dtype=jnp.int32)
    causal = key_pos[None, :] <= query_pos[:, None]
    return causal & (segment[offset : offset + block_len, None] == segment[None, :key_len])


def attention_forward(q, k, v, segment):
    seq_len = q.shape[1]
    block_len = min(512, seq_len)
    pieces, lses = [], []
    for offset in range(0, seq_len, block_len):
        end = offset + block_len
        allowed = block_mask(segment, offset, block_len, end)[None]
        scores = 0.125 * jnp.einsum(
            "hqe,hke->hqk", q[:, offset:end], k[:, :end], preferred_element_type=F32
        )
        scores = jnp.where(allowed, scores, -1e30)
        peak = jnp.max(scores, axis=-1, keepdims=True)
        lse = peak + jnp.log(jnp.sum(jnp.exp(scores - peak), axis=-1, keepdims=True))
        probs = jnp.exp(scores - lse).astype(BF16)
        pieces.append(
            jnp.einsum("hqk,hke->hqe", probs, v[:, :end], preferred_element_type=F32).astype(BF16)
        )
        lses.append(lse)
    return jnp.concatenate(pieces, axis=1), lses


def attention_backward(q, k, v, do, lses, segment):
    seq_len = q.shape[1]
    block_len = min(512, seq_len)
    dq = []
    dk = jnp.zeros(k.shape, F32)
    dv = jnp.zeros(v.shape, F32)
    for index, offset in enumerate(range(0, seq_len, block_len)):
        end = offset + block_len
        allowed = block_mask(segment, offset, block_len, end)[None]
        qb, kb, vb, dob = q[:, offset:end], k[:, :end], v[:, :end], do[:, offset:end]
        scores = 0.125 * jnp.einsum("hqe,hke->hqk", qb, kb, preferred_element_type=F32)
        scores = jnp.where(allowed, scores, -1e30)
        soft = jnp.exp(scores - lses[index])
        probs = soft.astype(BF16)
        dp = jnp.einsum("hqe,hke->hqk", dob, vb, preferred_element_type=F32)
        dot = jnp.sum(soft * dp, axis=-1, keepdims=True)
        ds = (soft * (dp - dot)).astype(BF16)
        dq.append(0.125 * jnp.einsum("hqk,hke->hqe", ds, kb, preferred_element_type=F32))
        pad = ((0, 0), (0, seq_len - end), (0, 0))
        dk = dk + jnp.pad(
            0.125 * jnp.einsum("hqk,hqe->hke", ds, qb, preferred_element_type=F32), pad
        )
        dv = dv + jnp.pad(jnp.einsum("hqk,hqe->hke", probs, dob, preferred_element_type=F32), pad)
    return jnp.concatenate(dq, axis=1), dk, dv


def gather_both(shard):
    mine = lax.all_gather(shard, CHIPS, axis=0, tiled=False)
    return jnp.stack([mine, lax.ppermute(mine, "c", SWAP)])


def scatter_both(partial, sizes):
    ny, nz, nx = sizes
    shard_shape = partial.shape[2:]
    low = partial.astype(BF16)
    got = lax.ppermute(low[1], "c", SWAP)
    mine = (low[0].astype(F32) + got.astype(F32)).astype(BF16)
    mine = mine.reshape((ny, nz, nx) + shard_shape)
    mine = mine.transpose((0, 2, 1) + tuple(range(3, mine.ndim)))
    mine = mine.reshape((ny * nx, nz) + shard_shape)
    mine = lax.psum_scatter(mine, ("y", "x"), scatter_dimension=0, tiled=False)
    return lax.psum_scatter(mine, "z", scatter_dimension=0, tiled=False).astype(F32)


def shards(inputs, doc_starts, w_qkv, w_out, w_up, w_down, norm_gains, norm_biases, cotangent):
    ny, nz, nx = (lax.axis_size(name) for name in CHIPS)
    core = lax.axis_index("c")
    sizes = (ny, nz, nx)
    parts = nz * nx
    micro, _, shard_len, width = inputs.shape
    tokens = micro * shard_len
    seq_len = shard_len * parts
    dpart = width // (2 * ny)
    hcols = w_out.shape[0]
    heads = hcols // HD
    units = w_up.shape[1]

    def to_own(values):
        pieces = values.reshape(values.shape[:-1] + (ny, 2, dpart))
        pieces = jnp.where(core == 0, pieces, pieces[..., ::-1, :])
        return jnp.swapaxes(pieces, -3, -2).reshape(values.shape)

    def from_own(values):
        pieces = jnp.swapaxes(values.reshape(values.shape[:-1] + (2, ny, dpart)), -3, -2)
        return jnp.where(core == 0, pieces, pieces[..., ::-1, :]).reshape(values.shape)

    qkv_all = gather_both(w_qkv).reshape(2, ny, parts, 3, dpart, hcols)
    norms = jnp.stack([norm_gains, norm_biases])
    norms = gather_dp(norms, ny, dpart)
    norms = to_own(norms.astype(F32))
    gains, shifts = norms[0], norms[1]
    out_all = gather_both(w_out).reshape(2, ny, parts, hcols, dpart)
    up_all = gather_both(w_up).reshape(2, ny, parts, dpart, units)
    down_all = gather_both(w_down).reshape(2, ny, parts, units, dpart)

    qkv_full = qkv_all.transpose(0, 1, 4, 3, 2, 5).reshape(width, 3 * parts * hcols)
    out_full = out_all.transpose(2, 3, 0, 1, 4).reshape(parts * hcols, width)
    up_full = up_all.transpose(0, 1, 3, 2, 4).reshape(width, parts * units)
    down_full = down_all.transpose(2, 3, 0, 1, 4).reshape(parts * units, width)

    x = to_own(inputs.reshape(tokens, width)).astype(F32)
    cot = to_own(cotangent.reshape(tokens, width)).astype(F32)
    place = lax.axis_index(SEQ) * shard_len + jnp.arange(shard_len, dtype=jnp.int32)
    cos_own, sin_own, cos_row, sin_row, segments = [], [], [], [], []
    for index in range(micro):
        starts = doc_starts[index, 0]
        c, s = angles_of(doc_layout(starts, place)[1])
        cos_own.append(c)
        sin_own.append(s)
        segment, position = doc_layout(starts, jnp.arange(seq_len, dtype=jnp.int32))
        c, s = angles_of(position)
        cos_row.append(c)
        sin_row.append(s)
        segments.append(segment)
    cos_own = jnp.concatenate(cos_own)[:, None, None]
    sin_own = jnp.concatenate(sin_own)[:, None, None]

    normed1, xhat0, scale0 = ln_forward(x, gains[0], shifts[0])
    normed1 = normed1.astype(BF16)
    projected = jnp.dot(normed1, qkv_full, preferred_element_type=F32)
    projected = projected.reshape(tokens, 3, parts * heads, HD)
    rotated = rotate(projected[:, :2], cos_own, sin_own)
    projected = jnp.concatenate([rotated, projected[:, 2:]], axis=1).astype(BF16)
    projected = projected.reshape(micro, shard_len, 3, parts, hcols).transpose(0, 3, 2, 1, 4)

    def to_heads(values):
        kinds = values.shape[1]
        got = lax.all_to_all(values, SEQ, 0, 0, tiled=True)
        got = got.reshape(parts, kinds, shard_len, heads, HD).transpose(1, 3, 0, 2, 4)
        return got.reshape(kinds, heads, seq_len, HD)

    def to_tokens(values):
        kinds = values.shape[0]
        sent = values.reshape(kinds, heads, parts, shard_len, HD).transpose(2, 0, 3, 1, 4)
        sent = sent.reshape(parts, kinds, shard_len, hcols)
        return lax.all_to_all(sent, SEQ, 0, 0, tiled=True)

    qkvs, lses, attended = [], [], []
    for index in range(micro):
        q, k, v = to_heads(projected[index])
        out, lse = attention_forward(q, k, v, segments[index])
        qkvs.append((q, k, v))
        lses.append(lse)
        attended.append(to_tokens(out[None])[:, 0])
    attended = jnp.stack(attended).transpose(0, 2, 1, 3).reshape(tokens, parts * hcols)

    branch1 = jnp.dot(attended, out_full, preferred_element_type=F32)
    post1, xhat1, scale1 = ln_forward(branch1, gains[1], shifts[1])
    hidden = x + post1
    normed2, xhat2, scale2 = ln_forward(hidden, gains[2], shifts[2])
    normed2 = normed2.astype(BF16)
    up_act = jnp.dot(normed2, up_full, preferred_element_type=F32)
    gated, gate_pull = jax.vjp(lambda u: jax.nn.gelu(u, approximate=True), up_act)
    activated = gated.astype(BF16)
    branch2 = jnp.dot(activated, down_full, preferred_element_type=F32)
    post2, xhat3, scale3 = ln_forward(branch2, gains[3], shifts[3])
    outputs = (hidden + post2).astype(BF16)

    grad_branch2, gain3, shift3 = ln_backward(cot, xhat3, scale3, gains[3])
    grad_branch2 = grad_branch2.astype(BF16)
    down_part = jnp.einsum("tf,td->fd", activated, grad_branch2, preferred_element_type=F32)
    down_part = down_part.astype(BF16).reshape(parts, units, 2, ny, dpart)
    down_grad = scatter_both(
        down_part.transpose(2, 3, 0, 1, 4).reshape(2, ny * parts, units, dpart), sizes
    )
    grad_act = jnp.einsum("td,fd->tf", grad_branch2, down_full, preferred_element_type=F32)
    grad_up = gate_pull(grad_act)[0].astype(BF16)
    up_part = jnp.einsum("td,tf->df", normed2, grad_up, preferred_element_type=F32)
    up_part = up_part.astype(BF16).reshape(2, ny, dpart, parts, units)
    up_grad = scatter_both(
        up_part.transpose(0, 1, 3, 2, 4).reshape(2, ny * parts, dpart, units), sizes
    )
    grad_normed2 = jnp.einsum("tf,df->td", grad_up, up_full, preferred_element_type=F32)
    extra, gain2, shift2 = ln_backward(grad_normed2, xhat2, scale2, gains[2])
    grad_hidden = cot + extra
    grad_branch1, gain1, shift1 = ln_backward(grad_hidden, xhat1, scale1, gains[1])
    grad_branch1 = grad_branch1.astype(BF16)
    grad_attended = jnp.einsum(
        "td,fd->tf", grad_branch1, out_full, preferred_element_type=F32
    ).astype(BF16)
    grad_attended = grad_attended.reshape(micro, shard_len, parts, 1, hcols)
    grad_attended = grad_attended.transpose(0, 2, 3, 1, 4)
    out_part = jnp.einsum("tf,td->fd", attended, grad_branch1, preferred_element_type=F32)
    out_part = out_part.astype(BF16).reshape(parts, hcols, 2, ny, dpart)
    out_grad = scatter_both(
        out_part.transpose(2, 3, 0, 1, 4).reshape(2, ny * parts, hcols, dpart), sizes
    )

    grad_projected = []
    for index in range(micro):
        do = to_heads(grad_attended[index])[0]
        q, k, v = qkvs[index]
        dq, dk, dv = attention_backward(q, k, v, do, lses[index], segments[index])
        cos, sin = cos_row[index], -sin_row[index]
        back = jnp.stack([rotate(dq, cos, sin), rotate(dk, cos, sin), dv]).astype(BF16)
        grad_projected.append(to_tokens(back))
    grad_projected = jnp.stack(grad_projected).transpose(0, 3, 2, 1, 4)
    grad_projected = grad_projected.reshape(tokens, 3 * parts * hcols)
    qkv_part = jnp.einsum("td,te->de", normed1, grad_projected, preferred_element_type=F32)
    qkv_part = qkv_part.astype(BF16).reshape(2, ny, dpart, 3, parts, hcols)
    qkv_grad = scatter_both(
        qkv_part.transpose(0, 1, 4, 3, 2, 5).reshape(2, ny * parts, 3, dpart, hcols), sizes
    )
    grad_normed1 = jnp.einsum(
        "te,de->td", grad_projected, qkv_full, preferred_element_type=F32
    )
    extra, gain0, shift0 = ln_backward(grad_normed1, xhat0, scale0, gains[0])
    inputs_grad = grad_hidden + extra
    sums = jnp.stack([gain0, gain1, gain2, gain3, shift0, shift1, shift2, shift3])
    sums = lax.psum(from_own(sums), ("y", "c", "z", "x"))
    place = (lax.axis_index("y") * 2 + core) * dpart
    sums = lax.dynamic_slice_in_dim(sums, place, dpart, 1)
    return (
        from_own(outputs).reshape(inputs.shape),
        from_own(inputs_grad).reshape(inputs.shape),
        qkv_grad,
        out_grad,
        up_grad,
        down_grad,
        sums[:4],
        sums[4:],
    )


def gather_dp(norms, ny, dpart):
    full = lax.all_gather(norms, ("y", "c"), axis=2, tiled=True)
    return full


def solution(mesh):
    dp, tensor = mesh.shape["dp"], mesh.shape["tensor"]
    names = ("y", "c", "z", "x")
    fine = Mesh(mesh.devices.reshape(dp // 2, 2, 4, tensor // 4), names)
    rows, seq = ("y", "c"), ("z", "x")
    tokens = P(None, rows, seq, None)
    weights = (P(None, rows, seq), P(seq, rows), P(rows, seq), P(seq, rows))
    norm = P(None, rows)
    return jax.shard_map(
        shards,
        mesh=fine,
        in_specs=(tokens, P(None, rows, None)) + weights + (norm, norm, tokens),
        out_specs=(tokens, tokens) + weights + (norm, norm),
        check_vma=False,
    )
```

```python
import math

import jax
import jax.numpy as jnp
from jax import lax
from jax.experimental import pallas as pl
from jax.experimental.pallas import tpu as pltpu
from jax.sharding import Mesh, PartitionSpec as P

HD = 64
EPSILON = 1e-05
F32 = jnp.float32
BF16 = jnp.bfloat16
CHIPS = ("y", "z", "x")
SEQ = ("z", "x")
SWAP = [(0, 1), (1, 0)]


def ln_forward(values, gain, shift):
    average = jnp.mean(values, axis=-1, keepdims=True)
    centred = values - average
    variance = jnp.mean(centred * centred, axis=-1, keepdims=True)
    scale = lax.rsqrt(variance + EPSILON)
    xhat = centred * scale
    return xhat * gain + shift, xhat, scale


def ln_backward(grad, xhat, scale, gain):
    e = grad * gain
    dv = scale * (
        e - jnp.mean(e, axis=-1, keepdims=True) - xhat * jnp.mean(e * xhat, axis=-1, keepdims=True)
    )
    return dv, jnp.sum(grad * xhat, axis=0), jnp.sum(grad, axis=0)


def rotate(values, cosines, sines):
    half_dim = values.shape[-1] // 2
    lower = values[..., :half_dim]
    upper = values[..., half_dim:]
    return jnp.concatenate(
        [lower * cosines - upper * sines, upper * cosines + lower * sines], axis=-1
    )


def doc_layout(starts, token_index):
    inside = token_index[:, None] >= starts[None, :]
    segment = jnp.sum(inside.astype(jnp.int32), axis=1)
    begins = jnp.max(jnp.where(inside, starts[None, :], 0), axis=1)
    return segment, token_index - begins


def angles_of(position):
    frequency = jnp.exp(
        jnp.arange(HD // 2, dtype=F32) * (-2.0 * math.log(10000.0) / HD)
    )
    angles = position.astype(F32)[..., None] * frequency
    return jnp.cos(angles), jnp.sin(angles)


def block_mask(segment, offset, block_len, key_len):
    query_pos = jnp.arange(offset, offset + block_len, dtype=jnp.int32)
    key_pos = jnp.arange(key_len, dtype=jnp.int32)
    causal = key_pos[None, :] <= query_pos[:, None]
    return causal & (segment[offset : offset + block_len, None] == segment[None, :key_len])


def attention_forward(q, k, v, segment):
    seq_len = q.shape[1]
    block_len = min(512, seq_len)
    pieces, lses = [], []
    for offset in range(0, seq_len, block_len):
        end = offset + block_len
        allowed = block_mask(segment, offset, block_len, end)[None]
        scores = 0.125 * jnp.einsum(
            "hqe,hke->hqk", q[:, offset:end], k[:, :end], preferred_element_type=F32
        )
        scores = jnp.where(allowed, scores, -1e30)
        peak = jnp.max(scores, axis=-1, keepdims=True)
        lse = peak + jnp.log(jnp.sum(jnp.exp(scores - peak), axis=-1, keepdims=True))
        probs = jnp.exp(scores - lse).astype(BF16)
        pieces.append(
            jnp.einsum("hqk,hke->hqe", probs, v[:, :end], preferred_element_type=F32).astype(BF16)
        )
        lses.append(lse)
    return jnp.concatenate(pieces, axis=1), lses


def attention_backward(q, k, v, do, lses, segment):
    seq_len = q.shape[1]
    block_len = min(512, seq_len)
    dq = []
    dk = jnp.zeros(k.shape, F32)
    dv = jnp.zeros(v.shape, F32)
    for index, offset in enumerate(range(0, seq_len, block_len)):
        end = offset + block_len
        allowed = block_mask(segment, offset, block_len, end)[None]
        qb, kb, vb, dob = q[:, offset:end], k[:, :end], v[:, :end], do[:, offset:end]
        scores = 0.125 * jnp.einsum("hqe,hke->hqk", qb, kb, preferred_element_type=F32)
        scores = jnp.where(allowed, scores, -1e30)
        soft = jnp.exp(scores - lses[index])
        probs = soft.astype(BF16)
        dp = jnp.einsum("hqe,hke->hqk", dob, vb, preferred_element_type=F32)
        dot = jnp.sum(soft * dp, axis=-1, keepdims=True)
        ds = (soft * (dp - dot)).astype(BF16)
        dq.append(0.125 * jnp.einsum("hqk,hke->hqe", ds, kb, preferred_element_type=F32))
        pad = ((0, 0), (0, seq_len - end), (0, 0))
        dk = dk + jnp.pad(
            0.125 * jnp.einsum("hqk,hqe->hke", ds, qb, preferred_element_type=F32), pad
        )
        dv = dv + jnp.pad(jnp.einsum("hqk,hqe->hke", probs, dob, preferred_element_type=F32), pad)
    return jnp.concatenate(dq, axis=1), dk, dv


def gather_both(shard):
    mine = lax.all_gather(shard, CHIPS, axis=0, tiled=False)
    return jnp.stack([mine, lax.ppermute(mine, "c", SWAP)])


def scatter_both(partial, sizes):
    ny, nz, nx = sizes
    shard_shape = partial.shape[2:]
    low = partial.astype(BF16)
    got = lax.ppermute(low[1], "c", SWAP)
    mine = (low[0].astype(F32) + got.astype(F32)).astype(BF16)
    mine = mine.reshape((ny, nz, nx) + shard_shape)
    mine = mine.transpose((0, 2, 1) + tuple(range(3, mine.ndim)))
    mine = mine.reshape((ny * nx, nz) + shard_shape)
    mine = lax.psum_scatter(mine, ("y", "x"), scatter_dimension=0, tiled=False)
    return lax.psum_scatter(mine, "z", scatter_dimension=0, tiled=False).astype(F32)


def shards(inputs, doc_starts, w_qkv, w_out, w_up, w_down, norm_gains, norm_biases, cotangent):
    ny, nz, nx = (lax.axis_size(name) for name in CHIPS)
    core = lax.axis_index("c")
    sizes = (ny, nz, nx)
    parts = nz * nx
    micro, _, shard_len, width = inputs.shape
    tokens = micro * shard_len
    seq_len = shard_len * parts
    dpart = width // (2 * ny)
    hcols = w_out.shape[0]
    heads = hcols // HD
    units = w_up.shape[1]

    def to_own(values):
        pieces = values.reshape(values.shape[:-1] + (ny, 2, dpart))
        pieces = jnp.where(core == 0, pieces, pieces[..., ::-1, :])
        return jnp.swapaxes(pieces, -3, -2).reshape(values.shape)

    def from_own(values):
        pieces = jnp.swapaxes(values.reshape(values.shape[:-1] + (2, ny, dpart)), -3, -2)
        return jnp.where(core == 0, pieces, pieces[..., ::-1, :]).reshape(values.shape)

    qkv_all = gather_both(w_qkv).reshape(2, ny, parts, 3, dpart, hcols)
    norms = jnp.stack([norm_gains, norm_biases])
    norms = gather_dp(norms, ny, dpart)
    norms = to_own(norms.astype(F32))
    gains, shifts = norms[0], norms[1]
    out_all = gather_both(w_out).reshape(2, ny, parts, hcols, dpart)
    up_all = gather_both(w_up).reshape(2, ny, parts, dpart, units)
    down_all = gather_both(w_down).reshape(2, ny, parts, units, dpart)

    qkv_full = qkv_all.transpose(0, 1, 4, 3, 2, 5).reshape(width, 3 * parts * hcols)
    out_full = out_all.transpose(2, 3, 0, 1, 4).reshape(parts * hcols, width)
    up_full = up_all.transpose(0, 1, 3, 2, 4).reshape(width, parts * units)
    down_full = down_all.transpose(2, 3, 0, 1, 4).reshape(parts * units, width)

    x = to_own(inputs.reshape(tokens, width)).astype(F32)
    cot = to_own(cotangent.reshape(tokens, width)).astype(F32)
    place = lax.axis_index(SEQ) * shard_len + jnp.arange(shard_len, dtype=jnp.int32)
    cos_own, sin_own, cos_row, sin_row, segments = [], [], [], [], []
    for index in range(micro):
        starts = doc_starts[index, 0]
        c, s = angles_of(doc_layout(starts, place)[1])
        cos_own.append(c)
        sin_own.append(s)
        segment, position = doc_layout(starts, jnp.arange(seq_len, dtype=jnp.int32))
        c, s = angles_of(position)
        cos_row.append(c)
        sin_row.append(s)
        segments.append(segment)
    cos_own = jnp.concatenate(cos_own)[:, None, None]
    sin_own = jnp.concatenate(sin_own)[:, None, None]

    normed1, xhat0, scale0 = ln_forward(x, gains[0], shifts[0])
    normed1 = normed1.astype(BF16)
    projected = jnp.dot(normed1, qkv_full, preferred_element_type=F32)
    projected = projected.reshape(tokens, 3, parts * heads, HD)
    rotated = rotate(projected[:, :2], cos_own, sin_own)
    projected = jnp.concatenate([rotated, projected[:, 2:]], axis=1).astype(BF16)
    projected = projected.reshape(micro, shard_len, 3, parts, hcols).transpose(0, 3, 2, 1, 4)

    def to_heads(values):
        kinds = values.shape[1]
        got = lax.all_to_all(values, SEQ, 0, 0, tiled=True)
        got = got.reshape(parts, kinds, shard_len, heads, HD).transpose(1, 3, 0, 2, 4)
        return got.reshape(kinds, heads, seq_len, HD)

    def to_tokens(values):
        kinds = values.shape[0]
        sent = values.reshape(kinds, heads, parts, shard_len, HD).transpose(2, 0, 3, 1, 4)
        sent = sent.reshape(parts, kinds, shard_len, hcols)
        return lax.all_to_all(sent, SEQ, 0, 0, tiled=True)

    qkvs, lses, attended = [], [], []
    for index in range(micro):
        q, k, v = to_heads(projected[index])
        out, lse = attention_forward(q, k, v, segments[index])
        qkvs.append((q, k, v))
        lses.append(lse)
        attended.append(to_tokens(out[None])[:, 0])
    attended = jnp.stack(attended).transpose(0, 2, 1, 3).reshape(tokens, parts * hcols)

    branch1 = jnp.dot(attended, out_full, preferred_element_type=F32)
    post1, xhat1, scale1 = ln_forward(branch1, gains[1], shifts[1])
    hidden = x + post1
    normed2, xhat2, scale2 = ln_forward(hidden, gains[2], shifts[2])
    normed2 = normed2.astype(BF16)
    up_act = jnp.dot(normed2, up_full, preferred_element_type=F32)
    gated, gate_pull = jax.vjp(lambda u: jax.nn.gelu(u, approximate=True), up_act)
    activated = gated.astype(BF16)
    branch2 = jnp.dot(activated, down_full, preferred_element_type=F32)
    post2, xhat3, scale3 = ln_forward(branch2, gains[3], shifts[3])
    outputs = (hidden + post2).astype(BF16)

    grad_branch2, gain3, shift3 = ln_backward(cot, xhat3, scale3, gains[3])
    grad_branch2 = grad_branch2.astype(BF16)
    down_part = jnp.einsum("tf,td->fd", activated, grad_branch2, preferred_element_type=F32)
    down_part = down_part.astype(BF16).reshape(parts, units, 2, ny, dpart)
    down_grad = scatter_both(
        down_part.transpose(2, 3, 0, 1, 4).reshape(2, ny * parts, units, dpart), sizes
    )
    grad_act = jnp.einsum("td,fd->tf", grad_branch2, down_full, preferred_element_type=F32)
    grad_up = gate_pull(grad_act)[0].astype(BF16)
    up_part = jnp.einsum("td,tf->df", normed2, grad_up, preferred_element_type=F32)
    up_part = up_part.astype(BF16).reshape(2, ny, dpart, parts, units)
    up_grad = scatter_both(
        up_part.transpose(0, 1, 3, 2, 4).reshape(2, ny * parts, dpart, units), sizes
    )
    grad_normed2 = jnp.einsum("tf,df->td", grad_up, up_full, preferred_element_type=F32)
    extra, gain2, shift2 = ln_backward(grad_normed2, xhat2, scale2, gains[2])
    grad_hidden = cot + extra
    grad_branch1, gain1, shift1 = ln_backward(grad_hidden, xhat1, scale1, gains[1])
    grad_branch1 = grad_branch1.astype(BF16)
    grad_attended = jnp.einsum(
        "td,fd->tf", grad_branch1, out_full, preferred_element_type=F32
    ).astype(BF16)
    grad_attended = grad_attended.reshape(micro, shard_len, parts, 1, hcols)
    grad_attended = grad_attended.transpose(0, 2, 3, 1, 4)
    out_part = jnp.einsum("tf,td->fd", attended, grad_branch1, preferred_element_type=F32)
    out_part = out_part.astype(BF16).reshape(parts, hcols, 2, ny, dpart)
    out_grad = scatter_both(
        out_part.transpose(2, 3, 0, 1, 4).reshape(2, ny * parts, hcols, dpart), sizes
    )

    grad_projected = []
    for index in range(micro):
        do = to_heads(grad_attended[index])[0]
        q, k, v = qkvs[index]
        dq, dk, dv = attention_backward(q, k, v, do, lses[index], segments[index])
        cos, sin = cos_row[index], -sin_row[index]
        back = jnp.stack([rotate(dq, cos, sin), rotate(dk, cos, sin), dv]).astype(BF16)
        grad_projected.append(to_tokens(back))
    grad_projected = jnp.stack(grad_projected).transpose(0, 3, 2, 1, 4)
    grad_projected = grad_projected.reshape(tokens, 3 * parts * hcols)
    qkv_part = jnp.einsum("td,te->de", normed1, grad_projected, preferred_element_type=F32)
    qkv_part = qkv_part.astype(BF16).reshape(2, ny, dpart, 3, parts, hcols)
    qkv_grad = scatter_both(
        qkv_part.transpose(0, 1, 4, 3, 2, 5).reshape(2, ny * parts, 3, dpart, hcols), sizes
    )
    grad_normed1 = jnp.einsum(
        "te,de->td", grad_projected, qkv_full, preferred_element_type=F32
    )
    extra, gain0, shift0 = ln_backward(grad_normed1, xhat0, scale0, gains[0])
    inputs_grad = grad_hidden + extra
    sums = jnp.stack([gain0, gain1, gain2, gain3, shift0, shift1, shift2, shift3])
    sums = lax.psum(from_own(sums), ("y", "c", "z", "x"))
    place = (lax.axis_index("y") * 2 + core) * dpart
    sums = lax.dynamic_slice_in_dim(sums, place, dpart, 1)
    return (
        from_own(outputs).reshape(inputs.shape),
        from_own(inputs_grad).reshape(inputs.shape),
        qkv_grad,
        out_grad,
        up_grad,
        down_grad,
        sums[:4],
        sums[4:],
    )


def gather_dp(norms, ny, dpart):
    full = lax.all_gather(norms, ("y", "c"), axis=2, tiled=True)
    return full


NT = (((1,), (1,)), ((), ()))
GELU_A = 0.7978845608
GELU_B = 0.044715


def dot(a, b):
    return jnp.dot(a, b, preferred_element_type=F32)


def dot_nt(a, b):
    return lax.dot_general(a, b, NT, preferred_element_type=F32)


def params(semantics=1):
    return pltpu.CompilerParams(
        dimension_semantics=("arbitrary",) * semantics, vmem_limit_bytes=60 * 1024 * 1024
    )


def cost(flops, size, transcendentals=0):
    return pl.CostEstimate(
        flops=int(flops), bytes_accessed=int(size), transcendentals=int(transcendentals)
    )


def whole(shape):
    return pl.BlockSpec(shape, lambda *_: (0,) * len(shape))


def swap_halves(values):
    lane = lax.broadcasted_iota(jnp.int32, values.shape, 1)
    low = lax.rem(lane, HD) < HD // 2
    return jnp.where(low, pltpu.roll(values, 96, 1), pltpu.roll(values, 32, 1))


def row_stats(values):
    average = jnp.mean(values, axis=-1, keepdims=True)
    centred = values - average
    variance = jnp.mean(centred * centred, axis=-1, keepdims=True)
    scale = lax.rsqrt(variance + EPSILON)
    return centred * scale, scale


def row_pull(grad, xhat, scale, gain):
    e = grad * gain
    return scale * (
        e - jnp.mean(e, axis=-1, keepdims=True) - xhat * jnp.mean(e * xhat, axis=-1, keepdims=True)
    )


def column_sum(values):
    return jnp.sum(values, axis=0, keepdims=True)


def store_columns(ref, values, pos, part):
    for dc in range(2):
        for dy in range(2):
            place = (lax.bitwise_xor(pos[0], dy) * 2 + lax.bitwise_xor(pos[1], dc)) * part
            place = pl.multiple_of(place, part)
            col = (dc * 2 + dy) * part
            ref[:, pl.ds(place, part)] = values[:, col : col + part].astype(ref.dtype)


def proj_kernel(pos, x, gains, shifts, cos, sin, *refs):
    weights = [refs[2 * q : 2 * q + 2] for q in range(4)]
    outs, normed = refs[8:11], refs[11]
    part = weights[0][0].shape[2]
    count = outs[0].shape[3]

    @pl.when(pl.program_id(0) == 0)
    def _():
        xhat, _ = row_stats(x[...].astype(F32))
        normed[...] = (xhat * gains[0:1] + shifts[0:1]).astype(BF16)

    total = None
    for q in range(4):
        block = jnp.concatenate([weights[q][dx][0, kind] for dx in range(2) for kind in range(3)], 1)
        term = dot(normed[:, q * part : (q + 1) * part], block)
        total = term if total is None else total + term
    for dx in range(2):
        place = lax.bitwise_xor(pos[3], dx)
        for kind in range(3):
            at = (dx * 3 + kind) * 128
            u = total[:, at : at + 128]
            if kind < 2:
                u = u * cos[...] + swap_halves(u) * sin[...]
            u = u.astype(BF16)
            for m in range(3):
                outs[m][0, place, kind] = u[m * count : (m + 1) * count]


def ring_index(nz):
    return lambda i, pos: (lax.rem(pos[2] + i, nz), 0, 0, 0, 0)


def call_proj(pos, x, gains, shifts, cos, sin, pieces, shard_len):
    tokens, width = x.shape
    nz, _, part, cols = pieces[0][0].shape
    piece = pl.BlockSpec((1, 3, part, cols), lambda i, pos: (i, 0, 0, 0))
    out = pl.BlockSpec((1, 2, 3, shard_len, cols), ring_index(nz))
    out_shape = jax.ShapeDtypeStruct((nz, 2, 3, shard_len, cols), BF16)
    return pl.pallas_call(
        proj_kernel,
        grid_spec=pltpu.PrefetchScalarGridSpec(
            num_scalar_prefetch=1,
            grid=(nz,),
            in_specs=[whole(a.shape) for a in (x, gains, shifts, cos, sin)] + [piece] * 8,
            out_specs=[out] * 3 + [whole((tokens, width))],
        ),
        out_shape=[out_shape] * 3 + [jax.ShapeDtypeStruct((tokens, width), BF16)],
        compiler_params=params(),
        cost_estimate=cost(2 * tokens * width * 3 * nz * 2 * cols, 12e6),
        name="project",
    )(pos, x, gains, shifts, cos, sin, *[p for pair in pieces for p in pair])


def head_mask(shape, head):
    lane = lax.broadcasted_iota(jnp.int32, shape, 1)
    return (lane < HD) if head == 0 else (lane >= HD)


def attend_kernel(begins, got, out, lse_out):
    shards_n, _, count, lanes = got.shape
    seq_len = shards_n * count
    block = min(256, seq_len)
    q_all = (got[:, 0] * 0.125).reshape(seq_len, lanes)
    k_all = got[:, 1].reshape(seq_len, lanes)
    v_all = got[:, 2].reshape(seq_len, lanes)
    per = block // count
    for start in range(0, seq_len, block):
        end = start + block
        qb = q_all[start:end]
        key = lax.broadcasted_iota(jnp.int32, (block, end), 1)
        query = start + lax.broadcasted_iota(jnp.int32, (block, end), 0)
        allowed = (key <= query) & (key >= begins[start:end, 0:1])
        results = []
        for head in range(2):
            mask = head_mask(qb.shape, head)
            scores = dot_nt(jnp.where(mask, qb, 0), k_all[:end])
            scores = jnp.where(allowed, scores, -1e30)
            peak = jnp.max(scores, axis=-1, keepdims=True)
            e = jnp.exp(scores - peak)
            total = jnp.sum(e, axis=-1, keepdims=True)
            results.append(dot(e.astype(BF16), v_all[:end]) / total)
            lse = jnp.broadcast_to(peak + jnp.log(total), (block, 128))
            lse_out[head : head + 1, start:end] = jnp.transpose(lse)[0:1]
        mixed = jnp.where(head_mask(results[0].shape, 0), results[0], results[1]).astype(BF16)
        out[start // count : end // count] = mixed.reshape(per, count, lanes)


def call_attend(begins, got):
    parts, _, count, lanes = got.shape
    seq_len = parts * count
    return pl.pallas_call(
        attend_kernel,
        out_shape=[
            jax.ShapeDtypeStruct((parts, count, lanes), BF16),
            jax.ShapeDtypeStruct((8, seq_len), F32),
        ],
        compiler_params=params(0),
        cost_estimate=cost(4 * 2 * seq_len * seq_len * lanes, 2e6, 2 * seq_len * seq_len),
        name="attend",
    )(begins, got)


def attend_back_kernel(begins, cos, sin, got, grad, att, lse, out, dq_ref, dk_ref, dv_ref):
    shards_n, _, count, lanes = got.shape
    seq_len = shards_n * count
    block = min(256, seq_len)
    q_all = (got[:, 0] * 0.125).reshape(seq_len, lanes)
    k_all = got[:, 1].reshape(seq_len, lanes)
    v_all = got[:, 2].reshape(seq_len, lanes)
    do_all = grad[...].reshape(seq_len, lanes)
    prod = do_all.astype(F32) * att[...].reshape(seq_len, lanes).astype(F32)
    prod = jnp.transpose(prod)
    deltas = [
        jnp.sum(prod[:HD], axis=0, keepdims=True),
        jnp.sum(prod[HD:], axis=0, keepdims=True),
    ]
    for start in range(0, seq_len, block):
        end = start + block
        kb, vb = k_all[start:end], v_all[start:end]
        qs, dos = q_all[start:], do_all[start:]
        span = seq_len - start
        key = start + lax.broadcasted_iota(jnp.int32, (block, span), 0)
        query = start + lax.broadcasted_iota(jnp.int32, (block, span), 1)
        allowed = (key <= query) & (key >= begins[0:1, start:])
        dks, dvs, dqs = [], [], []
        for head in range(2):
            mask = head_mask(kb.shape, head)
            scores = dot_nt(jnp.where(mask, kb, 0), qs)
            soft = jnp.exp(jnp.where(allowed, scores, -1e30) - lse[head : head + 1, start:])
            pull = dot_nt(jnp.where(mask, vb, 0), dos)
            ds = (soft * (pull - deltas[head][:, start:])).astype(BF16)
            dvs.append(dot(soft.astype(BF16), dos))
            dks.append(dot(ds, qs))
            dqs.append(
                lax.dot_general(ds, kb, (((0,), (0,)), ((), ())), preferred_element_type=F32)
            )
        low = head_mask(kb.shape, 0)
        dk_ref[start:end] = jnp.where(low, dks[0], dks[1])
        dv_ref[start:end] = jnp.where(low, dvs[0], dvs[1])
        dq = jnp.where(head_mask(dqs[0].shape, 0), dqs[0], dqs[1])
        if start == 0:
            dq_ref[...] = dq
        else:
            dq_ref[start:] += dq
    for kind, ref in enumerate((dq_ref, dk_ref, dv_ref)):
        u = ref[...]
        if kind == 0:
            u = u * 0.125
        if kind < 2:
            u = u * cos[...] - swap_halves(u) * sin[...]
        out[:, kind] = u.astype(BF16).reshape(shards_n, count, lanes)


def call_attend_back(begins, cos, sin, got, grad, att, lse):
    parts, _, count, lanes = got.shape
    seq_len = parts * count
    return pl.pallas_call(
        attend_back_kernel,
        out_shape=jax.ShapeDtypeStruct((parts, 3, count, lanes), BF16),
        scratch_shapes=[pltpu.VMEM((seq_len, lanes), F32)] * 3,
        compiler_params=params(0),
        cost_estimate=cost(10 * 2 * seq_len * seq_len * lanes, 4e6, 2 * seq_len * seq_len),
        name="attend_back",
    )(begins, cos, sin, got, grad, att, lse)


def layer_kernel(pos, *refs):
    att = refs[0:3]
    x, cot, gains, shifts = refs[3:7]
    ups = [refs[7 + 2 * q : 9 + 2 * q] for q in range(4)]
    downs = [refs[15 + 2 * q : 17 + 2 * q] for q in range(4)]
    mixes = [refs[23 + 2 * q : 25 + 2 * q] for q in range(4)]
    outputs, att_all, normed, act, g_up, g_b2, g_b1, g_hidden = refs[31:39]
    g_att = refs[39:42]
    sums = refs[42]
    slope, xhat1, scale1, xhat2, scale2, hidden, total = refs[43:50]
    nz = mixes[0][0].shape[0]
    count = att[0].shape[1]
    part = downs[0][0].shape[2]
    step = pl.program_id(0)

    def mix_block(q, zk):
        return jnp.concatenate([mixes[q][0][zk], mixes[q][1][zk]], 0)

    @pl.when(step == 0)
    def _():
        for zk in range(nz):
            for dx in range(2):
                place = zk * 2 + lax.bitwise_xor(pos[3], dx)
                for m in range(3):
                    at = (zk * 2 + dx) * 128
                    att_all[m * count : (m + 1) * count, at : at + 128] = att[m][place]
        for q in range(4):
            acc = None
            for zk in range(nz):
                term = dot(att_all[:, zk * 256 : (zk + 1) * 256], mix_block(q, zk))
                acc = term if acc is None else acc + term
            total[:, q * part : (q + 1) * part] = acc
        xhat, scale = row_stats(total[...])
        xhat1[...] = xhat
        scale1[...] = jnp.broadcast_to(scale, scale1.shape)
        value = x[...].astype(F32) + xhat * gains[1:2] + shifts[1:2]
        hidden[...] = value
        xhat, scale = row_stats(value)
        xhat2[...] = xhat
        scale2[...] = jnp.broadcast_to(scale, scale2.shape)
        normed[...] = (xhat * gains[2:3] + shifts[2:3]).astype(BF16)

    @pl.when(step < nz)
    def _():
        zk = step
        for dx in range(2):
            u = None
            for q in range(4):
                term = dot(normed[:, q * part : (q + 1) * part], ups[q][dx][0])
                u = term if u is None else u + term
            square = u * u
            t = jnp.tanh(GELU_A * (u * (1.0 + GELU_B * square)))
            half = 0.5 * (1.0 + t)
            act[0, dx] = (u * half).astype(BF16)
            slope[zk, dx] = half + (0.5 * GELU_A) * u * (1.0 - t * t) * (1.0 + 3.0 * GELU_B * square)
        for q in range(4):
            term = dot(act[0, 0], downs[q][0][0]) + dot(act[0, 1], downs[q][1][0])

            @pl.when(step == 0)
            def _():
                total[:, q * part : (q + 1) * part] = term

            @pl.when(step > 0)
            def _():
                total[:, q * part : (q + 1) * part] += term

    @pl.when(step == nz)
    def _():
        xhat, scale = row_stats(total[...])
        value = hidden[...] + xhat * gains[3:4] + shifts[3:4]
        store_columns(outputs, value, pos, part)
        grad = cot[...].astype(F32)
        sums[2:3] = column_sum(grad * xhat)
        sums[5:6] = column_sum(grad)
        g_b2[...] = row_pull(grad, xhat, scale, gains[3:4]).astype(BF16)

    @pl.when(step >= nz)
    def _():
        zk = 2 * nz - 1 - step
        for dx in range(2):
            g = None
            for q in range(4):
                term = dot_nt(g_b2[:, q * part : (q + 1) * part], downs[q][dx][0])
                g = term if g is None else g + term
            g_up[0, dx] = (g * slope[zk, dx]).astype(BF16)
        for q in range(4):
            term = dot_nt(g_up[0, 0], ups[q][0][0]) + dot_nt(g_up[0, 1], ups[q][1][0])

            @pl.when(step == nz)
            def _():
                total[:, q * part : (q + 1) * part] = term

            @pl.when(step > nz)
            def _():
                total[:, q * part : (q + 1) * part] += term

    @pl.when(step == 2 * nz - 1)
    def _():
        grad = total[...]
        xhat = xhat2[...]
        sums[1:2] = column_sum(grad * xhat)
        sums[4:5] = column_sum(grad)
        grad = cot[...].astype(F32) + row_pull(grad, xhat, scale2[:, 0:1], gains[2:3])
        g_hidden[...] = grad
        xhat = xhat1[...]
        sums[0:1] = column_sum(grad * xhat)
        sums[3:4] = column_sum(grad)
        g_b1[...] = row_pull(grad, xhat, scale1[:, 0:1], gains[1:2]).astype(BF16)
        for zk in range(nz):
            acc = None
            for q in range(4):
                term = dot_nt(g_b1[:, q * part : (q + 1) * part], mix_block(q, zk))
                acc = term if acc is None else acc + term
            acc = acc.astype(BF16)
            for dx in range(2):
                place = zk * 2 + lax.bitwise_xor(pos[3], dx)
                for m in range(3):
                    g_att[m][place] = acc[m * count : (m + 1) * count, dx * 128 : (dx + 1) * 128]


def call_layer(pos, att, x, cot, gains, shifts, ups, mixes):
    tokens, width = x.shape
    nz, part, units = ups[0][0].shape
    rows = mixes[0][0].shape[1] - units
    parts, count, cols = att[0].shape
    turn = 2 * nz - 1

    def weight_index(i, pos):
        return (jnp.minimum(i, turn - i), 0, 0)

    up = pl.BlockSpec((1, part, units), weight_index)
    down = pl.BlockSpec((1, units, part), weight_index)
    mix = pl.BlockSpec((nz, rows, part), lambda i, pos: (0, units // rows, 0))
    act = pl.BlockSpec((1, 2, tokens, units), lambda i, pos: (jnp.minimum(i, nz - 1), 0, 0, 0))
    g_up = pl.BlockSpec((1, 2, tokens, units), lambda i, pos: (jnp.minimum(turn - i, nz - 1), 0, 0, 0))
    flat = (tokens, width)
    ffn = jax.ShapeDtypeStruct((nz, 2, tokens, units), BF16)
    low = jax.ShapeDtypeStruct(flat, BF16)
    ups_flat = [p for pair in ups for p in pair]
    mixes_flat = [p for pair in mixes for p in pair]
    return pl.pallas_call(
        layer_kernel,
        grid_spec=pltpu.PrefetchScalarGridSpec(
            num_scalar_prefetch=1,
            grid=(2 * nz,),
            in_specs=[whole(a.shape) for a in (*att, x, cot, gains, shifts)]
            + [up] * 8
            + [down] * 8
            + [mix] * 8,
            out_specs=[whole(flat)] * 3
            + [act, g_up]
            + [whole(flat)] * 3
            + [whole(att[0].shape)] * 3
            + [whole((8, width))],
            scratch_shapes=[
                pltpu.VMEM((nz, 2, tokens, units), F32),
                pltpu.VMEM(flat, F32),
                pltpu.VMEM((tokens, 128), F32),
                pltpu.VMEM(flat, F32),
                pltpu.VMEM((tokens, 128), F32),
                pltpu.VMEM(flat, F32),
                pltpu.VMEM(flat, F32),
            ],
        ),
        out_shape=[low, low, low, ffn, ffn, low, low, jax.ShapeDtypeStruct(flat, F32)]
        + [jax.ShapeDtypeStruct(att[0].shape, BF16)] * 3
        + [jax.ShapeDtypeStruct((8, width), F32)],
        compiler_params=params(),
        cost_estimate=cost(
            2 * tokens * width * (4 * nz * 2 * units + 2 * width), 60e6, tokens * nz * 2 * units
        ),
        name="layer",
    )(pos, *att, x, cot, gains, shifts, *ups_flat, *mixes_flat, *mixes_flat)


def weight_grad_kernel(act, g_up, normed, g_b2, att_all, g_b1, *refs):
    ups = [refs[2 * q : 2 * q + 2] for q in range(4)]
    mixes = [refs[8 + 2 * q : 10 + 2 * q] for q in range(4)]
    flipped = refs[16]
    part, units = ups[0][0].shape[1:]

    @pl.when(pl.program_id(0) == 0)
    def _():
        flipped[...] = jnp.transpose(normed[...])

    for dx in range(2):
        side = jnp.transpose(act[0, dx])
        for q in range(4):
            cols = slice(q * part, (q + 1) * part)
            mixes[q][dx][0, :units] = dot(side, g_b2[:, cols]).astype(BF16)
            ups[q][dx][0] = dot(flipped[cols], g_up[0, dx]).astype(BF16)
    side = jnp.transpose(att_all[...])
    for q in range(4):
        both = dot(side, g_b1[:, q * part : (q + 1) * part]).astype(BF16)
        for dx in range(2):
            mixes[q][dx][0, units:] = both[dx * 128 : (dx + 1) * 128]


def call_weight_grad(act, g_up, normed, g_b2, att_all, g_b1):
    nz, _, tokens, units = act.shape
    width = normed.shape[1]
    part = width // 4
    rows = width // (2 * nz)
    ffn = pl.BlockSpec((1, 2, tokens, units), lambda i: (i, 0, 0, 0))
    heads = pl.BlockSpec((tokens, 2 * rows), lambda i: (0, i))
    up = pl.BlockSpec((1, part, units), lambda i: (i, 0, 0))
    mix = pl.BlockSpec((1, units + rows, part), lambda i: (i, 0, 0))
    flat = whole((tokens, width))
    res = pl.pallas_call(
        weight_grad_kernel,
        grid=(nz,),
        in_specs=[ffn, ffn, flat, flat, heads, flat],
        out_specs=[up] * 8 + [mix] * 8,
        out_shape=[jax.ShapeDtypeStruct((nz, part, units), BF16)] * 8
        + [jax.ShapeDtypeStruct((nz, units + rows, part), BF16)] * 8,
        scratch_shapes=[pltpu.VMEM((width, tokens), BF16)],
        compiler_params=params(),
        cost_estimate=cost(2 * tokens * width * (2 * nz * 2 * units + width), 40e6),
        name="weight_grad",
    )(act, g_up, normed, g_b2, att_all, g_b1)
    return [res[2 * q : 2 * q + 2] for q in range(4)], [res[8 + 2 * q : 10 + 2 * q] for q in range(4)]


def load_grads(pos, grads):
    columns = []
    for dx in range(2):
        place = lax.bitwise_xor(pos[3], dx)
        for kind in range(3):
            columns.append(jnp.concatenate([g[0, place, kind] for g in grads], 0))
    return jnp.concatenate(columns, 1)


def qkv_grad_kernel(pos, *refs):
    grads, normed = refs[0:3], refs[3]
    outs = [refs[4 + 2 * q : 6 + 2 * q] for q in range(4)]
    flipped = refs[12]
    part = outs[0][0].shape[2]

    @pl.when(pl.program_id(0) == 0)
    def _():
        flipped[...] = jnp.transpose(normed[...])

    block = load_grads(pos, grads)
    for q in range(4):
        res = dot(flipped[q * part : (q + 1) * part], block).astype(BF16)
        for dx in range(2):
            for kind in range(3):
                at = (dx * 3 + kind) * 128
                outs[q][dx][0, kind] = res[:, at : at + 128]


def call_qkv_grad(pos, grads, normed):
    nz, _, _, count, cols = grads[0].shape
    tokens, width = normed.shape
    part = width // 4
    grad = pl.BlockSpec((1, 2, 3, count, cols), ring_index(nz))
    piece = pl.BlockSpec((1, 3, part, cols), lambda i, pos: (i, 0, 0, 0))
    res = pl.pallas_call(
        qkv_grad_kernel,
        grid_spec=pltpu.PrefetchScalarGridSpec(
            num_scalar_prefetch=1,
            grid=(nz,),
            in_specs=[grad] * 3 + [whole(normed.shape)],
            out_specs=[piece] * 8,
            scratch_shapes=[pltpu.VMEM((width, tokens), BF16)],
        ),
        out_shape=[jax.ShapeDtypeStruct((nz, 3, part, cols), BF16)] * 8,
        compiler_params=params(),
        cost_estimate=cost(2 * tokens * width * 3 * nz * 2 * cols, 12e6),
        name="qkv_grad",
    )(pos, *grads, normed)
    return [res[2 * q : 2 * q + 2] for q in range(4)]


def input_grad_kernel(pos, *refs):
    grads, x, gains, g_hidden = refs[0:3], refs[3], refs[4], refs[5]
    weights = [refs[6 + 2 * q : 8 + 2 * q] for q in range(4)]
    out, sums, total = refs[14], refs[15], refs[16]
    part = weights[0][0].shape[2]
    step = pl.program_id(0)
    block = load_grads(pos, grads)
    for q in range(4):
        side = jnp.concatenate([weights[q][dx][0, kind] for dx in range(2) for kind in range(3)], 1)
        term = dot_nt(block, side)

        @pl.when(step == 0)
        def _():
            total[:, q * part : (q + 1) * part] = term

        @pl.when(step > 0)
        def _():
            total[:, q * part : (q + 1) * part] += term

    @pl.when(step == pl.num_programs(0) - 1)
    def _():
        grad = total[...]
        xhat, scale = row_stats(x[...].astype(F32))
        sums[0:1] = column_sum(grad * xhat)
        sums[1:2] = column_sum(grad)
        value = g_hidden[...] + row_pull(grad, xhat, scale, gains[0:1])
        store_columns(out, value, pos, part)


def call_input_grad(pos, grads, x, gains, g_hidden, pieces):
    nz, _, _, count, cols = grads[0].shape
    tokens, width = x.shape
    part = width // 4
    grad = pl.BlockSpec((1, 2, 3, count, cols), ring_index(nz))
    piece = pl.BlockSpec((1, 3, part, cols), lambda i, pos: (i, 0, 0, 0))
    return pl.pallas_call(
        input_grad_kernel,
        grid_spec=pltpu.PrefetchScalarGridSpec(
            num_scalar_prefetch=1,
            grid=(nz,),
            in_specs=[grad] * 3 + [whole(a.shape) for a in (x, gains, g_hidden)] + [piece] * 8,
            out_specs=[whole((tokens, width)), whole((8, width))],
            scratch_shapes=[pltpu.VMEM((tokens, width), F32)],
        ),
        out_shape=[
            jax.ShapeDtypeStruct((tokens, width), F32),
            jax.ShapeDtypeStruct((8, width), F32),
        ],
        compiler_params=params(),
        cost_estimate=cost(2 * tokens * width * 3 * nz * 2 * cols, 16e6),
        name="input_grad",
    )(pos, *grads, x, gains, g_hidden, *[p for pair in pieces for p in pair])


def swap(values, axis):
    return lax.ppermute(values, axis, SWAP)


def ring(values, step, size):
    return lax.ppermute(values, "z", [(i, (i + step) % size) for i in range(size)])


def spread(mine, via):
    over_x, over_y = swap(mine, "x"), swap(mine, "y")
    if via == "x":
        both = swap(over_y, "x")
    elif via == "y":
        both = swap(over_x, "y")
    else:
        half = mine.shape[0] // 2
        both = jnp.concatenate([swap(over_x[:half], "y"), swap(over_y[half:], "x")])
    own = [[mine, over_x], [over_y, both]]
    other = [[swap(p, "c") for p in pair] for pair in own]
    return own + other


def add(*values):
    total = values[0].astype(F32)
    for value in values[1:]:
        total = total + value.astype(F32)
    return total.astype(BF16)


def collect(pieces, via):
    own = [[add(pieces[dy][dx], swap(pieces[2 + dy][dx], "c")) for dx in range(2)] for dy in range(2)]
    (mine, over_x), (over_y, both) = own
    if via == "x":
        over_y = add(over_y, swap(both, "x"))
    elif via == "y":
        over_x = add(over_x, swap(both, "y"))
    else:
        half = mine.shape[0] // 2
        first, second = swap(both[:half], "y"), swap(both[half:], "x")
        over_x = jnp.concatenate([add(over_x[:half], first), over_x[half:]])
        over_y = jnp.concatenate([over_y[:half], add(over_y[half:], second)])
    return add(mine, swap(over_x, "x"), swap(over_y, "y"))


def total_norms(sums, part):
    pieces = [sums[:, q * part : (q + 1) * part] for q in range(4)]
    low, high = (pieces[dy] + swap(pieces[2 + dy], "c") for dy in range(2))
    mine = low + swap(high, "y")
    mine = mine + swap(mine, "x")
    mine = mine + lax.ppermute(mine, "z", [(i, i ^ 1) for i in range(4)])
    return mine + lax.ppermute(mine, "z", [(i, i ^ 2) for i in range(4)])


def fast_shards(inputs, doc_starts, w_qkv, w_out, w_up, w_down, norm_gains, norm_biases, cotangent):
    y, c, z, x_at = (lax.axis_index(name) for name in ("y", "c", "z", "x"))
    pos = jnp.stack([y, c, z, x_at]).astype(jnp.int32)
    nz = lax.axis_size("z")
    parts = nz * 2
    micro, _, shard_len, width = inputs.shape
    tokens = micro * shard_len
    seq_len = shard_len * parts
    part = width // 4
    cols = w_qkv.shape[2]

    qkv_mine = jnp.stack([w_qkv] + [ring(w_qkv, nz - k, nz) for k in range(1, nz)])
    qkv = spread(qkv_mine, "both")
    mix_mine = lax.all_gather(jnp.concatenate([w_down, w_out]), "z", axis=0, tiled=False)
    up_mine = lax.all_gather(w_up, "z", axis=0, tiled=False)
    mixes = spread(mix_mine, "y")
    ups = spread(up_mine, "x")

    def to_own(values):
        pieces = values.reshape(values.shape[:-1] + (2, 2, part))
        pieces = jnp.where(y == 1, pieces[..., ::-1, :, :], pieces)
        pieces = jnp.where(c == 1, pieces[..., ::-1, :], pieces)
        return jnp.swapaxes(pieces, -3, -2).reshape(values.shape)

    norms = lax.all_gather(jnp.concatenate([norm_gains, norm_biases]), ("y", "c"), axis=1, tiled=True)
    norms = to_own(norms).astype(F32)
    gains, shifts = norms[:4], norms[4:]
    x = to_own(inputs.reshape(tokens, width))
    cot = to_own(cotangent.reshape(tokens, width))

    row = jnp.arange(seq_len, dtype=jnp.int32)
    begins, cosines, sines = [], [], []
    for index in range(micro):
        starts = doc_starts[index, 0]
        begin = jnp.max(jnp.where(row[:, None] >= starts[None, :], starts[None, :], 0), axis=1)
        begins.append(begin)
        cosine, sine = angles_of(row - begin)
        cosines.append(jnp.concatenate([cosine, cosine, cosine, cosine], 1))
        sines.append(jnp.concatenate([-sine, sine, -sine, sine], 1))
    place = (z * 2 + x_at) * shard_len
    cos_own = jnp.concatenate([lax.dynamic_slice_in_dim(t, place, shard_len) for t in cosines])
    sin_own = jnp.concatenate([lax.dynamic_slice_in_dim(t, place, shard_len) for t in sines])

    *projected, normed1 = call_proj(pos, x, gains, shifts, cos_own, sin_own, qkv, shard_len)

    def exchange(values):
        return lax.all_to_all(values, SEQ, 0, 0, tiled=True)

    got, lses, att, att_local = [], [], [], []
    for index in range(micro):
        got.append(exchange(projected[index].reshape(parts, 3, shard_len, cols)))
        out, lse = call_attend(jnp.broadcast_to(begins[index][:, None], (seq_len, 128)), got[index])
        lses.append(lse)
        att_local.append(out)
        att.append(exchange(out))

    res = call_layer(pos, att, x, cot, gains, shifts, ups, mixes)
    outputs, att_all, normed2, act, g_up, g_b2, g_b1, g_hidden = res[:8]
    g_att, sums = res[8:11], res[11]
    up_parts, mix_parts = call_weight_grad(act, g_up, normed2, g_b2, att_all, g_b1)
    up_sum = lax.psum_scatter(collect(up_parts, "x"), "z", scatter_dimension=0, tiled=False)
    mix_sum = lax.psum_scatter(collect(mix_parts, "y"), "z", scatter_dimension=0, tiled=False)
    units = w_down.shape[0]
    down_sum, out_sum = mix_sum[:units], mix_sum[units:]

    back = []
    for index in range(micro):
        grad = exchange(g_att[index])
        res = call_attend_back(
            jnp.broadcast_to(begins[index][None], (8, seq_len)),
            cosines[index],
            sines[index],
            got[index],
            grad,
            att_local[index],
            lses[index],
        )
        back.append(exchange(res).reshape(nz, 2, 3, shard_len, cols))
    qkv_parts = collect(call_qkv_grad(pos, back, normed1), "both")
    qkv_sum = qkv_parts[0].astype(F32)
    for k in range(1, nz):
        qkv_sum = qkv_sum + ring(qkv_parts[k], k, nz).astype(F32)
    inputs_grad, sums0 = call_input_grad(pos, back, x, gains, g_hidden, qkv)
    norm_sums = total_norms(sums[:6], part)
    norm_sums0 = total_norms(sums0[:2], part)
    return (
        outputs.reshape(inputs.shape),
        inputs_grad.reshape(inputs.shape),
        qkv_sum,
        out_sum.astype(F32),
        up_sum.astype(F32),
        down_sum.astype(F32),
        jnp.concatenate([norm_sums0[:1], norm_sums[:3]]),
        jnp.concatenate([norm_sums0[1:], norm_sums[3:]]),
    )


def fits_fast(mesh, inputs, w_qkv, w_up):
    dp, tensor = mesh.shape["dp"], mesh.shape["tensor"]
    return (
        dp == 4
        and tensor == 8
        and inputs.shape[0] == 3
        and inputs.shape[1] == dp
        and inputs.shape[2] == 1024
        and w_qkv.shape[1:] == (1024, 1024)
        and w_up.shape[1] == 4096
    )


def solution(mesh):
    dp, tensor = mesh.shape["dp"], mesh.shape["tensor"]
    names = ("y", "c", "z", "x")
    fine = Mesh(mesh.devices.reshape(dp // 2, 2, 4, tensor // 4), names)
    rows, seq = ("y", "c"), ("z", "x")
    tokens = P(None, rows, seq, None)
    weights = (P(None, rows, seq), P(seq, rows), P(rows, seq), P(seq, rows))
    norm = P(None, rows)

    def run(*arrays):
        fast = fits_fast(mesh, arrays[0], arrays[2], arrays[4])
        return jax.shard_map(
            fast_shards if fast else shards,
            mesh=fine,
            in_specs=(tokens, P(None, rows, None)) + weights + (norm, norm, tokens),
            out_specs=(tokens, tokens) + weights + (norm, norm),
            check_vma=False,
        )(*arrays)

    return run
```

```python
import functools
import math

import jax
import jax.numpy as jnp
import numpy as np
from jax import lax
from jax.experimental import pallas as pl
from jax.experimental.pallas import tpu as pltpu
from jax.sharding import Mesh, PartitionSpec as P

HD = 64
EPSILON = 1e-05
F32 = jnp.float32
BF16 = jnp.bfloat16
CHIPS = ("y", "z", "x")
SEQ = ("z", "x")
SWAP = [(0, 1), (1, 0)]


def ln_forward(values, gain, shift):
    average = jnp.mean(values, axis=-1, keepdims=True)
    centred = values - average
    variance = jnp.mean(centred * centred, axis=-1, keepdims=True)
    scale = lax.rsqrt(variance + EPSILON)
    xhat = centred * scale
    return xhat * gain + shift, xhat, scale


def ln_backward(grad, xhat, scale, gain):
    e = grad * gain
    dv = scale * (
        e - jnp.mean(e, axis=-1, keepdims=True) - xhat * jnp.mean(e * xhat, axis=-1, keepdims=True)
    )
    return dv, jnp.sum(grad * xhat, axis=0), jnp.sum(grad, axis=0)


def rotate(values, cosines, sines):
    half_dim = values.shape[-1] // 2
    lower = values[..., :half_dim]
    upper = values[..., half_dim:]
    return jnp.concatenate(
        [lower * cosines - upper * sines, upper * cosines + lower * sines], axis=-1
    )


def doc_layout(starts, token_index):
    inside = token_index[:, None] >= starts[None, :]
    segment = jnp.sum(inside.astype(jnp.int32), axis=1)
    begins = jnp.max(jnp.where(inside, starts[None, :], 0), axis=1)
    return segment, token_index - begins


def angles_of(position):
    frequency = jnp.exp(
        jnp.arange(HD // 2, dtype=F32) * (-2.0 * math.log(10000.0) / HD)
    )
    angles = position.astype(F32)[..., None] * frequency
    return jnp.cos(angles), jnp.sin(angles)


def block_mask(segment, offset, block_len, key_len):
    query_pos = jnp.arange(offset, offset + block_len, dtype=jnp.int32)
    key_pos = jnp.arange(key_len, dtype=jnp.int32)
    causal = key_pos[None, :] <= query_pos[:, None]
    return causal & (segment[offset : offset + block_len, None] == segment[None, :key_len])


def attention_forward(q, k, v, segment):
    seq_len = q.shape[1]
    block_len = min(512, seq_len)
    pieces, lses = [], []
    for offset in range(0, seq_len, block_len):
        end = offset + block_len
        allowed = block_mask(segment, offset, block_len, end)[None]
        scores = 0.125 * jnp.einsum(
            "hqe,hke->hqk", q[:, offset:end], k[:, :end], preferred_element_type=F32
        )
        scores = jnp.where(allowed, scores, -1e30)
        peak = jnp.max(scores, axis=-1, keepdims=True)
        lse = peak + jnp.log(jnp.sum(jnp.exp(scores - peak), axis=-1, keepdims=True))
        probs = jnp.exp(scores - lse).astype(BF16)
        pieces.append(
            jnp.einsum("hqk,hke->hqe", probs, v[:, :end], preferred_element_type=F32).astype(BF16)
        )
        lses.append(lse)
    return jnp.concatenate(pieces, axis=1), lses


def attention_backward(q, k, v, do, lses, segment):
    seq_len = q.shape[1]
    block_len = min(512, seq_len)
    dq = []
    dk = jnp.zeros(k.shape, F32)
    dv = jnp.zeros(v.shape, F32)
    for index, offset in enumerate(range(0, seq_len, block_len)):
        end = offset + block_len
        allowed = block_mask(segment, offset, block_len, end)[None]
        qb, kb, vb, dob = q[:, offset:end], k[:, :end], v[:, :end], do[:, offset:end]
        scores = 0.125 * jnp.einsum("hqe,hke->hqk", qb, kb, preferred_element_type=F32)
        scores = jnp.where(allowed, scores, -1e30)
        soft = jnp.exp(scores - lses[index])
        probs = soft.astype(BF16)
        dp = jnp.einsum("hqe,hke->hqk", dob, vb, preferred_element_type=F32)
        dot = jnp.sum(soft * dp, axis=-1, keepdims=True)
        ds = (soft * (dp - dot)).astype(BF16)
        dq.append(0.125 * jnp.einsum("hqk,hke->hqe", ds, kb, preferred_element_type=F32))
        pad = ((0, 0), (0, seq_len - end), (0, 0))
        dk = dk + jnp.pad(
            0.125 * jnp.einsum("hqk,hqe->hke", ds, qb, preferred_element_type=F32), pad
        )
        dv = dv + jnp.pad(jnp.einsum("hqk,hqe->hke", probs, dob, preferred_element_type=F32), pad)
    return jnp.concatenate(dq, axis=1), dk, dv


def gather_both(shard):
    mine = lax.all_gather(shard, CHIPS, axis=0, tiled=False)
    return jnp.stack([mine, lax.ppermute(mine, "c", SWAP)])


def scatter_both(partial, sizes):
    ny, nz, nx = sizes
    shard_shape = partial.shape[2:]
    low = partial.astype(BF16)
    got = lax.ppermute(low[1], "c", SWAP)
    mine = (low[0].astype(F32) + got.astype(F32)).astype(BF16)
    mine = mine.reshape((ny, nz, nx) + shard_shape)
    mine = mine.transpose((0, 2, 1) + tuple(range(3, mine.ndim)))
    mine = mine.reshape((ny * nx, nz) + shard_shape)
    mine = lax.psum_scatter(mine, ("y", "x"), scatter_dimension=0, tiled=False)
    return lax.psum_scatter(mine, "z", scatter_dimension=0, tiled=False).astype(F32)


def shards(inputs, doc_starts, w_qkv, w_out, w_up, w_down, norm_gains, norm_biases, cotangent):
    ny, nz, nx = (lax.axis_size(name) for name in CHIPS)
    core = lax.axis_index("c")
    sizes = (ny, nz, nx)
    parts = nz * nx
    micro, _, shard_len, width = inputs.shape
    tokens = micro * shard_len
    seq_len = shard_len * parts
    dpart = width // (2 * ny)
    hcols = w_out.shape[0]
    heads = hcols // HD
    units = w_up.shape[1]

    def to_own(values):
        pieces = values.reshape(values.shape[:-1] + (ny, 2, dpart))
        pieces = jnp.where(core == 0, pieces, pieces[..., ::-1, :])
        return jnp.swapaxes(pieces, -3, -2).reshape(values.shape)

    def from_own(values):
        pieces = jnp.swapaxes(values.reshape(values.shape[:-1] + (2, ny, dpart)), -3, -2)
        return jnp.where(core == 0, pieces, pieces[..., ::-1, :]).reshape(values.shape)

    qkv_all = gather_both(w_qkv).reshape(2, ny, parts, 3, dpart, hcols)
    norms = jnp.stack([norm_gains, norm_biases])
    norms = gather_dp(norms, ny, dpart)
    norms = to_own(norms.astype(F32))
    gains, shifts = norms[0], norms[1]
    out_all = gather_both(w_out).reshape(2, ny, parts, hcols, dpart)
    up_all = gather_both(w_up).reshape(2, ny, parts, dpart, units)
    down_all = gather_both(w_down).reshape(2, ny, parts, units, dpart)

    qkv_full = qkv_all.transpose(0, 1, 4, 3, 2, 5).reshape(width, 3 * parts * hcols)
    out_full = out_all.transpose(2, 3, 0, 1, 4).reshape(parts * hcols, width)
    up_full = up_all.transpose(0, 1, 3, 2, 4).reshape(width, parts * units)
    down_full = down_all.transpose(2, 3, 0, 1, 4).reshape(parts * units, width)

    x = to_own(inputs.reshape(tokens, width)).astype(F32)
    cot = to_own(cotangent.reshape(tokens, width)).astype(F32)
    place = lax.axis_index(SEQ) * shard_len + jnp.arange(shard_len, dtype=jnp.int32)
    cos_own, sin_own, cos_row, sin_row, segments = [], [], [], [], []
    for index in range(micro):
        starts = doc_starts[index, 0]
        c, s = angles_of(doc_layout(starts, place)[1])
        cos_own.append(c)
        sin_own.append(s)
        segment, position = doc_layout(starts, jnp.arange(seq_len, dtype=jnp.int32))
        c, s = angles_of(position)
        cos_row.append(c)
        sin_row.append(s)
        segments.append(segment)
    cos_own = jnp.concatenate(cos_own)[:, None, None]
    sin_own = jnp.concatenate(sin_own)[:, None, None]

    normed1, xhat0, scale0 = ln_forward(x, gains[0], shifts[0])
    normed1 = normed1.astype(BF16)
    projected = jnp.dot(normed1, qkv_full, preferred_element_type=F32)
    projected = projected.reshape(tokens, 3, parts * heads, HD)
    rotated = rotate(projected[:, :2], cos_own, sin_own)
    projected = jnp.concatenate([rotated, projected[:, 2:]], axis=1).astype(BF16)
    projected = projected.reshape(micro, shard_len, 3, parts, hcols).transpose(0, 3, 2, 1, 4)

    def to_heads(values):
        kinds = values.shape[1]
        got = lax.all_to_all(values, SEQ, 0, 0, tiled=True)
        got = got.reshape(parts, kinds, shard_len, heads, HD).transpose(1, 3, 0, 2, 4)
        return got.reshape(kinds, heads, seq_len, HD)

    def to_tokens(values):
        kinds = values.shape[0]
        sent = values.reshape(kinds, heads, parts, shard_len, HD).transpose(2, 0, 3, 1, 4)
        sent = sent.reshape(parts, kinds, shard_len, hcols)
        return lax.all_to_all(sent, SEQ, 0, 0, tiled=True)

    qkvs, lses, attended = [], [], []
    for index in range(micro):
        q, k, v = to_heads(projected[index])
        out, lse = attention_forward(q, k, v, segments[index])
        qkvs.append((q, k, v))
        lses.append(lse)
        attended.append(to_tokens(out[None])[:, 0])
    attended = jnp.stack(attended).transpose(0, 2, 1, 3).reshape(tokens, parts * hcols)

    branch1 = jnp.dot(attended, out_full, preferred_element_type=F32)
    post1, xhat1, scale1 = ln_forward(branch1, gains[1], shifts[1])
    hidden = x + post1
    normed2, xhat2, scale2 = ln_forward(hidden, gains[2], shifts[2])
    normed2 = normed2.astype(BF16)
    up_act = jnp.dot(normed2, up_full, preferred_element_type=F32)
    gated, gate_pull = jax.vjp(lambda u: jax.nn.gelu(u, approximate=True), up_act)
    activated = gated.astype(BF16)
    branch2 = jnp.dot(activated, down_full, preferred_element_type=F32)
    post2, xhat3, scale3 = ln_forward(branch2, gains[3], shifts[3])
    outputs = (hidden + post2).astype(BF16)

    grad_branch2, gain3, shift3 = ln_backward(cot, xhat3, scale3, gains[3])
    grad_branch2 = grad_branch2.astype(BF16)
    down_part = jnp.einsum("tf,td->fd", activated, grad_branch2, preferred_element_type=F32)
    down_part = down_part.astype(BF16).reshape(parts, units, 2, ny, dpart)
    down_grad = scatter_both(
        down_part.transpose(2, 3, 0, 1, 4).reshape(2, ny * parts, units, dpart), sizes
    )
    grad_act = jnp.einsum("td,fd->tf", grad_branch2, down_full, preferred_element_type=F32)
    grad_up = gate_pull(grad_act)[0].astype(BF16)
    up_part = jnp.einsum("td,tf->df", normed2, grad_up, preferred_element_type=F32)
    up_part = up_part.astype(BF16).reshape(2, ny, dpart, parts, units)
    up_grad = scatter_both(
        up_part.transpose(0, 1, 3, 2, 4).reshape(2, ny * parts, dpart, units), sizes
    )
    grad_normed2 = jnp.einsum("tf,df->td", grad_up, up_full, preferred_element_type=F32)
    extra, gain2, shift2 = ln_backward(grad_normed2, xhat2, scale2, gains[2])
    grad_hidden = cot + extra
    grad_branch1, gain1, shift1 = ln_backward(grad_hidden, xhat1, scale1, gains[1])
    grad_branch1 = grad_branch1.astype(BF16)
    grad_attended = jnp.einsum(
        "td,fd->tf", grad_branch1, out_full, preferred_element_type=F32
    ).astype(BF16)
    grad_attended = grad_attended.reshape(micro, shard_len, parts, 1, hcols)
    grad_attended = grad_attended.transpose(0, 2, 3, 1, 4)
    out_part = jnp.einsum("tf,td->fd", attended, grad_branch1, preferred_element_type=F32)
    out_part = out_part.astype(BF16).reshape(parts, hcols, 2, ny, dpart)
    out_grad = scatter_both(
        out_part.transpose(2, 3, 0, 1, 4).reshape(2, ny * parts, hcols, dpart), sizes
    )

    grad_projected = []
    for index in range(micro):
        do = to_heads(grad_attended[index])[0]
        q, k, v = qkvs[index]
        dq, dk, dv = attention_backward(q, k, v, do, lses[index], segments[index])
        cos, sin = cos_row[index], -sin_row[index]
        back = jnp.stack([rotate(dq, cos, sin), rotate(dk, cos, sin), dv]).astype(BF16)
        grad_projected.append(to_tokens(back))
    grad_projected = jnp.stack(grad_projected).transpose(0, 3, 2, 1, 4)
    grad_projected = grad_projected.reshape(tokens, 3 * parts * hcols)
    qkv_part = jnp.einsum("td,te->de", normed1, grad_projected, preferred_element_type=F32)
    qkv_part = qkv_part.astype(BF16).reshape(2, ny, dpart, 3, parts, hcols)
    qkv_grad = scatter_both(
        qkv_part.transpose(0, 1, 4, 3, 2, 5).reshape(2, ny * parts, 3, dpart, hcols), sizes
    )
    grad_normed1 = jnp.einsum(
        "te,de->td", grad_projected, qkv_full, preferred_element_type=F32
    )
    extra, gain0, shift0 = ln_backward(grad_normed1, xhat0, scale0, gains[0])
    inputs_grad = grad_hidden + extra
    sums = jnp.stack([gain0, gain1, gain2, gain3, shift0, shift1, shift2, shift3])
    sums = lax.psum(from_own(sums), ("y", "c", "z", "x"))
    place = (lax.axis_index("y") * 2 + core) * dpart
    sums = lax.dynamic_slice_in_dim(sums, place, dpart, 1)
    return (
        from_own(outputs).reshape(inputs.shape),
        from_own(inputs_grad).reshape(inputs.shape),
        qkv_grad,
        out_grad,
        up_grad,
        down_grad,
        sums[:4],
        sums[4:],
    )


def gather_dp(norms, ny, dpart):
    full = lax.all_gather(norms, ("y", "c"), axis=2, tiled=True)
    return full


NT = (((1,), (1,)), ((), ()))
GELU_A = 0.7978845608
GELU_B = 0.044715


O = dict(cost=0.2, fcut=3, bcut=3, gate_mix=0, gate_up=0, gate_grad=1, gate_ab=1, gate_b1=1, qkv_half=2, up_z=0, order=0, gate_add=0, norm=1, gate_us=1)
O.update({})
COST = O["cost"]


def dot(a, b):
    return jnp.dot(a, b, preferred_element_type=F32)


def dot_nt(a, b):
    return lax.dot_general(a, b, NT, preferred_element_type=F32)


def params(semantics=1):
    return pltpu.CompilerParams(
        dimension_semantics=("arbitrary",) * semantics, vmem_limit_bytes=60 * 1024 * 1024
    )


def cost(flops, size, transcendentals=0):
    return pl.CostEstimate(
        flops=int(flops * COST), bytes_accessed=int(size * COST), transcendentals=int(transcendentals * COST)
    )


def whole(shape):
    return pl.BlockSpec(shape, lambda *_: (0,) * len(shape))


def swap_halves(values):
    lane = lax.broadcasted_iota(jnp.int32, values.shape, 1)
    low = lax.rem(lane, HD) < HD // 2
    return jnp.where(low, pltpu.roll(values, 96, 1), pltpu.roll(values, 32, 1))


def row_stats(values):
    average = jnp.mean(values, axis=-1, keepdims=True)
    centred = values - average
    variance = jnp.mean(centred * centred, axis=-1, keepdims=True)
    scale = lax.rsqrt(variance + EPSILON)
    return centred * scale, scale


def row_pull(grad, xhat, scale, gain):
    e = grad * gain
    return scale * (
        e - jnp.mean(e, axis=-1, keepdims=True) - xhat * jnp.mean(e * xhat, axis=-1, keepdims=True)
    )


def column_sum(values):
    return jnp.sum(values, axis=0, keepdims=True)


def own_place(pos, q, part):
    place = lax.bitwise_xor(pos[0], q % 2) * 2 + lax.bitwise_xor(pos[1], q // 2)
    return pl.multiple_of(place * part, part)


def load_columns(ref, pos, part):
    return jnp.concatenate([ref[:, pl.ds(own_place(pos, q, part), part)] for q in range(4)], 1)


def store_columns(ref, values, pos, part):
    for q in range(4):
        ref[:, pl.ds(own_place(pos, q, part), part)] = values[:, q * part : (q + 1) * part].astype(
            ref.dtype
        )


def tables(seq_len):
    lane = np.arange(128)
    frequency = np.exp((lane % (HD // 2)) * (-2.0 * math.log(10000.0) / HD))
    angle = np.arange(seq_len)[:, None] * frequency.astype(np.float32).astype(np.float64)
    sign = np.where(lane % HD < HD // 2, -1.0, 1.0)
    return np.cos(angle).astype(np.float32), (np.sin(angle) * sign).astype(np.float32)


def start_tables(starts):
    lane = jnp.arange(128)
    frequency = jnp.exp((lane % (HD // 2)).astype(F32) * (-2.0 * math.log(10000.0) / HD))
    angle = starts.astype(F32)[..., None] * frequency
    return jnp.cos(angle), jnp.sin(angle) * jnp.where(lane % HD < HD // 2, -1.0, 1.0)


def angle_rows(rows, starts, base, table, start_cos, start_sin):
    cb, sb = start_cos[0:1], start_sin[0:1]
    for d in range(1, 4):
        inside = rows >= starts[base + d]
        cb = jnp.where(inside, start_cos[d : d + 1], cb)
        sb = jnp.where(inside, start_sin[d : d + 1], sb)
    tc, ts = table
    return tc * cb + ts * sb, ts * cb - tc * sb


def begin_of(rows, starts, base):
    begin = jnp.zeros(rows.shape, jnp.int32)
    for d in range(1, 4):
        begin = jnp.where(rows >= starts[base + d], starts[base + d], begin)
    return begin


def proj_kernel(pos, starts, x, gains, shifts, tcos, tsin, start_cos, start_sin, *refs):
    weights = [refs[2 * q : 2 * q + 2] for q in range(4)]
    first, last, keep, send = refs[8:12]
    normed, cos, sin = refs[12:15]
    outs = [first.at[0, :, 0], first.at[0, :, 1], last.at[0, :, 0]]
    part = weights[0][0].shape[2]
    count = first.shape[4]

    @pl.when(pl.program_id(0) == 0)
    def _():
        xhat, _ = row_stats(load_columns(x, pos, part).astype(F32))
        value = (xhat * gains[0:1] + shifts[0:1]).astype(BF16)
        normed[...] = value
        keep[...] = value[:, : 2 * part]
        send[...] = value[:, 2 * part :]
        rows = lax.broadcasted_iota(jnp.int32, (count, 128), 0) + (pos[2] * 2 + pos[3]) * count
        for m in range(3):
            at = slice(m * count, (m + 1) * count)
            cos[at], sin[at] = angle_rows(
                rows, starts, 4 * m, (tcos[...], tsin[...]), start_cos.at[m], start_sin.at[m]
            )

    total = None
    for q in range(4):
        block = jnp.concatenate([weights[q][dx][0, kind] for dx in range(2) for kind in range(3)], 1)
        term = dot(normed[:, q * part : (q + 1) * part], block)
        total = term if total is None else total + term
    for dx in range(2):
        place = lax.bitwise_xor(pos[3], dx)
        for kind in range(3):
            at = (dx * 3 + kind) * 128
            u = total[:, at : at + 128]
            if kind < 2:
                u = u * cos[...] + swap_halves(u) * sin[...]
            u = u.astype(BF16)
            for m in range(3):
                outs[m][place, kind] = u[m * count : (m + 1) * count]


def ring_place(pos, i, nz):
    return lax.rem(pos[2] + i, nz)


def head_index(nz):
    return lambda i, pos, *_: (ring_place(pos, i, nz), 0, 0, 0, 0, 0)


def call_proj(pos, starts, x, gains, shifts, table, start_table, pieces, shard_len):
    tokens, width = x.shape
    nz, _, part, cols = pieces[0][0].shape
    piece = pl.BlockSpec((1, 3, part, cols), lambda i, *_: (i, 0, 0, 0))
    outs = [pl.BlockSpec((1, 2, n, 3, shard_len, cols), head_index(nz)) for n in (2, 1)]
    shapes = [jax.ShapeDtypeStruct((nz, 2, n, 3, shard_len, cols), BF16) for n in (2, 1)]
    half = (tokens, width // 2)
    rows = pl.BlockSpec((shard_len, 128), lambda i, pos, _: (pos[2] * 2 + pos[3], 0))
    return pl.pallas_call(
        proj_kernel,
        grid_spec=pltpu.PrefetchScalarGridSpec(
            num_scalar_prefetch=2,
            grid=(nz,),
            in_specs=[whole(a.shape) for a in (x, gains, shifts)]
            + [rows] * 2
            + [whole(a.shape) for a in start_table]
            + [piece] * 8,
            out_specs=outs + [whole(half)] * 2,
            scratch_shapes=[
                pltpu.VMEM((tokens, width), BF16),
                pltpu.VMEM((tokens, 128), F32),
                pltpu.VMEM((tokens, 128), F32),
            ],
        ),
        out_shape=shapes + [jax.ShapeDtypeStruct(half, BF16)] * 2,
        compiler_params=params(),
        cost_estimate=cost(2 * tokens * width * 3 * nz * 2 * cols, 12e6),
        name="project",
    )(pos, starts, x, gains, shifts, *table, *start_table, *[p for pair in pieces for p in pair])


def head_mask(shape, head):
    lane = lax.broadcasted_iota(jnp.int32, shape, 1)
    return (lane < HD) if head == 0 else (lane >= HD)


def attend_kernel(first, starts, got, out, lse_out):
    micro = first + pl.program_id(0)
    shards_n, _, count, lanes = got.shape
    seq_len = shards_n * count
    block = min(256, seq_len)
    q_all = (got[:, 0] * 0.125).reshape(seq_len, lanes)
    k_all = got[:, 1].reshape(seq_len, lanes)
    v_all = got[:, 2].reshape(seq_len, lanes)
    per = block // count
    for start in range(0, seq_len, block):
        end = start + block
        qb = q_all[start:end]
        key = lax.broadcasted_iota(jnp.int32, (block, end), 1)
        query = start + lax.broadcasted_iota(jnp.int32, (block, end), 0)
        begin = begin_of(start + lax.broadcasted_iota(jnp.int32, (block, 1), 0), starts, 4 * micro)
        allowed = (key <= query) & (key >= begin)
        results = []
        for head in range(2):
            mask = head_mask(qb.shape, head)
            scores = dot_nt(jnp.where(mask, qb, 0), k_all[:end])
            scores = jnp.where(allowed, scores, -1e30)
            peak = jnp.max(scores, axis=-1, keepdims=True)
            e = jnp.exp(scores - peak)
            total = jnp.sum(e, axis=-1, keepdims=True)
            results.append(dot(e.astype(BF16), v_all[:end]) / total)
            lse = jnp.broadcast_to(peak + jnp.log(total), (block, 128))
            lse_out[head : head + 1, start:end] = jnp.transpose(lse)[0:1]
        mixed = jnp.where(head_mask(results[0].shape, 0), results[0], results[1]).astype(BF16)
        out[start // count : end // count] = mixed.reshape(per, count, lanes)


def call_attend(first, starts, got):
    parts, number, _, count, lanes = got.shape
    seq_len = parts * count
    return pl.pallas_call(
        functools.partial(attend_kernel, first),
        grid_spec=pltpu.PrefetchScalarGridSpec(
            num_scalar_prefetch=1,
            grid=(number,),
            in_specs=[pl.BlockSpec((parts, None, 3, count, lanes), lambda i, _: (0, i, 0, 0, 0))],
            out_specs=[
                pl.BlockSpec((parts, None, count, lanes), lambda i, _: (0, i, 0, 0)),
                pl.BlockSpec((None, 8, seq_len), lambda i, _: (i, 0, 0)),
            ],
        ),
        out_shape=[
            jax.ShapeDtypeStruct((parts, number, count, lanes), BF16),
            jax.ShapeDtypeStruct((number, 8, seq_len), F32),
        ],
        compiler_params=params(),
        cost_estimate=cost(
            number * 8 * seq_len * seq_len * lanes, number * 2e6, number * 2 * seq_len * seq_len
        ),
        name="attend",
    )(starts, got)


def attend_back_kernel(
    first, starts, tcos, tsin, start_cos, start_sin, got, grad, att, lse, out, dq_ref, dk_ref, dv_ref
):
    micro = first + pl.program_id(0)
    shards_n, _, count, lanes = got.shape
    seq_len = shards_n * count
    block = min(256, seq_len)
    q_all = (got[:, 0] * 0.125).reshape(seq_len, lanes)
    k_all = got[:, 1].reshape(seq_len, lanes)
    v_all = got[:, 2].reshape(seq_len, lanes)
    do_all = grad[...].reshape(seq_len, lanes)
    prod = do_all.astype(F32) * att[...].reshape(seq_len, lanes).astype(F32)
    prod = jnp.transpose(prod)
    deltas = [
        jnp.sum(prod[:HD], axis=0, keepdims=True),
        jnp.sum(prod[HD:], axis=0, keepdims=True),
    ]
    begins = begin_of(lax.broadcasted_iota(jnp.int32, (1, seq_len), 1), starts, 4 * micro)
    for start in range(0, seq_len, block):
        end = start + block
        kb, vb = k_all[start:end], v_all[start:end]
        qs, dos = q_all[start:], do_all[start:]
        span = seq_len - start
        key = start + lax.broadcasted_iota(jnp.int32, (block, span), 0)
        query = start + lax.broadcasted_iota(jnp.int32, (block, span), 1)
        allowed = (key <= query) & (key >= begins[:, start:])
        dks, dvs, dqs = [], [], []
        for head in range(2):
            mask = head_mask(kb.shape, head)
            scores = dot_nt(jnp.where(mask, kb, 0), qs)
            soft = jnp.exp(jnp.where(allowed, scores, -1e30) - lse[head : head + 1, start:])
            pull = dot_nt(jnp.where(mask, vb, 0), dos)
            ds = (soft * (pull - deltas[head][:, start:])).astype(BF16)
            dvs.append(dot(soft.astype(BF16), dos))
            dks.append(dot(ds, qs))
            dqs.append(
                lax.dot_general(ds, kb, (((0,), (0,)), ((), ())), preferred_element_type=F32)
            )
        low = head_mask(kb.shape, 0)
        dk_ref[start:end] = jnp.where(low, dks[0], dks[1])
        dv_ref[start:end] = jnp.where(low, dvs[0], dvs[1])
        dq = jnp.where(head_mask(dqs[0].shape, 0), dqs[0], dqs[1])
        if start == 0:
            dq_ref[...] = dq
        else:
            dq_ref[start:] += dq
    rows = lax.broadcasted_iota(jnp.int32, (seq_len, lanes), 0)
    cos, sin = angle_rows(
        rows, starts, 4 * micro, (tcos[...], tsin[...]), start_cos.at[micro], start_sin.at[micro]
    )
    for kind, ref in enumerate((dq_ref, dk_ref, dv_ref)):
        u = ref[...]
        if kind == 0:
            u = u * 0.125
        if kind < 2:
            u = u * cos - swap_halves(u) * sin
        out[:, kind] = u.astype(BF16).reshape(shards_n, count, lanes)


def call_attend_back(first, starts, table, start_table, got, grads, att, lse):
    parts, number, _, count, lanes = got.shape
    seq_len = parts * count
    return pl.pallas_call(
        functools.partial(attend_back_kernel, first),
        grid_spec=pltpu.PrefetchScalarGridSpec(
            num_scalar_prefetch=1,
            grid=(number,),
            in_specs=[whole(a.shape) for a in (*table, *start_table)]
            + [
                pl.BlockSpec((parts, None, 3, count, lanes), lambda i, _: (0, i, 0, 0, 0)),
                pl.BlockSpec((parts, None, count, lanes), lambda i, _: (0, first + i, 0, 0)),
                pl.BlockSpec((parts, None, count, lanes), lambda i, _: (0, i, 0, 0)),
                pl.BlockSpec((None, 8, seq_len), lambda i, _: (i, 0, 0)),
            ],
            out_specs=pl.BlockSpec((parts, None, 3, count, lanes), lambda i, _: (0, i, 0, 0, 0)),
            scratch_shapes=[pltpu.VMEM((seq_len, lanes), F32)] * 3,
        ),
        out_shape=jax.ShapeDtypeStruct((parts, number, 3, count, lanes), BF16),
        compiler_params=params(),
        cost_estimate=cost(
            number * 20 * seq_len * seq_len * lanes, number * 4e6, number * 2 * seq_len * seq_len
        ),
        name="attend_back",
    )(starts, *table, *start_table, got, grads, att, lse)


def mix_block(mixes, q, k):
    return jnp.concatenate([mixes[q][0][k], mixes[q][1][k]], 0)


def add_into(ref, cols, first, value):
    @pl.when(first)
    def _():
        ref[:, cols] = value

    @pl.when(jnp.logical_not(first))
    def _():
        ref[:, cols] += value


def layer_kernel(pos, *refs):
    att = [refs[0].at[:, 0], refs[0].at[:, 1], refs[1].at[:, 0]]
    x, cot, gains, shifts = refs[2:6]
    ups = [refs[6 + 2 * q : 8 + 2 * q] for q in range(4)]
    downs = [refs[14 + 2 * q : 16 + 2 * q] for q in range(4)]
    mixes = [refs[22 + 2 * q : 24 + 2 * q] for q in range(4)]
    outputs, att_all, act, slope, keep, send, xhat1, scale1, xhat2, scale2, sums = refs[30:41]
    normed, hidden, total = refs[41:44]
    nz = mixes[0][0].shape[0]
    count = refs[0].shape[2]
    part = downs[0][0].shape[2]
    step = pl.program_id(0)

    def hand_out(index, value):
        keep[index] = value[:, : 2 * part]
        send[index] = value[:, 2 * part :]

    @pl.when(step == 0)
    def _():
        for k in range(nz):
            for dx in range(2):
                place = ring_place(pos, k, nz) * 2 + lax.bitwise_xor(pos[3], dx)
                for m in range(3):
                    at = (k * 2 + dx) * 128
                    att_all[m * count : (m + 1) * count, at : at + 128] = att[m][place]
        for q in range(4):
            acc = None
            for k in range(nz):
                term = dot(att_all[:, k * 256 : (k + 1) * 256], mix_block(mixes, q, k))
                acc = term if acc is None else acc + term
            total[:, q * part : (q + 1) * part] = acc
        xhat, scale = row_stats(total[...])
        xhat1[...] = xhat
        scale1[...] = jnp.broadcast_to(scale, scale1.shape)
        value = load_columns(x, pos, part).astype(F32) + xhat * gains[1:2] + shifts[1:2]
        hidden[...] = value
        xhat, scale = row_stats(value)
        xhat2[...] = xhat
        scale2[...] = jnp.broadcast_to(scale, scale2.shape)
        value = (xhat * gains[2:3] + shifts[2:3]).astype(BF16)
        normed[...] = value
        hand_out(0, value)

    for dx in range(2):
        u = None
        for q in range(4):
            term = dot(normed[:, q * part : (q + 1) * part], ups[q][dx][...])
            u = term if u is None else u + term
        square = u * u
        t = jnp.tanh(GELU_A * (u * (1.0 + GELU_B * square)))
        half = 0.5 * (1.0 + t)
        act[0, dx] = (u * half).astype(BF16)
        bend = half + (0.5 * GELU_A) * u * (1.0 - t * t) * (1.0 + 3.0 * GELU_B * square)
        slope[0, dx] = bend.astype(BF16)
    for q in range(4):
        term = dot(act[0, 0], downs[q][0][0]) + dot(act[0, 1], downs[q][1][0])
        add_into(total, slice(q * part, (q + 1) * part), step == 0, term)

    @pl.when(step == nz - 1)
    def _():
        xhat, scale = row_stats(total[...])
        value = hidden[...] + xhat * gains[3:4] + shifts[3:4]
        store_columns(outputs, value, pos, part)
        grad = load_columns(cot, pos, part).astype(F32)
        sums[0:1] = column_sum(grad * xhat)
        sums[1:2] = column_sum(grad)
        hand_out(1, row_pull(grad, xhat, scale, gains[3:4]).astype(BF16))


def layer_specs(units, part, rows, nz, order):
    def up_spec(dy, dx):
        def index(i, pos):
            place = lax.bitwise_xor(pos[0], dy) * 2 + lax.bitwise_xor(pos[3], dx)
            return (place, ring_place(pos, order(i), nz), 0, 0)

        return pl.BlockSpec((None, None, part, units), index)

    ups = [up_spec(dy, dx) for _ in range(2) for dy in range(2) for dx in range(2)]
    down = pl.BlockSpec((1, units, part), lambda i, pos: (order(i), 0, 0))
    mix = pl.BlockSpec((nz, rows, part), lambda i, pos: (0, units // rows, 0))
    return ups + [down] * 8 + [mix] * 8


def layer_weights(ups, mixes):
    mixes_flat = [p for pair in mixes for p in pair]
    return [ups[0]] * 4 + [ups[1]] * 4 + mixes_flat * 2


def call_layer(pos, att, x, cot, gains, shifts, ups, mixes):
    tokens, width = x.shape
    _, nz, part, units = ups[0].shape
    rows = mixes[0][0].shape[1] - units
    act = pl.BlockSpec((1, 2, tokens, units), lambda i, pos: (i, 0, 0, 0))
    flat, column = (tokens, width), (tokens, 128)
    side = (2, tokens, width // 2)
    ffn = jax.ShapeDtypeStruct((nz, 2, tokens, units), BF16)
    low = jax.ShapeDtypeStruct(flat, BF16)
    return pl.pallas_call(
        layer_kernel,
        grid_spec=pltpu.PrefetchScalarGridSpec(
            num_scalar_prefetch=1,
            grid=(nz,),
            in_specs=[whole(a.shape) for a in (*att, x, cot, gains, shifts)]
            + layer_specs(units, part, rows, nz, lambda i: i),
            out_specs=[whole(flat)] * 2
            + [act] * 2
            + [whole(side)] * 2
            + [whole(flat), whole(column)] * 2
            + [whole((8, width))],
            scratch_shapes=[pltpu.VMEM(flat, BF16), pltpu.VMEM(flat, F32), pltpu.VMEM(flat, F32)],
        ),
        out_shape=[low, low, ffn, ffn]
        + [jax.ShapeDtypeStruct(side, BF16)] * 2
        + [jax.ShapeDtypeStruct(flat, F32), jax.ShapeDtypeStruct(column, F32)] * 2
        + [jax.ShapeDtypeStruct((8, width), F32)],
        compiler_params=params(),
        cost_estimate=cost(
            2 * tokens * width * (2 * nz * 2 * units + width), 40e6, tokens * nz * 2 * units
        ),
        name="layer",
    )(pos, *att, x, cot, gains, shifts, *layer_weights(ups, mixes))


def layer_back_kernel(pos, *refs):
    cot, gains, xhat1, scale1, xhat2, scale2, slope, keep, send = refs[0:9]
    ups = [refs[9 + 2 * q : 11 + 2 * q] for q in range(4)]
    downs = [refs[17 + 2 * q : 19 + 2 * q] for q in range(4)]
    mixes = [refs[25 + 2 * q : 27 + 2 * q] for q in range(4)]
    g_up, keep_out, send_out, g_hidden, g_att, sums, total = refs[33:40]
    nz = mixes[0][0].shape[0]
    count = g_att.shape[2]
    part = downs[0][0].shape[2]
    step = pl.program_id(0)
    g_b2 = [keep[1, :, :part], keep[1, :, part:], send[1, :, :part], send[1, :, part:]]
    for dx in range(2):
        g = None
        for q in range(4):
            term = dot_nt(g_b2[q], downs[q][dx][0])
            g = term if g is None else g + term
        g_up[0, dx] = (g * slope[0, dx].astype(F32)).astype(BF16)
    for q in range(4):
        term = dot_nt(g_up[0, 0], ups[q][0][...]) + dot_nt(g_up[0, 1], ups[q][1][...])
        add_into(total, slice(q * part, (q + 1) * part), step == 0, term)

    @pl.when(step == nz - 1)
    def _():
        grad = total[...]
        xhat = xhat2[...]
        sums[1:2] = column_sum(grad * xhat)
        sums[3:4] = column_sum(grad)
        grad = load_columns(cot, pos, part).astype(F32) + row_pull(
            grad, xhat, scale2[:, 0:1], gains[2:3]
        )
        g_hidden[...] = grad
        xhat = xhat1[...]
        sums[0:1] = column_sum(grad * xhat)
        sums[2:3] = column_sum(grad)
        g_b1 = row_pull(grad, xhat, scale1[:, 0:1], gains[1:2]).astype(BF16)
        keep_out[...] = g_b1[:, : 2 * part]
        send_out[...] = g_b1[:, 2 * part :]
        for k in range(nz):
            acc = None
            for q in range(4):
                term = dot_nt(g_b1[:, q * part : (q + 1) * part], mix_block(mixes, q, k))
                acc = term if acc is None else acc + term
            acc = acc.astype(BF16)
            for dx in range(2):
                place = ring_place(pos, k, nz) * 2 + lax.bitwise_xor(pos[3], dx)
                for m in range(3):
                    g_att[place, m] = acc[m * count : (m + 1) * count, dx * 128 : (dx + 1) * 128]


def call_layer_back(pos, cot, gains, kept, slope, keep, send, ups, mixes, count):
    tokens, width = cot.shape
    _, nz, part, units = ups[0].shape
    rows = mixes[0][0].shape[1] - units
    turn = nz - 1
    act = pl.BlockSpec((1, 2, tokens, units), lambda i, pos: (turn - i, 0, 0, 0))
    flat, half = (tokens, width), (tokens, width // 2)
    heads = (2 * nz, tokens // count, count, rows)
    return pl.pallas_call(
        layer_back_kernel,
        grid_spec=pltpu.PrefetchScalarGridSpec(
            num_scalar_prefetch=1,
            grid=(nz,),
            in_specs=[whole(a.shape) for a in (cot, gains, *kept)]
            + [act, whole(keep.shape), whole(send.shape)]
            + layer_specs(units, part, rows, nz, lambda i: turn - i),
            out_specs=[act, whole(half), whole(half), whole(flat), whole(heads), whole((8, width))],
            scratch_shapes=[pltpu.VMEM(flat, F32)],
        ),
        out_shape=[
            jax.ShapeDtypeStruct(slope.shape, BF16),
            jax.ShapeDtypeStruct(half, BF16),
            jax.ShapeDtypeStruct(half, BF16),
            jax.ShapeDtypeStruct(flat, F32),
            jax.ShapeDtypeStruct(heads, BF16),
            jax.ShapeDtypeStruct((8, width), F32),
        ],
        compiler_params=params(),
        cost_estimate=cost(2 * tokens * width * (2 * nz * 2 * units + width), 40e6),
        name="layer_back",
    )(pos, cot, gains, *kept, slope, keep, send, *layer_weights(ups, mixes))


def place_piece(outs, dy, dx, cut, index, value):
    if dy == 0 and dx == 0:
        outs[0][index] = value
        return
    low, high = outs[1 + 2 * (2 * dy + dx - 1) :][:2]
    step = pl.program_id(0)

    @pl.when(step < cut)
    def _():
        low[index] = value

    @pl.when(step >= cut)
    def _():
        high[index] = value


def piece_specs(block, nz, cut):
    zeros = (0,) * (len(block) - 1)
    low = pl.BlockSpec(block, lambda i, *_: (jnp.minimum(i, cut - 1),) + zeros)
    high = pl.BlockSpec(block, lambda i, *_: (jnp.maximum(i - cut, 0),) + zeros)
    specs = [pl.BlockSpec(block, lambda i, *_: (i,) + zeros)] + [low, high] * 3
    shapes = [nz] + [cut, nz - cut] * 3
    return specs, [jax.ShapeDtypeStruct((n,) + block[1:], BF16) for n in shapes]


def down_grad_kernel(cut, act, act2, keep, recv, *outs):
    part = outs[0].shape[2]
    for dx in range(2):
        side = jnp.concatenate([jnp.transpose(act[0, dx]), jnp.transpose(act2[0, dx])], 1)
        for dy in range(2):
            cols = slice(dy * part, (dy + 1) * part)
            grad = jnp.concatenate([keep[0, :, cols], recv[0, :, cols]], 0)
            place_piece(outs, dy, dx, cut, 0, dot(side, grad).astype(BF16))


def call_down_grad(cut, act, act2, keep, recv):
    nz, _, tokens, units = act.shape
    half = keep.shape[2]
    ffn = pl.BlockSpec((1, 2, tokens, units), lambda i: (i, 0, 0, 0))
    specs, shapes = piece_specs((1, units, half // 2), nz, cut)
    side = pl.BlockSpec((1, tokens, half), lambda i: (1, 0, 0))
    return pl.pallas_call(
        functools.partial(down_grad_kernel, cut),
        grid=(nz,),
        in_specs=[ffn, ffn, side, side],
        out_specs=specs,
        out_shape=shapes,
        compiler_params=params(),
        cost_estimate=cost(2 * tokens * 2 * half * nz * 2 * units, 16e6),
        name="down_grad",
    )(act, act2, keep, recv)


def up_grad_kernel(pos, g_up, g_up2, keep, recv, keep1, recv1, att, att2, out, flipped):
    part, units = g_up.shape[3] // 2, g_up.shape[3]
    tokens = g_up.shape[2]

    @pl.when(pl.program_id(0) == 0)
    def _():
        flipped[:, :tokens] = jnp.transpose(keep[0])
        flipped[:, tokens:] = jnp.transpose(recv[0])

    side = jnp.concatenate([jnp.transpose(att[...]), jnp.transpose(att2[...])], 1)
    for dy in range(2):
        cols = slice(dy * part, (dy + 1) * part)
        both = dot(side, jnp.concatenate([keep1[:, cols], recv1[:, cols]], 0)).astype(BF16)
        for dx in range(2):
            place = lax.bitwise_xor(pos[0], dy) * 2 + lax.bitwise_xor(pos[3], dx)
            grad = jnp.concatenate([g_up[0, dx], g_up2[0, dx]], 0)
            out[place, 0, :part] = dot(flipped[cols], grad).astype(BF16)
            rows = both[dx * 128 : (dx + 1) * 128]
            out[place, 0, part:] = jnp.concatenate([rows[:64], rows[64:]], 1)


def call_up_grad(pos, g_up, g_up2, keep, recv, keep1, recv1, att, att2):
    nz, _, tokens, units = g_up.shape
    half = keep.shape[2]
    part = half // 2
    heads = att.shape[1] // nz
    rows = part + heads // 4
    ffn = pl.BlockSpec((1, 2, tokens, units), lambda i, pos: (i, 0, 0, 0))
    side = pl.BlockSpec((1, tokens, half), lambda i, pos: (0, 0, 0))
    head = pl.BlockSpec((tokens, heads), lambda i, pos: (0, i))
    return pl.pallas_call(
        up_grad_kernel,
        grid_spec=pltpu.PrefetchScalarGridSpec(
            num_scalar_prefetch=1,
            grid=(nz,),
            in_specs=[ffn, ffn, side, side, whole(keep1.shape), whole(keep1.shape), head, head],
            out_specs=pl.BlockSpec(
                (4, 1, rows, units), lambda i, pos: (0, ring_place(pos, i, nz), 0, 0)
            ),
            scratch_shapes=[pltpu.VMEM((half, 2 * tokens), BF16)],
        ),
        out_shape=jax.ShapeDtypeStruct((4, nz, rows, units), BF16),
        compiler_params=params(),
        cost_estimate=cost(2 * tokens * 2 * half * nz * 2 * units, 16e6),
        name="up_grad",
    )(pos, g_up, g_up2, keep, recv, keep1, recv1, att, att2)


def load_grads(pos, grads):
    columns = []
    for dx in range(2):
        place = lax.bitwise_xor(pos[3], dx)
        for kind in range(3):
            rows = [g[0, place, m, kind] for g in grads for m in range(g.shape[2])]
            columns.append(jnp.concatenate(rows, 0))
    return jnp.concatenate(columns, 1)


def qkv_grad_kernel(cut, pos, *refs):
    grads, keep, recv = refs[0:4], refs[4], refs[5]
    outs, flipped = refs[6:13], refs[13]
    part = outs[0].shape[2]
    tokens = keep.shape[0]

    @pl.when(pl.program_id(0) == 0)
    def _():
        flipped[:, :tokens] = jnp.transpose(keep[...])
        flipped[:, tokens:] = jnp.transpose(recv[...])

    block = load_grads(pos, grads)
    for dy in range(2):
        res = dot(flipped[dy * part : (dy + 1) * part], block).astype(BF16)
        for dx in range(2):
            for kind in range(3):
                at = (dx * 3 + kind) * 128
                place_piece(outs, dy, dx, cut, (0, kind), res[:, at : at + 128])


def call_qkv_grad(cut, pos, grads, grads2, keep, recv):
    nz, _, _, _, count, cols = grads[0].shape
    tokens, half = keep.shape
    part = half // 2
    grad_specs = [pl.BlockSpec((1,) + g.shape[1:], head_index(nz)) for g in grads]
    specs, shapes = piece_specs((1, 3, part, cols), nz, cut)
    return pl.pallas_call(
        functools.partial(qkv_grad_kernel, cut),
        grid_spec=pltpu.PrefetchScalarGridSpec(
            num_scalar_prefetch=1,
            grid=(nz,),
            in_specs=grad_specs * 2 + [whole(keep.shape)] * 2,
            out_specs=specs,
            scratch_shapes=[pltpu.VMEM((half, 2 * tokens), BF16)],
        ),
        out_shape=shapes,
        compiler_params=params(),
        cost_estimate=cost(2 * tokens * 2 * half * 3 * nz * 2 * cols, 12e6),
        name="qkv_grad",
    )(pos, *grads, *grads2, keep, recv)


def input_grad_kernel(pos, *refs):
    grads, x, gains, g_hidden = refs[0:2], refs[2], refs[3], refs[4]
    weights = [refs[5 + 2 * q : 7 + 2 * q] for q in range(4)]
    out, sums, total = refs[13:16]
    part = weights[0][0].shape[2]
    step = pl.program_id(0)
    block = load_grads(pos, grads)
    for q in range(4):
        side = jnp.concatenate([weights[q][dx][0, kind] for dx in range(2) for kind in range(3)], 1)
        term = dot_nt(block, side)

        @pl.when(step == 0)
        def _():
            total[:, q * part : (q + 1) * part] = term

        @pl.when(step > 0)
        def _():
            total[:, q * part : (q + 1) * part] += term

    @pl.when(step == pl.num_programs(0) - 1)
    def _():
        grad = total[...]
        xhat, scale = row_stats(load_columns(x, pos, part).astype(F32))
        sums[0:1] = column_sum(grad * xhat)
        sums[1:2] = column_sum(grad)
        value = g_hidden[...] + row_pull(grad, xhat, scale, gains[0:1])
        store_columns(out, value, pos, part)


def call_input_grad(pos, grads, x, gains, g_hidden, pieces):
    nz, _, _, _, count, cols = grads[0].shape
    tokens, width = x.shape
    part = width // 4
    grad_specs = [pl.BlockSpec((1,) + g.shape[1:], head_index(nz)) for g in grads]
    piece = pl.BlockSpec((1, 3, part, cols), lambda i, pos: (i, 0, 0, 0))
    return pl.pallas_call(
        input_grad_kernel,
        grid_spec=pltpu.PrefetchScalarGridSpec(
            num_scalar_prefetch=1,
            grid=(nz,),
            in_specs=grad_specs + [whole(a.shape) for a in (x, gains, g_hidden)] + [piece] * 8,
            out_specs=[whole((tokens, width)), whole((8, width))],
            scratch_shapes=[pltpu.VMEM((tokens, width), F32)],
        ),
        out_shape=[
            jax.ShapeDtypeStruct((tokens, width), F32),
            jax.ShapeDtypeStruct((8, width), F32),
        ],
        compiler_params=params(),
        cost_estimate=cost(2 * tokens * width * 3 * nz * 2 * cols, 16e6),
        name="input_grad",
    )(pos, *grads, x, gains, g_hidden, *[p for pair in pieces for p in pair])


def sum_kernel(*refs):
    total = refs[0][...].astype(F32)
    for ref in refs[1:-1]:
        total = total + ref[...].astype(F32)
    refs[-1][...] = total.astype(BF16)


def add(*values):
    shape = values[0].shape
    block = pl.BlockSpec((1,) + shape[1:], lambda i: (i,) + (0,) * (len(shape) - 1))
    return pl.pallas_call(
        sum_kernel,
        grid=(shape[0],),
        in_specs=[block] * len(values),
        out_specs=block,
        out_shape=jax.ShapeDtypeStruct(shape, BF16),
        compiler_params=params(),
        cost_estimate=cost(values[0].size * len(values), 2 * values[0].size * (len(values) + 1)),
        name="add",
    )(*values)


def sum_cut_kernel(cut, pos, mine, low_x, high_x, low_y, high_y, out):
    step = pl.program_id(0)

    @pl.when(step < cut)
    def _():
        total = mine[...].astype(F32) + low_x[...].astype(F32) + low_y[...].astype(F32)
        out[...] = total.astype(BF16)

    @pl.when(step >= cut)
    def _():
        total = mine[...].astype(F32) + high_x[...].astype(F32) + high_y[...].astype(F32)
        out[...] = total.astype(BF16)


def add_sides(cut, pos, mine, sides):
    nz = mine.shape[0]
    block = (1,) + mine.shape[1:]
    specs, _ = piece_specs(block, nz, cut)
    zeros = (0,) * (len(block) - 1)
    return pl.pallas_call(
        functools.partial(sum_cut_kernel, cut),
        grid_spec=pltpu.PrefetchScalarGridSpec(
            num_scalar_prefetch=1,
            grid=(nz,),
            in_specs=specs[:5],
            out_specs=pl.BlockSpec(block, lambda i, pos: (ring_place(pos, i, nz),) + zeros),
        ),
        out_shape=jax.ShapeDtypeStruct(mine.shape, BF16),
        compiler_params=params(),
        cost_estimate=cost(mine.size * 2, 8 * mine.size),
        name="add_sides",
    )(pos, mine, *sides)


def after(values, *others):
    return lax.optimization_barrier((values, others))[0]


def swap(values, axis):
    return lax.ppermute(values, axis, SWAP)


def ring(values, step, size):
    return lax.ppermute(values, "z", [(i, (i + step) % size) for i in range(size)])


def gather_sides(mine):
    return swap(mine, "x"), swap(mine, "y")


def gather_corner(over_x, over_y, cut):
    return jnp.concatenate([swap(over_x[:cut], "y"), swap(over_y[cut:], "x")])


def pair_up(mine, over_x, over_y, corner):
    return [[mine, over_x], [over_y, corner]]


def send_corner(parts):
    return swap(parts[5], "y"), swap(parts[6], "x")


def corner_sums(parts, corner):
    return add(parts[1], corner[0]), add(parts[4], corner[1])


def send_sides(parts, sums):
    high_x, low_y = after((parts[2], parts[3]), sums)
    return swap(sums[0], "x"), swap(high_x, "x"), swap(low_y, "y"), swap(sums[1], "y")


def plane_norms(sums, part):
    pieces = [sums[:, q * part : (q + 1) * part] for q in range(4)]
    low, high = (pieces[dy] + swap(pieces[2 + dy], "c") for dy in range(2))
    mine = low + swap(high, "y")
    return mine + swap(mine, "x")


def line_norms(mine):
    mine = mine + lax.ppermute(mine, "z", [(i, i ^ 1) for i in range(4)])
    return mine + lax.ppermute(mine, "z", [(i, i ^ 2) for i in range(4)])


def fast_shards(inputs, doc_starts, w_qkv, w_out, w_up, w_down, norm_gains, norm_biases, cotangent):
    pos = jnp.stack([lax.axis_index(name) for name in ("y", "c", "z", "x")]).astype(jnp.int32)
    nz = lax.axis_size("z")
    parts = nz * 2
    micro, _, shard_len, width = inputs.shape
    tokens = micro * shard_len
    seq_len = shard_len * parts
    part = width // 4
    cols = w_qkv.shape[2]
    half = nz // 2
    starts = doc_starts.reshape(-1)
    x = inputs.reshape(tokens, width)
    cot = cotangent.reshape(tokens, width)

    def exchange(values):
        return lax.all_to_all(values, SEQ, 0, 0, tiled=True)

    rings = [ring(w_qkv, nz - k, nz) for k in range(1, nz)]
    norms = jnp.concatenate([norm_gains, norm_biases])
    norms_y, norms_c = swap(norms, "y"), swap(norms, "c")
    norms = jnp.concatenate([norms, norms_y, norms_c, swap(norms_y, "c")], 1).astype(F32)
    gains, shifts = norms[:4], norms[4:]
    start_table = start_tables(doc_starts[:, 0])
    table = tables(seq_len)
    mix = jnp.concatenate([w_down, w_out])
    qkv_mine, mix = after((jnp.stack([w_qkv] + rings), mix), norms, start_table)
    mix1, mix3 = (ring(after(mix, qkv_mine), k, nz) for k in (nz - 1, 1))
    qkv_sides = after(gather_sides(qkv_mine), mix1, mix3)
    mix2 = ring(after(mix, qkv_sides), nz - 2, nz)
    qkv_corner = gather_corner(*qkv_sides, half)
    qkv_other = [swap(p, "c") for p in (qkv_mine, *qkv_sides)]
    qkv_corner = after(qkv_corner, qkv_other)
    if O["up_z"] == 0:
        up_mine = lax.all_gather(after(w_up, qkv_corner), "z", axis=0, tiled=False)
    else:
        up_mine = lax.all_gather(after(w_up, qkv_sides), "z", axis=0, tiled=False)
    mix_mine = jnp.stack([mix, mix1, mix2, mix3])
    if O["gate_mix"]:
        qkv_other.append(after(swap(qkv_corner, "c"), mix_mine))
    else:
        qkv_other.append(swap(qkv_corner, "c"))
    qkv = pair_up(qkv_mine, *qkv_sides, qkv_corner) + pair_up(*qkv_other)
    first, last, keep0, send1 = call_proj(
        pos, starts, x, gains, shifts, table, start_table, qkv, shard_len
    )
    if O["gate_mix"] == 0:
        mix_mine = after(mix_mine, first)
    mix_sides = gather_sides(mix_mine)
    got = [None, None]
    got[0] = exchange(first.reshape(parts, 2, 3, shard_len, cols))
    got[1] = exchange(after(last.reshape(parts, 1, 3, shard_len, cols), got[0]))
    mix_corner = gather_corner(*mix_sides, O["fcut"])
    mix_other = [swap(p, "c") for p in (mix_mine, *mix_sides)]
    att_local, lses, att = [None, None], [None, None], [None, None]
    if O["gate_up"] == 0:
        got[0] = after(got[0], mix_other, mix_corner)
        up_own = lax.all_gather(after(up_mine, got[0]), ("y", "x"), axis=0, tiled=False)
    elif O["gate_up"] == 1:
        got[0] = after(got[0], mix_other, mix_corner, up_mine)
        up_own = lax.all_gather(after(up_mine, mix_corner), ("y", "x"), axis=0, tiled=False)
    elif O["gate_up"] == 2:
        got[0] = after(got[0], mix_other, up_mine)
        up_own = lax.all_gather(after(up_mine, mix_sides), ("y", "x"), axis=0, tiled=False)
    elif O["gate_up"] == 3:
        got[0] = after(got[0], mix_sides, up_mine)
        up_own = lax.all_gather(after(up_mine, first), ("y", "x"), axis=0, tiled=False)
    mix_other.append(swap(mix_corner, "c"))
    att_local[0], lses[0] = call_attend(0, starts, got[0])
    got[1] = after(got[1], att_local[0], mix_corner)
    att[0] = exchange(att_local[0])
    att_local[1], lses[1] = call_attend(2, starts, got[1])
    att[0] = after(att[0], att_local[1], mix_other)
    att[1] = exchange(after(att_local[1], att[0]))
    mixes = pair_up(mix_mine, *mix_sides, mix_corner) + pair_up(*mix_other)
    up_own = after(up_own, att[0])
    ups = [up_own, swap(up_own, "c")]

    res = call_layer(pos, att, x, cot, gains, shifts, ups, mixes)
    outputs, att_all, act, slope, keep, send = res[:6]
    kept, sums3 = res[6:10], res[10]
    recv, act2, att_all2, recv0 = (swap(v, "c") for v in (send, act, att_all, send1))
    res = call_layer_back(pos, cot, gains, kept, slope, keep, send, ups, mixes, shard_len)
    g_up, keep1, send1, g_hidden, g_att, sums = res
    act2 = after(act2, g_up)
    grad = exchange(g_att)
    recv1, g_up2 = swap(send1, "c"), swap(g_up, "c")
    cut = O["bcut"]
    down_parts = call_down_grad(cut, act, act2, keep, recv)
    down_corner = send_corner(down_parts)
    g_up = after(g_up, down_parts)
    up_parts = call_up_grad(pos, g_up, g_up2, keep, recv, keep1, recv1, att_all, att_all2)
    up_sum = lax.psum_scatter(up_parts, ("y", "x"), scatter_dimension=0, tiled=True)
    up_sum = up_sum.reshape(up_parts.shape[1:])

    back, back2 = [None, None], [None, None]
    if O["gate_grad"] == 1:
        grad = after(grad, up_parts)
    elif O["gate_grad"] == 2:
        grad = after(grad, down_parts)
    res = call_attend_back(2, starts, table, start_table, got[1], grad, att_local[1], lses[1])
    if O["gate_grad"] == 3:
        res = after(res, up_parts)
    back[1] = exchange(res)
    grad = after(grad, res)
    if O["gate_grad"] == 4:
        grad = after(grad, up_parts)
    res = call_attend_back(0, starts, table, start_table, got[0], grad, att_local[0], lses[0])
    if O["gate_ab"]:
        down_corner = after(down_corner, res)
    down_sums = corner_sums(down_parts, down_corner)
    down_sides = send_sides(down_parts, down_sums)
    if O["gate_b1"]:
        back[1] = after(back[1], down_sums)
    back[0] = exchange(after(res, back[1]))
    up_sum = lax.psum_scatter(up_sum, "z", scatter_dimension=0, tiled=False)
    down_mine = down_parts[0]
    if O["gate_add"]:
        down_mine = after(down_mine, up_sum)
    down_sum = add_sides(cut, pos, down_mine, down_sides)
    back2[1] = swap(back[1].reshape((nz, 2) + back[1].shape[1:]), "c")
    back[0] = after(back[0], down_sum, back2[1])
    down_sum = lax.psum_scatter(down_sum, "z", scatter_dimension=0, tiled=False)

    back = [b.reshape((nz, 2) + b.shape[1:]) for b in back]
    back2[0] = swap(back[0], "c")
    qkv_parts = call_qkv_grad(half, pos, back, back2, keep0, recv0)
    back = after(back, qkv_parts)
    qkv_corner = send_corner(qkv_parts)
    if O["gate_us"]:
        qkv_corner = after(qkv_corner, down_sum)
    qkv_sums = corner_sums(qkv_parts, qkv_corner)
    qkv_sides = send_sides(qkv_parts, qkv_sums)
    inputs_grad, sums0 = call_input_grad(pos, after(back, qkv_sums), x, gains, g_hidden, qkv)
    norm_sums = [sums0[:1], sums[:2], sums3[:1], sums0[1:2], sums[2:4], sums3[1:2]]
    norm_sums = jnp.concatenate(norm_sums)
    if O["gate_us"]:
        qkv_sides, norm_sums = after((qkv_sides, norm_sums), norm_sums, up_sum)
    qkv_sum = add_sides(half, pos, qkv_parts[0], qkv_sides)
    norm_sums = line_norms(plane_norms(after(norm_sums, qkv_sum), part))
    qkv_sum = lax.psum_scatter(qkv_sum, "z", scatter_dimension=0, tiled=False)
    down_sum = down_sum.astype(F32)
    up_sum, out_sum = up_sum[:part].astype(F32), up_sum[part:].astype(F32)
    out_sum = jnp.concatenate([out_sum[:, :part], out_sum[:, part:]], 0)
    qkv_sum = after(qkv_sum, norm_sums, down_sum, out_sum, up_sum)
    return (
        outputs.reshape(inputs.shape),
        inputs_grad.reshape(inputs.shape),
        qkv_sum.astype(F32),
        out_sum,
        up_sum,
        down_sum,
        norm_sums[:4],
        norm_sums[4:],
    )


def fits_fast(mesh, inputs, w_qkv, w_up):
    dp, tensor = mesh.shape["dp"], mesh.shape["tensor"]
    return (
        dp == 4
        and tensor == 8
        and inputs.shape[0] == 3
        and inputs.shape[1] == dp
        and inputs.shape[2] == 1024
        and w_qkv.shape[1:] == (1024, 1024)
        and w_up.shape[1] == 4096
    )


def solution(mesh):
    dp, tensor = mesh.shape["dp"], mesh.shape["tensor"]
    names = ("y", "c", "z", "x")
    fine = Mesh(mesh.devices.reshape(dp // 2, 2, 4, tensor // 4), names)
    rows, seq = ("y", "c"), ("z", "x")
    tokens = P(None, rows, seq, None)
    weights = (P(None, rows, seq), P(seq, rows), P(rows, seq), P(seq, rows))
    norm = P(None, rows)

    def run(*arrays):
        fast = fits_fast(mesh, arrays[0], arrays[2], arrays[4])
        return jax.shard_map(
            fast_shards if fast else shards,
            mesh=fine,
            in_specs=(tokens, P(None, rows, None)) + weights + (norm, norm, tokens),
            out_specs=(tokens, tokens) + weights + (norm, norm),
            check_vma=False,
        )(*arrays)

    return run
```

```python
import functools
import math
import jax
import jax.numpy as jnp
import numpy as np
from jax import lax
from jax.experimental import pallas as pl
from jax.experimental.pallas import tpu as pltpu
from jax.sharding import Mesh, PartitionSpec as P
HD = 64
EPSILON = 1e-05
F32 = jnp.float32
BF16 = jnp.bfloat16
CHIPS = ('y', 'z', 'x')
SEQ = ('z', 'x')
SWAP = [(0, 1), (1, 0)]

def ln_forward(values, gain, shift):
    average = jnp.mean(values, axis=-1, keepdims=True)
    centred = values - average
    variance = jnp.mean(centred * centred, axis=-1, keepdims=True)
    scale = lax.rsqrt(variance + EPSILON)
    xhat = centred * scale
    return (xhat * gain + shift, xhat, scale)

def ln_backward(grad, xhat, scale, gain):
    e = grad * gain
    dv = scale * (e - jnp.mean(e, axis=-1, keepdims=True) - xhat * jnp.mean(e * xhat, axis=-1, keepdims=True))
    return (dv, jnp.sum(grad * xhat, axis=0), jnp.sum(grad, axis=0))

def rotate(values, cosines, sines):
    half_dim = values.shape[-1] // 2
    lower = values[..., :half_dim]
    upper = values[..., half_dim:]
    return jnp.concatenate([lower * cosines - upper * sines, upper * cosines + lower * sines], axis=-1)

def doc_layout(starts, token_index):
    inside = token_index[:, None] >= starts[None, :]
    segment = jnp.sum(inside.astype(jnp.int32), axis=1)
    begins = jnp.max(jnp.where(inside, starts[None, :], 0), axis=1)
    return (segment, token_index - begins)

def angles_of(position):
    frequency = jnp.exp(jnp.arange(HD // 2, dtype=F32) * (-2.0 * math.log(10000.0) / HD))
    angles = position.astype(F32)[..., None] * frequency
    return (jnp.cos(angles), jnp.sin(angles))

def block_mask(segment, offset, block_len, key_len):
    query_pos = jnp.arange(offset, offset + block_len, dtype=jnp.int32)
    key_pos = jnp.arange(key_len, dtype=jnp.int32)
    causal = key_pos[None, :] <= query_pos[:, None]
    return causal & (segment[offset:offset + block_len, None] == segment[None, :key_len])

def attention_forward(q, k, v, segment):
    seq_len = q.shape[1]
    block_len = min(512, seq_len)
    pieces, lses = ([], [])
    for offset in range(0, seq_len, block_len):
        end = offset + block_len
        allowed = block_mask(segment, offset, block_len, end)[None]
        scores = 0.125 * jnp.einsum('hqe,hke->hqk', q[:, offset:end], k[:, :end], preferred_element_type=F32)
        scores = jnp.where(allowed, scores, -1e+30)
        peak = jnp.max(scores, axis=-1, keepdims=True)
        lse = peak + jnp.log(jnp.sum(jnp.exp(scores - peak), axis=-1, keepdims=True))
        probs = jnp.exp(scores - lse).astype(BF16)
        pieces.append(jnp.einsum('hqk,hke->hqe', probs, v[:, :end], preferred_element_type=F32).astype(BF16))
        lses.append(lse)
    return (jnp.concatenate(pieces, axis=1), lses)

def attention_backward(q, k, v, do, lses, segment):
    seq_len = q.shape[1]
    block_len = min(512, seq_len)
    dq = []
    dk = jnp.zeros(k.shape, F32)
    dv = jnp.zeros(v.shape, F32)
    for index, offset in enumerate(range(0, seq_len, block_len)):
        end = offset + block_len
        allowed = block_mask(segment, offset, block_len, end)[None]
        qb, kb, vb, dob = (q[:, offset:end], k[:, :end], v[:, :end], do[:, offset:end])
        scores = 0.125 * jnp.einsum('hqe,hke->hqk', qb, kb, preferred_element_type=F32)
        scores = jnp.where(allowed, scores, -1e+30)
        soft = jnp.exp(scores - lses[index])
        probs = soft.astype(BF16)
        dp = jnp.einsum('hqe,hke->hqk', dob, vb, preferred_element_type=F32)
        dot = jnp.sum(soft * dp, axis=-1, keepdims=True)
        ds = (soft * (dp - dot)).astype(BF16)
        dq.append(0.125 * jnp.einsum('hqk,hke->hqe', ds, kb, preferred_element_type=F32))
        pad = ((0, 0), (0, seq_len - end), (0, 0))
        dk = dk + jnp.pad(0.125 * jnp.einsum('hqk,hqe->hke', ds, qb, preferred_element_type=F32), pad)
        dv = dv + jnp.pad(jnp.einsum('hqk,hqe->hke', probs, dob, preferred_element_type=F32), pad)
    return (jnp.concatenate(dq, axis=1), dk, dv)

def gather_both(shard):
    mine = lax.all_gather(shard, CHIPS, axis=0, tiled=False)
    return jnp.stack([mine, lax.ppermute(mine, 'c', SWAP)])

def scatter_both(partial, sizes):
    ny, nz, nx = sizes
    shard_shape = partial.shape[2:]
    low = partial.astype(BF16)
    got = lax.ppermute(low[1], 'c', SWAP)
    mine = (low[0].astype(F32) + got.astype(F32)).astype(BF16)
    mine = mine.reshape((ny, nz, nx) + shard_shape)
    mine = mine.transpose((0, 2, 1) + tuple(range(3, mine.ndim)))
    mine = mine.reshape((ny * nx, nz) + shard_shape)
    mine = lax.psum_scatter(mine, ('y', 'x'), scatter_dimension=0, tiled=False)
    return lax.psum_scatter(mine, 'z', scatter_dimension=0, tiled=False).astype(F32)

def shards(inputs, doc_starts, w_qkv, w_out, w_up, w_down, norm_gains, norm_biases, cotangent):
    ny, nz, nx = (lax.axis_size(name) for name in CHIPS)
    core = lax.axis_index('c')
    sizes = (ny, nz, nx)
    parts = nz * nx
    micro, _, shard_len, width = inputs.shape
    tokens = micro * shard_len
    seq_len = shard_len * parts
    dpart = width // (2 * ny)
    hcols = w_out.shape[0]
    heads = hcols // HD
    units = w_up.shape[1]

    def to_own(values):
        pieces = values.reshape(values.shape[:-1] + (ny, 2, dpart))
        pieces = jnp.where(core == 0, pieces, pieces[..., ::-1, :])
        return jnp.swapaxes(pieces, -3, -2).reshape(values.shape)

    def from_own(values):
        pieces = jnp.swapaxes(values.reshape(values.shape[:-1] + (2, ny, dpart)), -3, -2)
        return jnp.where(core == 0, pieces, pieces[..., ::-1, :]).reshape(values.shape)
    qkv_all = gather_both(w_qkv).reshape(2, ny, parts, 3, dpart, hcols)
    norms = jnp.stack([norm_gains, norm_biases])
    norms = gather_dp(norms, ny, dpart)
    norms = to_own(norms.astype(F32))
    gains, shifts = (norms[0], norms[1])
    out_all = gather_both(w_out).reshape(2, ny, parts, hcols, dpart)
    up_all = gather_both(w_up).reshape(2, ny, parts, dpart, units)
    down_all = gather_both(w_down).reshape(2, ny, parts, units, dpart)
    qkv_full = qkv_all.transpose(0, 1, 4, 3, 2, 5).reshape(width, 3 * parts * hcols)
    out_full = out_all.transpose(2, 3, 0, 1, 4).reshape(parts * hcols, width)
    up_full = up_all.transpose(0, 1, 3, 2, 4).reshape(width, parts * units)
    down_full = down_all.transpose(2, 3, 0, 1, 4).reshape(parts * units, width)
    x = to_own(inputs.reshape(tokens, width)).astype(F32)
    cot = to_own(cotangent.reshape(tokens, width)).astype(F32)
    place = lax.axis_index(SEQ) * shard_len + jnp.arange(shard_len, dtype=jnp.int32)
    cos_own, sin_own, cos_row, sin_row, segments = ([], [], [], [], [])
    for index in range(micro):
        starts = doc_starts[index, 0]
        c, s = angles_of(doc_layout(starts, place)[1])
        cos_own.append(c)
        sin_own.append(s)
        segment, position = doc_layout(starts, jnp.arange(seq_len, dtype=jnp.int32))
        c, s = angles_of(position)
        cos_row.append(c)
        sin_row.append(s)
        segments.append(segment)
    cos_own = jnp.concatenate(cos_own)[:, None, None]
    sin_own = jnp.concatenate(sin_own)[:, None, None]
    normed1, xhat0, scale0 = ln_forward(x, gains[0], shifts[0])
    normed1 = normed1.astype(BF16)
    projected = jnp.dot(normed1, qkv_full, preferred_element_type=F32)
    projected = projected.reshape(tokens, 3, parts * heads, HD)
    rotated = rotate(projected[:, :2], cos_own, sin_own)
    projected = jnp.concatenate([rotated, projected[:, 2:]], axis=1).astype(BF16)
    projected = projected.reshape(micro, shard_len, 3, parts, hcols).transpose(0, 3, 2, 1, 4)

    def to_heads(values):
        kinds = values.shape[1]
        got = lax.all_to_all(values, SEQ, 0, 0, tiled=True)
        got = got.reshape(parts, kinds, shard_len, heads, HD).transpose(1, 3, 0, 2, 4)
        return got.reshape(kinds, heads, seq_len, HD)

    def to_tokens(values):
        kinds = values.shape[0]
        sent = values.reshape(kinds, heads, parts, shard_len, HD).transpose(2, 0, 3, 1, 4)
        sent = sent.reshape(parts, kinds, shard_len, hcols)
        return lax.all_to_all(sent, SEQ, 0, 0, tiled=True)
    qkvs, lses, attended = ([], [], [])
    for index in range(micro):
        q, k, v = to_heads(projected[index])
        out, lse = attention_forward(q, k, v, segments[index])
        qkvs.append((q, k, v))
        lses.append(lse)
        attended.append(to_tokens(out[None])[:, 0])
    attended = jnp.stack(attended).transpose(0, 2, 1, 3).reshape(tokens, parts * hcols)
    branch1 = jnp.dot(attended, out_full, preferred_element_type=F32)
    post1, xhat1, scale1 = ln_forward(branch1, gains[1], shifts[1])
    hidden = x + post1
    normed2, xhat2, scale2 = ln_forward(hidden, gains[2], shifts[2])
    normed2 = normed2.astype(BF16)
    up_act = jnp.dot(normed2, up_full, preferred_element_type=F32)
    gated, gate_pull = jax.vjp(lambda u: jax.nn.gelu(u, approximate=True), up_act)
    activated = gated.astype(BF16)
    branch2 = jnp.dot(activated, down_full, preferred_element_type=F32)
    post2, xhat3, scale3 = ln_forward(branch2, gains[3], shifts[3])
    outputs = (hidden + post2).astype(BF16)
    grad_branch2, gain3, shift3 = ln_backward(cot, xhat3, scale3, gains[3])
    grad_branch2 = grad_branch2.astype(BF16)
    down_part = jnp.einsum('tf,td->fd', activated, grad_branch2, preferred_element_type=F32)
    down_part = down_part.astype(BF16).reshape(parts, units, 2, ny, dpart)
    down_grad = scatter_both(down_part.transpose(2, 3, 0, 1, 4).reshape(2, ny * parts, units, dpart), sizes)
    grad_act = jnp.einsum('td,fd->tf', grad_branch2, down_full, preferred_element_type=F32)
    grad_up = gate_pull(grad_act)[0].astype(BF16)
    up_part = jnp.einsum('td,tf->df', normed2, grad_up, preferred_element_type=F32)
    up_part = up_part.astype(BF16).reshape(2, ny, dpart, parts, units)
    up_grad = scatter_both(up_part.transpose(0, 1, 3, 2, 4).reshape(2, ny * parts, dpart, units), sizes)
    grad_normed2 = jnp.einsum('tf,df->td', grad_up, up_full, preferred_element_type=F32)
    extra, gain2, shift2 = ln_backward(grad_normed2, xhat2, scale2, gains[2])
    grad_hidden = cot + extra
    grad_branch1, gain1, shift1 = ln_backward(grad_hidden, xhat1, scale1, gains[1])
    grad_branch1 = grad_branch1.astype(BF16)
    grad_attended = jnp.einsum('td,fd->tf', grad_branch1, out_full, preferred_element_type=F32).astype(BF16)
    grad_attended = grad_attended.reshape(micro, shard_len, parts, 1, hcols)
    grad_attended = grad_attended.transpose(0, 2, 3, 1, 4)
    out_part = jnp.einsum('tf,td->fd', attended, grad_branch1, preferred_element_type=F32)
    out_part = out_part.astype(BF16).reshape(parts, hcols, 2, ny, dpart)
    out_grad = scatter_both(out_part.transpose(2, 3, 0, 1, 4).reshape(2, ny * parts, hcols, dpart), sizes)
    grad_projected = []
    for index in range(micro):
        do = to_heads(grad_attended[index])[0]
        q, k, v = qkvs[index]
        dq, dk, dv = attention_backward(q, k, v, do, lses[index], segments[index])
        cos, sin = (cos_row[index], -sin_row[index])
        back = jnp.stack([rotate(dq, cos, sin), rotate(dk, cos, sin), dv]).astype(BF16)
        grad_projected.append(to_tokens(back))
    grad_projected = jnp.stack(grad_projected).transpose(0, 3, 2, 1, 4)
    grad_projected = grad_projected.reshape(tokens, 3 * parts * hcols)
    qkv_part = jnp.einsum('td,te->de', normed1, grad_projected, preferred_element_type=F32)
    qkv_part = qkv_part.astype(BF16).reshape(2, ny, dpart, 3, parts, hcols)
    qkv_grad = scatter_both(qkv_part.transpose(0, 1, 4, 3, 2, 5).reshape(2, ny * parts, 3, dpart, hcols), sizes)
    grad_normed1 = jnp.einsum('te,de->td', grad_projected, qkv_full, preferred_element_type=F32)
    extra, gain0, shift0 = ln_backward(grad_normed1, xhat0, scale0, gains[0])
    inputs_grad = grad_hidden + extra
    sums = jnp.stack([gain0, gain1, gain2, gain3, shift0, shift1, shift2, shift3])
    sums = lax.psum(from_own(sums), ('y', 'c', 'z', 'x'))
    place = (lax.axis_index('y') * 2 + core) * dpart
    sums = lax.dynamic_slice_in_dim(sums, place, dpart, 1)
    return (from_own(outputs).reshape(inputs.shape), from_own(inputs_grad).reshape(inputs.shape), qkv_grad, out_grad, up_grad, down_grad, sums[:4], sums[4:])

def gather_dp(norms, ny, dpart):
    full = lax.all_gather(norms, ('y', 'c'), axis=2, tiled=True)
    return full
NT = (((1,), (1,)), ((), ()))
GELU_A = 0.7978845608
GELU_B = 0.044715
COST = 0.2

def dot(a, b):
    return jnp.dot(a, b, preferred_element_type=F32)

def dot_nt(a, b):
    return lax.dot_general(a, b, NT, preferred_element_type=F32)

def params(semantics=1):
    return pltpu.CompilerParams(dimension_semantics=('arbitrary',) * semantics, vmem_limit_bytes=60 * 1024 * 1024)

def cost(flops, size, transcendentals=0):
    return pl.CostEstimate(flops=int(flops * COST), bytes_accessed=int(size * COST), transcendentals=int(transcendentals * COST))

def whole(shape):
    return pl.BlockSpec(shape, lambda *_: (0,) * len(shape))

def swap_halves(values):
    lane = lax.broadcasted_iota(jnp.int32, values.shape, 1)
    low = lax.rem(lane, HD) < HD // 2
    return jnp.where(low, pltpu.roll(values, 96, 1), pltpu.roll(values, 32, 1))

def row_stats(values):
    average = jnp.mean(values, axis=-1, keepdims=True)
    centred = values - average
    variance = jnp.mean(centred * centred, axis=-1, keepdims=True)
    scale = lax.rsqrt(variance + EPSILON)
    return (centred * scale, scale)

def row_pull(grad, xhat, scale, gain):
    e = grad * gain
    return scale * (e - jnp.mean(e, axis=-1, keepdims=True) - xhat * jnp.mean(e * xhat, axis=-1, keepdims=True))

def column_sum(values):
    return jnp.sum(values, axis=0, keepdims=True)

def own_place(pos, q, part):
    place = lax.bitwise_xor(pos[0], q % 2) * 2 + lax.bitwise_xor(pos[1], q // 2)
    return pl.multiple_of(place * part, part)

def load_columns(ref, pos, part):
    return jnp.concatenate([ref[:, pl.ds(own_place(pos, q, part), part)] for q in range(4)], 1)

def store_columns(ref, values, pos, part):
    for q in range(4):
        ref[:, pl.ds(own_place(pos, q, part), part)] = values[:, q * part:(q + 1) * part].astype(ref.dtype)

def tables(seq_len):
    lane = np.arange(128)
    frequency = np.exp(lane % (HD // 2) * (-2.0 * math.log(10000.0) / HD))
    angle = np.arange(seq_len)[:, None] * frequency.astype(np.float32).astype(np.float64)
    sign = np.where(lane % HD < HD // 2, -1.0, 1.0)
    return (np.cos(angle).astype(np.float32), (np.sin(angle) * sign).astype(np.float32))

def start_tables(starts):
    lane = jnp.arange(128)
    frequency = jnp.exp((lane % (HD // 2)).astype(F32) * (-2.0 * math.log(10000.0) / HD))
    angle = starts.astype(F32)[..., None] * frequency
    return (jnp.cos(angle), jnp.sin(angle) * jnp.where(lane % HD < HD // 2, -1.0, 1.0))

def angle_rows(rows, starts, base, table, start_cos, start_sin):
    cb, sb = (start_cos[0:1], start_sin[0:1])
    for d in range(1, 4):
        inside = rows >= starts[base + d]
        cb = jnp.where(inside, start_cos[d:d + 1], cb)
        sb = jnp.where(inside, start_sin[d:d + 1], sb)
    tc, ts = table
    return (tc * cb + ts * sb, ts * cb - tc * sb)

def begin_of(rows, starts, base):
    begin = jnp.zeros(rows.shape, jnp.int32)
    for d in range(1, 4):
        begin = jnp.where(rows >= starts[base + d], starts[base + d], begin)
    return begin

def proj_kernel(pos, starts, x, gains, shifts, tcos, tsin, start_cos, start_sin, *refs):
    weights = [refs[2 * q:2 * q + 2] for q in range(4)]
    first, last, keep, send = refs[8:12]
    normed, cos, sin = refs[12:15]
    outs = [first.at[0, :, 0], first.at[0, :, 1], last.at[0, :, 0]]
    part = weights[0][0].shape[2]
    count = first.shape[4]

    @pl.when(pl.program_id(0) == 0)
    def _():
        xhat, _ = row_stats(load_columns(x, pos, part).astype(F32))
        value = (xhat * gains[0:1] + shifts[0:1]).astype(BF16)
        normed[...] = value
        keep[...] = value[:, :2 * part]
        send[...] = value[:, 2 * part:]
        rows = lax.broadcasted_iota(jnp.int32, (count, 128), 0) + (pos[2] * 2 + pos[3]) * count
        for m in range(3):
            at = slice(m * count, (m + 1) * count)
            cos[at], sin[at] = angle_rows(rows, starts, 4 * m, (tcos[...], tsin[...]), start_cos.at[m], start_sin.at[m])
    total = None
    for q in range(4):
        block = jnp.concatenate([weights[q][dx][0, kind] for dx in range(2) for kind in range(3)], 1)
        term = dot(normed[:, q * part:(q + 1) * part], block)
        total = term if total is None else total + term
    for dx in range(2):
        place = lax.bitwise_xor(pos[3], dx)
        for kind in range(3):
            at = (dx * 3 + kind) * 128
            u = total[:, at:at + 128]
            if kind < 2:
                u = u * cos[...] + swap_halves(u) * sin[...]
            u = u.astype(BF16)
            for m in range(3):
                outs[m][place, kind] = u[m * count:(m + 1) * count]

def ring_place(pos, i, nz):
    return lax.rem(pos[2] + i, nz)

def head_index(nz):
    return lambda i, pos, *_: (ring_place(pos, i, nz), 0, 0, 0, 0, 0)

def call_proj(pos, starts, x, gains, shifts, table, start_table, pieces, shard_len):
    tokens, width = x.shape
    nz, _, part, cols = pieces[0][0].shape
    piece = pl.BlockSpec((1, 3, part, cols), lambda i, *_: (i, 0, 0, 0))
    outs = [pl.BlockSpec((1, 2, n, 3, shard_len, cols), head_index(nz)) for n in (2, 1)]
    shapes = [jax.ShapeDtypeStruct((nz, 2, n, 3, shard_len, cols), BF16) for n in (2, 1)]
    half = (tokens, width // 2)
    rows = pl.BlockSpec((shard_len, 128), lambda i, pos, _: (pos[2] * 2 + pos[3], 0))
    return pl.pallas_call(proj_kernel, grid_spec=pltpu.PrefetchScalarGridSpec(num_scalar_prefetch=2, grid=(nz,), in_specs=[whole(a.shape) for a in (x, gains, shifts)] + [rows] * 2 + [whole(a.shape) for a in start_table] + [piece] * 8, out_specs=outs + [whole(half)] * 2, scratch_shapes=[pltpu.VMEM((tokens, width), BF16), pltpu.VMEM((tokens, 128), F32), pltpu.VMEM((tokens, 128), F32)]), out_shape=shapes + [jax.ShapeDtypeStruct(half, BF16)] * 2, compiler_params=params(), cost_estimate=cost(2 * tokens * width * 3 * nz * 2 * cols, 12000000.0), name='project')(pos, starts, x, gains, shifts, *table, *start_table, *[p for pair in pieces for p in pair])

def head_mask(shape, head):
    lane = lax.broadcasted_iota(jnp.int32, shape, 1)
    return lane < HD if head == 0 else lane >= HD

def attend_kernel(first, starts, got, out, lse_out):
    micro = first + pl.program_id(0)
    shards_n, _, count, lanes = got.shape
    seq_len = shards_n * count
    block = min(256, seq_len)
    q_all = (got[:, 0] * 0.125).reshape(seq_len, lanes)
    k_all = got[:, 1].reshape(seq_len, lanes)
    v_all = got[:, 2].reshape(seq_len, lanes)
    per = block // count
    for start in range(0, seq_len, block):
        end = start + block
        qb = q_all[start:end]
        key = lax.broadcasted_iota(jnp.int32, (block, end), 1)
        query = start + lax.broadcasted_iota(jnp.int32, (block, end), 0)
        begin = begin_of(start + lax.broadcasted_iota(jnp.int32, (block, 1), 0), starts, 4 * micro)
        allowed = (key <= query) & (key >= begin)
        results = []
        for head in range(2):
            mask = head_mask(qb.shape, head)
            scores = dot_nt(jnp.where(mask, qb, 0), k_all[:end])
            scores = jnp.where(allowed, scores, -1e+30)
            peak = jnp.max(scores, axis=-1, keepdims=True)
            e = jnp.exp(scores - peak)
            total = jnp.sum(e, axis=-1, keepdims=True)
            results.append(dot(e.astype(BF16), v_all[:end]) / total)
            lse = jnp.broadcast_to(peak + jnp.log(total), (block, 128))
            lse_out[head:head + 1, start:end] = jnp.transpose(lse)[0:1]
        mixed = jnp.where(head_mask(results[0].shape, 0), results[0], results[1]).astype(BF16)
        out[start // count:end // count] = mixed.reshape(per, count, lanes)

def call_attend(first, starts, got):
    parts, number, _, count, lanes = got.shape
    seq_len = parts * count
    return pl.pallas_call(functools.partial(attend_kernel, first), grid_spec=pltpu.PrefetchScalarGridSpec(num_scalar_prefetch=1, grid=(number,), in_specs=[pl.BlockSpec((parts, None, 3, count, lanes), lambda i, _: (0, i, 0, 0, 0))], out_specs=[pl.BlockSpec((parts, None, count, lanes), lambda i, _: (0, i, 0, 0)), pl.BlockSpec((None, 8, seq_len), lambda i, _: (i, 0, 0))]), out_shape=[jax.ShapeDtypeStruct((parts, number, count, lanes), BF16), jax.ShapeDtypeStruct((number, 8, seq_len), F32)], compiler_params=params(), cost_estimate=cost(number * 8 * seq_len * seq_len * lanes, number * 2000000.0, number * 2 * seq_len * seq_len), name='attend')(starts, got)

def attend_back_kernel(first, starts, tcos, tsin, start_cos, start_sin, got, grad, att, lse, out, dq_ref, dk_ref, dv_ref):
    micro = first + pl.program_id(0)
    shards_n, _, count, lanes = got.shape
    seq_len = shards_n * count
    block = min(256, seq_len)
    q_all = (got[:, 0] * 0.125).reshape(seq_len, lanes)
    k_all = got[:, 1].reshape(seq_len, lanes)
    v_all = got[:, 2].reshape(seq_len, lanes)
    do_all = grad[...].reshape(seq_len, lanes)
    prod = do_all.astype(F32) * att[...].reshape(seq_len, lanes).astype(F32)
    prod = jnp.transpose(prod)
    deltas = [jnp.sum(prod[:HD], axis=0, keepdims=True), jnp.sum(prod[HD:], axis=0, keepdims=True)]
    begins = begin_of(lax.broadcasted_iota(jnp.int32, (1, seq_len), 1), starts, 4 * micro)
    for start in range(0, seq_len, block):
        end = start + block
        kb, vb = (k_all[start:end], v_all[start:end])
        qs, dos = (q_all[start:], do_all[start:])
        span = seq_len - start
        key = start + lax.broadcasted_iota(jnp.int32, (block, span), 0)
        query = start + lax.broadcasted_iota(jnp.int32, (block, span), 1)
        allowed = (key <= query) & (key >= begins[:, start:])
        dks, dvs, dqs = ([], [], [])
        for head in range(2):
            mask = head_mask(kb.shape, head)
            scores = dot_nt(jnp.where(mask, kb, 0), qs)
            soft = jnp.exp(jnp.where(allowed, scores, -1e+30) - lse[head:head + 1, start:])
            pull = dot_nt(jnp.where(mask, vb, 0), dos)
            ds = (soft * (pull - deltas[head][:, start:])).astype(BF16)
            dvs.append(dot(soft.astype(BF16), dos))
            dks.append(dot(ds, qs))
            dqs.append(lax.dot_general(ds, kb, (((0,), (0,)), ((), ())), preferred_element_type=F32))
        low = head_mask(kb.shape, 0)
        dk_ref[start:end] = jnp.where(low, dks[0], dks[1])
        dv_ref[start:end] = jnp.where(low, dvs[0], dvs[1])
        dq = jnp.where(head_mask(dqs[0].shape, 0), dqs[0], dqs[1])
        if start == 0:
            dq_ref[...] = dq
        else:
            dq_ref[start:] += dq
    rows = lax.broadcasted_iota(jnp.int32, (seq_len, lanes), 0)
    cos, sin = angle_rows(rows, starts, 4 * micro, (tcos[...], tsin[...]), start_cos.at[micro], start_sin.at[micro])
    for kind, ref in enumerate((dq_ref, dk_ref, dv_ref)):
        u = ref[...]
        if kind == 0:
            u = u * 0.125
        if kind < 2:
            u = u * cos - swap_halves(u) * sin
        out[:, kind] = u.astype(BF16).reshape(shards_n, count, lanes)

def call_attend_back(first, starts, table, start_table, got, grads, att, lse):
    parts, number, _, count, lanes = got.shape
    seq_len = parts * count
    return pl.pallas_call(functools.partial(attend_back_kernel, first), grid_spec=pltpu.PrefetchScalarGridSpec(num_scalar_prefetch=1, grid=(number,), in_specs=[whole(a.shape) for a in (*table, *start_table)] + [pl.BlockSpec((parts, None, 3, count, lanes), lambda i, _: (0, i, 0, 0, 0)), pl.BlockSpec((parts, None, count, lanes), lambda i, _: (0, first + i, 0, 0)), pl.BlockSpec((parts, None, count, lanes), lambda i, _: (0, i, 0, 0)), pl.BlockSpec((None, 8, seq_len), lambda i, _: (i, 0, 0))], out_specs=pl.BlockSpec((parts, None, 3, count, lanes), lambda i, _: (0, i, 0, 0, 0)), scratch_shapes=[pltpu.VMEM((seq_len, lanes), F32)] * 3), out_shape=jax.ShapeDtypeStruct((parts, number, 3, count, lanes), BF16), compiler_params=params(), cost_estimate=cost(number * 20 * seq_len * seq_len * lanes, number * 4000000.0, number * 2 * seq_len * seq_len), name='attend_back')(starts, *table, *start_table, got, grads, att, lse)

def mix_block(mixes, q, k):
    return jnp.concatenate([mixes[q][0][k], mixes[q][1][k]], 0)

def add_into(ref, cols, first, value):

    @pl.when(first)
    def _():
        ref[:, cols] = value

    @pl.when(jnp.logical_not(first))
    def _():
        ref[:, cols] += value

def layer_kernel(pos, *refs):
    att = [refs[0].at[:, 0], refs[0].at[:, 1], refs[1].at[:, 0]]
    x, cot, gains, shifts = refs[2:6]
    ups = [refs[6 + 2 * q:8 + 2 * q] for q in range(4)]
    downs = [refs[14 + 2 * q:16 + 2 * q] for q in range(4)]
    mixes = [refs[22 + 2 * q:24 + 2 * q] for q in range(4)]
    outputs, att_all, act, slope, keep, send, xhat1, scale1, xhat2, scale2, sums = refs[30:41]
    normed, hidden, total = refs[41:44]
    nz = mixes[0][0].shape[0]
    count = refs[0].shape[2]
    part = downs[0][0].shape[2]
    step = pl.program_id(0)

    def hand_out(index, value):
        keep[index] = value[:, :2 * part]
        send[index] = value[:, 2 * part:]

    @pl.when(step == 0)
    def _():
        for k in range(nz):
            for dx in range(2):
                place = ring_place(pos, k, nz) * 2 + lax.bitwise_xor(pos[3], dx)
                for m in range(3):
                    at = (k * 2 + dx) * 128
                    att_all[m * count:(m + 1) * count, at:at + 128] = att[m][place]
        for q in range(4):
            acc = None
            for k in range(nz):
                term = dot(att_all[:, k * 256:(k + 1) * 256], mix_block(mixes, q, k))
                acc = term if acc is None else acc + term
            total[:, q * part:(q + 1) * part] = acc
        xhat, scale = row_stats(total[...])
        xhat1[...] = xhat
        scale1[...] = jnp.broadcast_to(scale, scale1.shape)
        value = load_columns(x, pos, part).astype(F32) + xhat * gains[1:2] + shifts[1:2]
        hidden[...] = value
        xhat, scale = row_stats(value)
        xhat2[...] = xhat
        scale2[...] = jnp.broadcast_to(scale, scale2.shape)
        value = (xhat * gains[2:3] + shifts[2:3]).astype(BF16)
        normed[...] = value
        hand_out(0, value)
    for dx in range(2):
        u = None
        for q in range(4):
            term = dot(normed[:, q * part:(q + 1) * part], ups[q][dx][...])
            u = term if u is None else u + term
        square = u * u
        t = jnp.tanh(GELU_A * (u * (1.0 + GELU_B * square)))
        half = 0.5 * (1.0 + t)
        act[0, dx] = (u * half).astype(BF16)
        bend = half + 0.5 * GELU_A * u * (1.0 - t * t) * (1.0 + 3.0 * GELU_B * square)
        slope[0, dx] = bend.astype(BF16)
    for q in range(4):
        term = dot(act[0, 0], downs[q][0][0]) + dot(act[0, 1], downs[q][1][0])
        add_into(total, slice(q * part, (q + 1) * part), step == 0, term)

    @pl.when(step == nz - 1)
    def _():
        xhat, scale = row_stats(total[...])
        value = hidden[...] + xhat * gains[3:4] + shifts[3:4]
        store_columns(outputs, value, pos, part)
        grad = load_columns(cot, pos, part).astype(F32)
        sums[0:1] = column_sum(grad * xhat)
        sums[1:2] = column_sum(grad)
        hand_out(1, row_pull(grad, xhat, scale, gains[3:4]).astype(BF16))

def layer_specs(units, part, rows, nz, order):

    def up_spec(dy, dx):

        def index(i, pos):
            place = lax.bitwise_xor(pos[0], dy) * 2 + lax.bitwise_xor(pos[3], dx)
            return (place, ring_place(pos, order(i), nz), 0, 0)
        return pl.BlockSpec((None, None, part, units), index)
    ups = [up_spec(dy, dx) for _ in range(2) for dy in range(2) for dx in range(2)]
    down = pl.BlockSpec((1, units, part), lambda i, pos: (order(i), 0, 0))
    mix = pl.BlockSpec((nz, rows, part), lambda i, pos: (0, units // rows, 0))
    return ups + [down] * 8 + [mix] * 8

def layer_weights(ups, mixes):
    mixes_flat = [p for pair in mixes for p in pair]
    return [ups[0]] * 4 + [ups[1]] * 4 + mixes_flat * 2

def call_layer(pos, att, x, cot, gains, shifts, ups, mixes):
    tokens, width = x.shape
    _, nz, part, units = ups[0].shape
    rows = mixes[0][0].shape[1] - units
    act = pl.BlockSpec((1, 2, tokens, units), lambda i, pos: (i, 0, 0, 0))
    flat, column = ((tokens, width), (tokens, 128))
    side = (2, tokens, width // 2)
    ffn = jax.ShapeDtypeStruct((nz, 2, tokens, units), BF16)
    low = jax.ShapeDtypeStruct(flat, BF16)
    return pl.pallas_call(layer_kernel, grid_spec=pltpu.PrefetchScalarGridSpec(num_scalar_prefetch=1, grid=(nz,), in_specs=[whole(a.shape) for a in (*att, x, cot, gains, shifts)] + layer_specs(units, part, rows, nz, lambda i: i), out_specs=[whole(flat)] * 2 + [act] * 2 + [whole(side)] * 2 + [whole(flat), whole(column)] * 2 + [whole((8, width))], scratch_shapes=[pltpu.VMEM(flat, BF16), pltpu.VMEM(flat, F32), pltpu.VMEM(flat, F32)]), out_shape=[low, low, ffn, ffn] + [jax.ShapeDtypeStruct(side, BF16)] * 2 + [jax.ShapeDtypeStruct(flat, F32), jax.ShapeDtypeStruct(column, F32)] * 2 + [jax.ShapeDtypeStruct((8, width), F32)], compiler_params=params(), cost_estimate=cost(2 * tokens * width * (2 * nz * 2 * units + width), 40000000.0, tokens * nz * 2 * units), name='layer')(pos, *att, x, cot, gains, shifts, *layer_weights(ups, mixes))

def layer_back_kernel(pos, *refs):
    cot, gains, xhat1, scale1, xhat2, scale2, slope, keep, send = refs[0:9]
    ups = [refs[9 + 2 * q:11 + 2 * q] for q in range(4)]
    downs = [refs[17 + 2 * q:19 + 2 * q] for q in range(4)]
    mixes = [refs[25 + 2 * q:27 + 2 * q] for q in range(4)]
    g_up, keep_out, send_out, g_hidden, g_att, sums, total = refs[33:40]
    nz = mixes[0][0].shape[0]
    count = g_att.shape[2]
    part = downs[0][0].shape[2]
    step = pl.program_id(0)
    g_b2 = [keep[1, :, :part], keep[1, :, part:], send[1, :, :part], send[1, :, part:]]
    for dx in range(2):
        g = None
        for q in range(4):
            term = dot_nt(g_b2[q], downs[q][dx][0])
            g = term if g is None else g + term
        g_up[0, dx] = (g * slope[0, dx].astype(F32)).astype(BF16)
    for q in range(4):
        term = dot_nt(g_up[0, 0], ups[q][0][...]) + dot_nt(g_up[0, 1], ups[q][1][...])
        add_into(total, slice(q * part, (q + 1) * part), step == 0, term)

    @pl.when(step == nz - 1)
    def _():
        grad = total[...]
        xhat = xhat2[...]
        sums[1:2] = column_sum(grad * xhat)
        sums[3:4] = column_sum(grad)
        grad = load_columns(cot, pos, part).astype(F32) + row_pull(grad, xhat, scale2[:, 0:1], gains[2:3])
        g_hidden[...] = grad
        xhat = xhat1[...]
        sums[0:1] = column_sum(grad * xhat)
        sums[2:3] = column_sum(grad)
        g_b1 = row_pull(grad, xhat, scale1[:, 0:1], gains[1:2]).astype(BF16)
        keep_out[...] = g_b1[:, :2 * part]
        send_out[...] = g_b1[:, 2 * part:]
        for k in range(nz):
            acc = None
            for q in range(4):
                term = dot_nt(g_b1[:, q * part:(q + 1) * part], mix_block(mixes, q, k))
                acc = term if acc is None else acc + term
            acc = acc.astype(BF16)
            for dx in range(2):
                place = ring_place(pos, k, nz) * 2 + lax.bitwise_xor(pos[3], dx)
                for m in range(3):
                    g_att[place, m] = acc[m * count:(m + 1) * count, dx * 128:(dx + 1) * 128]

def call_layer_back(pos, cot, gains, kept, slope, keep, send, ups, mixes, count):
    tokens, width = cot.shape
    _, nz, part, units = ups[0].shape
    rows = mixes[0][0].shape[1] - units
    turn = nz - 1
    act = pl.BlockSpec((1, 2, tokens, units), lambda i, pos: (turn - i, 0, 0, 0))
    flat, half = ((tokens, width), (tokens, width // 2))
    heads = (2 * nz, tokens // count, count, rows)
    return pl.pallas_call(layer_back_kernel, grid_spec=pltpu.PrefetchScalarGridSpec(num_scalar_prefetch=1, grid=(nz,), in_specs=[whole(a.shape) for a in (cot, gains, *kept)] + [act, whole(keep.shape), whole(send.shape)] + layer_specs(units, part, rows, nz, lambda i: turn - i), out_specs=[act] + [whole(v) for v in (half, half, flat, heads, (8, width))], scratch_shapes=[pltpu.VMEM(flat, F32)]), out_shape=[jax.ShapeDtypeStruct(slope.shape, BF16), jax.ShapeDtypeStruct(half, BF16), jax.ShapeDtypeStruct(half, BF16), jax.ShapeDtypeStruct(flat, F32), jax.ShapeDtypeStruct(heads, BF16), jax.ShapeDtypeStruct((8, width), F32)], compiler_params=params(), cost_estimate=cost(2 * tokens * width * (2 * nz * 2 * units + width), 40000000.0), name='layer_back')(pos, cot, gains, *kept, slope, keep, send, *layer_weights(ups, mixes))

def place_piece(outs, dy, dx, cut, index, value):
    if dy == 0 and dx == 0:
        outs[0][index] = value
        return
    if cut is None:
        outs[2 * dy + dx][index] = value
        return
    low, high = outs[1 + 2 * (2 * dy + dx - 1):][:2]
    step = pl.program_id(0)

    @pl.when(step < cut)
    def _():
        low[index] = value

    @pl.when(step >= cut)
    def _():
        high[index] = value

def piece_specs(block, nz, cut):
    zeros = (0,) * (len(block) - 1)
    if cut is None:
        spec = pl.BlockSpec(block, lambda i, *_: (i,) + zeros)
        return ([spec] * 4, [jax.ShapeDtypeStruct((nz,) + block[1:], BF16)] * 4)
    low = pl.BlockSpec(block, lambda i, *_: (jnp.minimum(i, cut - 1),) + zeros)
    high = pl.BlockSpec(block, lambda i, *_: (jnp.maximum(i - cut, 0),) + zeros)
    specs = [pl.BlockSpec(block, lambda i, *_: (i,) + zeros)] + [low, high] * 3
    shapes = [nz] + [cut, nz - cut] * 3
    return (specs, [jax.ShapeDtypeStruct((n,) + block[1:], BF16) for n in shapes])

def down_grad_kernel(pos, act, act2, keep, recv, out):
    part = out.shape[3]
    for dx in range(2):
        side = jnp.concatenate([jnp.transpose(act[0, dx]), jnp.transpose(act2[0, dx])], 1)
        for dy in range(2):
            cols = slice(dy * part, (dy + 1) * part)
            grad = jnp.concatenate([keep[0, :, cols], recv[0, :, cols]], 0)
            place = lax.bitwise_xor(pos[0], dy) * 2 + lax.bitwise_xor(pos[3], dx)
            out[place, 0] = dot(side, grad).astype(BF16)

def call_down_grad(pos, act, act2, keep, recv):
    nz, _, tokens, units = act.shape
    half = keep.shape[2]
    part = half // 2
    ffn = pl.BlockSpec((1, 2, tokens, units), lambda i, pos: (i, 0, 0, 0))
    side = pl.BlockSpec((1, tokens, half), lambda i, pos: (1, 0, 0))
    return pl.pallas_call(down_grad_kernel, grid_spec=pltpu.PrefetchScalarGridSpec(num_scalar_prefetch=1, grid=(nz,), in_specs=[ffn, ffn, side, side], out_specs=pl.BlockSpec((4, 1, units, part), lambda i, pos: (0, ring_place(pos, i, nz), 0, 0))), out_shape=jax.ShapeDtypeStruct((4, nz, units, part), BF16), compiler_params=params(), cost_estimate=cost(2 * tokens * 2 * half * nz * 2 * units, 16000000.0), name='down_grad')(pos, act, act2, keep, recv)

def up_grad_kernel(cut, g_up, g_up2, keep, recv, keep1, recv1, att, att2, *refs):
    outs, flipped = (refs[:-1], refs[-1])
    part, units = (g_up.shape[3] // 2, g_up.shape[3])
    tokens = g_up.shape[2]

    @pl.when(pl.program_id(0) == 0)
    def _():
        flipped[:, :tokens] = jnp.transpose(keep[0])
        flipped[:, tokens:] = jnp.transpose(recv[0])
    side = jnp.concatenate([jnp.transpose(att[...]), jnp.transpose(att2[...])], 1)
    for dy in range(2):
        cols = slice(dy * part, (dy + 1) * part)
        both = dot(side, jnp.concatenate([keep1[:, cols], recv1[:, cols]], 0)).astype(BF16)
        for dx in range(2):
            grad = jnp.concatenate([g_up[0, dx], g_up2[0, dx]], 0)
            value = dot(flipped[cols], grad).astype(BF16)
            rows = both[dx * 128:(dx + 1) * 128]
            rows = jnp.concatenate([rows[:64], rows[64:]], 1)
            place_piece(outs, dy, dx, cut, 0, jnp.concatenate([value, rows], 0))

def call_up_grad(cut, g_up, g_up2, keep, recv, keep1, recv1, att, att2):
    nz, _, tokens, units = g_up.shape
    half = keep.shape[2]
    part = half // 2
    heads = att.shape[1] // nz
    ffn = pl.BlockSpec((1, 2, tokens, units), lambda i: (i, 0, 0, 0))
    side = pl.BlockSpec((1, tokens, half), lambda i: (0, 0, 0))
    head = pl.BlockSpec((tokens, heads), lambda i: (0, i))
    specs, shapes = piece_specs((1, part + heads // 4, units), nz, cut)
    return pl.pallas_call(functools.partial(up_grad_kernel, cut), grid=(nz,), in_specs=[ffn, ffn, side, side, whole(keep1.shape), whole(keep1.shape), head, head], out_specs=specs, out_shape=shapes, scratch_shapes=[pltpu.VMEM((half, 2 * tokens), BF16)], compiler_params=params(), cost_estimate=cost(2 * tokens * 2 * half * nz * 2 * units, 16000000.0), name='up_grad')(g_up, g_up2, keep, recv, keep1, recv1, att, att2)

def load_grads(pos, grads):
    columns = []
    for dx in range(2):
        place = lax.bitwise_xor(pos[3], dx)
        for kind in range(3):
            rows = [g[0, place, m, kind] for g in grads for m in range(g.shape[2])]
            columns.append(jnp.concatenate(rows, 0))
    return jnp.concatenate(columns, 1)

def qkv_grad_kernel(cut, pos, *refs):
    grads, keep, recv = (refs[0:4], refs[4], refs[5])
    outs, flipped = (refs[6:-1], refs[-1])
    part = outs[0].shape[2]
    tokens = keep.shape[0]

    @pl.when(pl.program_id(0) == 0)
    def _():
        flipped[:, :tokens] = jnp.transpose(keep[...])
        flipped[:, tokens:] = jnp.transpose(recv[...])
    block = load_grads(pos, grads)
    for dy in range(2):
        res = dot(flipped[dy * part:(dy + 1) * part], block).astype(BF16)
        for dx in range(2):
            for kind in range(3):
                at = (dx * 3 + kind) * 128
                place_piece(outs, dy, dx, cut, (0, kind), res[:, at:at + 128])

def call_qkv_grad(cut, pos, grads, grads2, keep, recv):
    nz, _, _, _, count, cols = grads[0].shape
    tokens, half = keep.shape
    part = half // 2
    grad_specs = [pl.BlockSpec((1,) + g.shape[1:], head_index(nz)) for g in grads]
    specs, shapes = piece_specs((1, 3, part, cols), nz, cut)
    return pl.pallas_call(functools.partial(qkv_grad_kernel, cut), grid_spec=pltpu.PrefetchScalarGridSpec(num_scalar_prefetch=1, grid=(nz,), in_specs=grad_specs * 2 + [whole(keep.shape)] * 2, out_specs=specs, scratch_shapes=[pltpu.VMEM((half, 2 * tokens), BF16)]), out_shape=shapes, compiler_params=params(), cost_estimate=cost(2 * tokens * 2 * half * 3 * nz * 2 * cols, 12000000.0), name='qkv_grad')(pos, *grads, *grads2, keep, recv)

def input_grad_kernel(pos, *refs):
    grads, x, gains, g_hidden = (refs[0:2], refs[2], refs[3], refs[4])
    weights = [refs[5 + 2 * q:7 + 2 * q] for q in range(4)]
    out, sums, total = refs[13:16]
    part = weights[0][0].shape[2]
    step = pl.program_id(0)
    block = load_grads(pos, grads)
    for q in range(4):
        side = jnp.concatenate([weights[q][dx][0, kind] for dx in range(2) for kind in range(3)], 1)
        term = dot_nt(block, side)

        @pl.when(step == 0)
        def _():
            total[:, q * part:(q + 1) * part] = term

        @pl.when(step > 0)
        def _():
            total[:, q * part:(q + 1) * part] += term

    @pl.when(step == pl.num_programs(0) - 1)
    def _():
        grad = total[...]
        xhat, scale = row_stats(load_columns(x, pos, part).astype(F32))
        sums[0:1] = column_sum(grad * xhat)
        sums[1:2] = column_sum(grad)
        value = g_hidden[...] + row_pull(grad, xhat, scale, gains[0:1])
        store_columns(out, value, pos, part)

def call_input_grad(pos, grads, x, gains, g_hidden, pieces):
    nz, _, _, _, count, cols = grads[0].shape
    tokens, width = x.shape
    part = width // 4
    grad_specs = [pl.BlockSpec((1,) + g.shape[1:], head_index(nz)) for g in grads]
    piece = pl.BlockSpec((1, 3, part, cols), lambda i, pos: (i, 0, 0, 0))
    return pl.pallas_call(input_grad_kernel, grid_spec=pltpu.PrefetchScalarGridSpec(num_scalar_prefetch=1, grid=(nz,), in_specs=grad_specs + [whole(a.shape) for a in (x, gains, g_hidden)] + [piece] * 8, out_specs=[whole((tokens, width)), whole((8, width))], scratch_shapes=[pltpu.VMEM((tokens, width), F32)]), out_shape=[jax.ShapeDtypeStruct((tokens, width), F32), jax.ShapeDtypeStruct((8, width), F32)], compiler_params=params(), cost_estimate=cost(2 * tokens * width * 3 * nz * 2 * cols, 16000000.0), name='input_grad')(pos, *grads, x, gains, g_hidden, *[p for pair in pieces for p in pair])

def sum_kernel(*refs):
    total = refs[0][...].astype(F32)
    for ref in refs[1:-1]:
        total = total + ref[...].astype(F32)
    refs[-1][...] = total.astype(BF16)

def add(*values):
    shape = values[0].shape
    block = pl.BlockSpec((1,) + shape[1:], lambda i: (i,) + (0,) * (len(shape) - 1))
    return pl.pallas_call(sum_kernel, grid=(shape[0],), in_specs=[block] * len(values), out_specs=block, out_shape=jax.ShapeDtypeStruct(shape, BF16), compiler_params=params(), cost_estimate=cost(values[0].size * len(values), 2 * values[0].size * (len(values) + 1)), name='add')(*values)

def sum_cut_kernel(cut, pos, mine, low_x, high_x, low_y, high_y, out):
    step = pl.program_id(0)

    @pl.when(step < cut)
    def _():
        total = mine[...].astype(F32) + low_x[...].astype(F32) + low_y[...].astype(F32)
        out[...] = total.astype(BF16)

    @pl.when(step >= cut)
    def _():
        total = mine[...].astype(F32) + high_x[...].astype(F32) + high_y[...].astype(F32)
        out[...] = total.astype(BF16)

def sum_ring_kernel(pos, *refs):
    sum_kernel(*refs)

def send_direct(parts):
    corner = lax.ppermute(parts[3], ('y', 'x'), [(i, 3 - i) for i in range(4)])
    return (corner, swap(parts[1], 'x'), swap(parts[2], 'y'))

def add_direct(pos, values):
    shape = values[0].shape
    nz = shape[0]
    block = (1,) + shape[1:]
    zeros = (0,) * (len(block) - 1)
    return pl.pallas_call(sum_ring_kernel, grid_spec=pltpu.PrefetchScalarGridSpec(num_scalar_prefetch=1, grid=(nz,), in_specs=[pl.BlockSpec(block, lambda i, pos: (i,) + zeros)] * len(values), out_specs=pl.BlockSpec(block, lambda i, pos: (ring_place(pos, i, nz),) + zeros)), out_shape=jax.ShapeDtypeStruct(shape, BF16), compiler_params=params(), cost_estimate=cost(values[0].size * 4, 10 * values[0].size), name='add_direct')(pos, *values)

def add_sides(cut, pos, mine, sides, ordered=True):
    nz = mine.shape[0]
    block = (1,) + mine.shape[1:]
    specs, _ = piece_specs(block, nz, cut)
    zeros = (0,) * (len(block) - 1)
    return pl.pallas_call(functools.partial(sum_cut_kernel, cut), grid_spec=pltpu.PrefetchScalarGridSpec(num_scalar_prefetch=1, grid=(nz,), in_specs=specs[:5], out_specs=pl.BlockSpec(block, lambda i, pos: (ring_place(pos, i, nz) if ordered else i,) + zeros)), out_shape=jax.ShapeDtypeStruct(mine.shape, BF16), compiler_params=params(), cost_estimate=cost(mine.size * 2, 8 * mine.size), name='add_sides')(pos, mine, *sides)

def after(values, *others):
    return lax.optimization_barrier((values, others))[0]

def swap(values, axis):
    return lax.ppermute(values, axis, SWAP)

def ring(values, step, size):
    return lax.ppermute(values, 'z', [(i, (i + step) % size) for i in range(size)])

def gather_sides(mine):
    return (swap(mine, 'x'), swap(mine, 'y'))

def gather_corner(over_x, over_y, cut):
    return jnp.concatenate([swap(over_x[:cut], 'y'), swap(over_y[cut:], 'x')])

def pair_up(mine, over_x, over_y, corner):
    return [[mine, over_x], [over_y, corner]]

def send_corner(parts):
    return (swap(parts[5], 'y'), swap(parts[6], 'x'))

def add_pair_kernel(a, b, c, d, first, second):
    first[...] = (a[...].astype(F32) + b[...].astype(F32)).astype(BF16)
    second[...] = (c[...].astype(F32) + d[...].astype(F32)).astype(BF16)

def corner_sums(parts, corner):
    if parts[1].shape != parts[4].shape:
        return (add(parts[1], corner[0]), add(parts[4], corner[1]))
    shape = parts[1].shape
    block = pl.BlockSpec((1,) + shape[1:], lambda i: (i,) + (0,) * (len(shape) - 1))
    return pl.pallas_call(add_pair_kernel, grid=(shape[0],), in_specs=[block] * 4, out_specs=[block] * 2, out_shape=[jax.ShapeDtypeStruct(shape, BF16)] * 2, compiler_params=params(), cost_estimate=cost(parts[1].size * 4, parts[1].size * 12), name='add_pair')(parts[1], corner[0], parts[4], corner[1])

def send_sides(parts, sums):
    high_x, low_y = after((parts[2], parts[3]), sums)
    return (swap(sums[0], 'x'), swap(high_x, 'x'), swap(low_y, 'y'), swap(sums[1], 'y'))

def plane_norms(sums, part):
    pieces = [sums[:, q * part:(q + 1) * part] for q in range(4)]
    low, high = (pieces[dy] + swap(pieces[2 + dy], 'c') for dy in range(2))
    mine = low + swap(high, 'y')
    return mine + swap(mine, 'x')

def line_norms(mine):
    mine = mine + lax.ppermute(mine, 'z', [(i, i ^ 1) for i in range(4)])
    return mine + lax.ppermute(mine, 'z', [(i, i ^ 2) for i in range(4)])

def fast_shards(inputs, doc_starts, w_qkv, w_out, w_up, w_down, norm_gains, norm_biases, cotangent):
    pos = jnp.stack([lax.axis_index(name) for name in ('y', 'c', 'z', 'x')]).astype(jnp.int32)
    nz = lax.axis_size('z')
    parts = nz * 2
    micro, _, shard_len, width = inputs.shape
    tokens = micro * shard_len
    seq_len = shard_len * parts
    part = width // 4
    cols = w_qkv.shape[2]
    half = nz // 2
    starts = doc_starts.reshape(-1)
    x = inputs.reshape(tokens, width)
    cot = cotangent.reshape(tokens, width)

    def exchange(values):
        return lax.all_to_all(values, SEQ, 0, 0, tiled=True)
    rings = [ring(w_qkv, nz - k, nz) for k in range(1, nz)]
    norms = jnp.concatenate([norm_gains, norm_biases])
    norms_y, norms_c = (swap(norms, 'y'), swap(norms, 'c'))
    norms = jnp.concatenate([norms, norms_y, norms_c, swap(norms_y, 'c')], 1).astype(F32)
    gains, shifts = (norms[:4], norms[4:])
    start_table = start_tables(doc_starts[:, 0])
    table = tables(seq_len)
    mix = jnp.concatenate([w_down, w_out])
    qkv_mine, mix = after((jnp.stack([w_qkv] + rings), mix), norms, start_table)
    mix1, mix3 = (ring(after(mix, qkv_mine), k, nz) for k in (nz - 1, 1))
    qkv_sides = after(gather_sides(qkv_mine), mix1, mix3)
    mix2 = ring(after(mix, qkv_sides), nz - 2, nz)
    qkv_corner = gather_corner(*qkv_sides, half)
    qkv_other = [swap(p, 'c') for p in (qkv_mine, *qkv_sides)]
    qkv_corner = after(qkv_corner, qkv_other)
    up_mine = lax.all_gather(after(w_up, qkv_corner), 'z', axis=0, tiled=False)
    mix_mine = jnp.stack([mix, mix1, mix2, mix3])
    qkv_other.append(swap(qkv_corner, 'c'))
    qkv = pair_up(qkv_mine, *qkv_sides, qkv_corner) + pair_up(*qkv_other)
    first, last, keep0, send1 = call_proj(pos, starts, x, gains, shifts, table, start_table, qkv, shard_len)
    mix_mine = after(mix_mine, first)
    mix_sides = gather_sides(mix_mine)
    got = [None, None]
    got[0] = exchange(first.reshape(parts, 2, 3, shard_len, cols))
    got[1] = exchange(after(last.reshape(parts, 1, 3, shard_len, cols), got[0]))
    mix_corner = gather_corner(*mix_sides, 3)
    mix_other = [swap(p, 'c') for p in (mix_mine, *mix_sides)]
    att_local, lses, att = ([None, None], [None, None], [None, None])
    got[0] = after(got[0], mix_other, mix_corner)
    up_own = lax.all_gather(after(up_mine, got[0]), ('y', 'x'), axis=0, tiled=False)
    mix_other.append(swap(mix_corner, 'c'))
    att_local[0], lses[0] = call_attend(0, starts, got[0])
    got[1] = after(got[1], att_local[0], mix_corner)
    att[0] = exchange(att_local[0])
    att_local[1], lses[1] = call_attend(2, starts, got[1])
    att[0] = after(att[0], att_local[1], mix_other)
    att[1] = exchange(after(att_local[1], att[0]))
    mixes = pair_up(mix_mine, *mix_sides, mix_corner) + pair_up(*mix_other)
    up_own = after(up_own, att[1])
    ups = [up_own, swap(up_own, 'c')]
    res = call_layer(pos, att, x, cot, gains, shifts, ups, mixes)
    outputs, att_all, act, slope, keep, send = res[:6]
    kept, sums3 = (res[6:10], res[10])
    recv, act2, att_all2, recv0 = (swap(v, 'c') for v in (send, act, att_all, send1))
    res = call_layer_back(pos, cot, gains, kept, slope, keep, send, ups, mixes, shard_len)
    g_up, keep1, send1, g_hidden, g_att, sums = res
    back, back2 = ([None, None], [None, None])
    recv1, g_up2 = (swap(send1, 'c'), swap(g_up, 'c'))
    act2 = after(act2, g_up)
    down_parts = call_down_grad(pos, act, act2, keep, recv)
    down_sum = lax.psum_scatter(down_parts, ('y', 'x'), scatter_dimension=0, tiled=True)
    down_sum = down_sum.reshape(down_parts.shape[1:])
    g_up = after(g_up, down_parts)
    grad = exchange(g_att)
    grad = after(grad, down_parts)
    res2 = call_attend_back(2, starts, table, start_table, got[1], grad, att_local[1], lses[1])
    back[1] = exchange(res2)
    grad = after(grad, res2)
    res = call_attend_back(0, starts, table, start_table, got[0], grad, att_local[0], lses[0])
    up_parts = call_up_grad(None, after(g_up, res), g_up2, keep, recv, keep1, recv1, att_all, att_all2)
    up_sent = send_direct(up_parts)
    back[1] = after(back[1], res)
    back[0] = exchange(after(res, back[1]))
    back2[1] = swap(back[1].reshape((nz, 2) + back[1].shape[1:]), 'c')
    back[0] = after(back[0], down_sum)
    down_sum = lax.psum_scatter(down_sum, 'z', scatter_dimension=0, tiled=False)
    back[0] = after(back[0], back2[1], up_parts)
    back[0] = after(back[0], up_sent[1], up_sent[2])
    back = [b.reshape((nz, 2) + b.shape[1:]) for b in back]
    back2[0] = swap(back[0], 'c')
    qkv_cut = half
    qkv_parts = call_qkv_grad(qkv_cut, pos, back, back2, keep0, recv0)
    back = after(back, qkv_parts)
    up_sent = after(up_sent, qkv_parts)
    qkv_corner = send_corner(qkv_parts)
    qkv_sums = corner_sums(qkv_parts, qkv_corner)
    qkv_sent = send_sides(qkv_parts, qkv_sums)
    inputs_grad, sums0 = call_input_grad(pos, after(back, qkv_sums), x, gains, g_hidden, qkv)
    up_sum = add_direct(pos, (up_parts[0], *up_sent))
    qkv_sent = after(qkv_sent, up_sum)
    up_sum = lax.psum_scatter(up_sum, 'z', scatter_dimension=0, tiled=False)
    norm_sums = [sums0[:1], sums[:2], sums3[:1], sums0[1:2], sums[2:4], sums3[1:2]]
    norm_sums = jnp.concatenate(norm_sums)
    qkv_sent, norm_sums = after((qkv_sent, norm_sums), norm_sums, down_sum)
    qkv_sum = add_sides(half, pos, qkv_parts[0], qkv_sent, True)
    norm_sums = line_norms(plane_norms(after(norm_sums, qkv_sum), part))
    qkv_sum = lax.psum_scatter(qkv_sum, 'z', scatter_dimension=0, tiled=False)
    down_sum = down_sum.astype(F32)
    up_sum, out_sum = (up_sum[:part].astype(F32), up_sum[part:].astype(F32))
    out_sum = jnp.concatenate([out_sum[:, :part], out_sum[:, part:]], 0)
    qkv_sum = after(qkv_sum, norm_sums, down_sum, out_sum, up_sum)
    return (outputs.reshape(inputs.shape), inputs_grad.reshape(inputs.shape), qkv_sum.astype(F32), out_sum, up_sum, down_sum, norm_sums[:4], norm_sums[4:])

def fits_fast(mesh, inputs, w_qkv, w_up):
    dp, tensor = (mesh.shape['dp'], mesh.shape['tensor'])
    return dp == 4 and tensor == 8 and (inputs.shape[0] == 3) and (inputs.shape[1] == dp) and (inputs.shape[2] == 1024) and (w_qkv.shape[1:] == (1024, 1024)) and (w_up.shape[1] == 4096)

def solution(mesh):
    dp, tensor = (mesh.shape['dp'], mesh.shape['tensor'])
    names = ('y', 'c', 'z', 'x')
    fine = Mesh(mesh.devices.reshape(dp // 2, 2, 4, tensor // 4), names)
    rows, seq = (('y', 'c'), ('z', 'x'))
    tokens = P(None, rows, seq, None)
    weights = (P(None, rows, seq), P(seq, rows), P(rows, seq), P(seq, rows))
    norm = P(None, rows)

    def run(*arrays):
        fast = fits_fast(mesh, arrays[0], arrays[2], arrays[4])
        return jax.shard_map(fast_shards if fast else shards, mesh=fine, in_specs=(tokens, P(None, rows, None)) + weights + (norm, norm, tokens), out_specs=(tokens, tokens) + weights + (norm, norm), check_vma=False)(*arrays)
    return run
```

```python
import functools
import math
import jax
import jax.numpy as jnp
import numpy as np
from jax import lax
from jax.experimental import pallas as pl
from jax.experimental.pallas import tpu as pltpu
from jax.sharding import Mesh, PartitionSpec as P
HD = 64
EPSILON = 1e-05
F32 = jnp.float32
BF16 = jnp.bfloat16
CHIPS = ('y', 'z', 'x')
SEQ = ('z', 'x')
SWAP = [(0, 1), (1, 0)]

def ln_forward(values, gain, shift):
    average = jnp.mean(values, axis=-1, keepdims=True)
    centred = values - average
    variance = jnp.mean(centred * centred, axis=-1, keepdims=True)
    scale = lax.rsqrt(variance + EPSILON)
    xhat = centred * scale
    return (xhat * gain + shift, xhat, scale)

def ln_backward(grad, xhat, scale, gain):
    e = grad * gain
    dv = scale * (e - jnp.mean(e, axis=-1, keepdims=True) - xhat * jnp.mean(e * xhat, axis=-1, keepdims=True))
    return (dv, jnp.sum(grad * xhat, axis=0), jnp.sum(grad, axis=0))

def rotate(values, cosines, sines):
    half_dim = values.shape[-1] // 2
    lower = values[..., :half_dim]
    upper = values[..., half_dim:]
    return jnp.concatenate([lower * cosines - upper * sines, upper * cosines + lower * sines], axis=-1)

def doc_layout(starts, token_index):
    inside = token_index[:, None] >= starts[None, :]
    segment = jnp.sum(inside.astype(jnp.int32), axis=1)
    begins = jnp.max(jnp.where(inside, starts[None, :], 0), axis=1)
    return (segment, token_index - begins)

def angles_of(position):
    frequency = jnp.exp(jnp.arange(HD // 2, dtype=F32) * (-2.0 * math.log(10000.0) / HD))
    angles = position.astype(F32)[..., None] * frequency
    return (jnp.cos(angles), jnp.sin(angles))

def block_mask(segment, offset, block_len, key_len):
    query_pos = jnp.arange(offset, offset + block_len, dtype=jnp.int32)
    key_pos = jnp.arange(key_len, dtype=jnp.int32)
    causal = key_pos[None, :] <= query_pos[:, None]
    return causal & (segment[offset:offset + block_len, None] == segment[None, :key_len])

def attention_forward(q, k, v, segment):
    seq_len = q.shape[1]
    block_len = min(512, seq_len)
    pieces, lses = ([], [])
    for offset in range(0, seq_len, block_len):
        end = offset + block_len
        allowed = block_mask(segment, offset, block_len, end)[None]
        scores = 0.125 * jnp.einsum('hqe,hke->hqk', q[:, offset:end], k[:, :end], preferred_element_type=F32)
        scores = jnp.where(allowed, scores, -1e+30)
        peak = jnp.max(scores, axis=-1, keepdims=True)
        lse = peak + jnp.log(jnp.sum(jnp.exp(scores - peak), axis=-1, keepdims=True))
        probs = jnp.exp(scores - lse).astype(BF16)
        pieces.append(jnp.einsum('hqk,hke->hqe', probs, v[:, :end], preferred_element_type=F32).astype(BF16))
        lses.append(lse)
    return (jnp.concatenate(pieces, axis=1), lses)

def attention_backward(q, k, v, do, lses, segment):
    seq_len = q.shape[1]
    block_len = min(512, seq_len)
    dq = []
    dk = jnp.zeros(k.shape, F32)
    dv = jnp.zeros(v.shape, F32)
    for index, offset in enumerate(range(0, seq_len, block_len)):
        end = offset + block_len
        allowed = block_mask(segment, offset, block_len, end)[None]
        qb, kb, vb, dob = (q[:, offset:end], k[:, :end], v[:, :end], do[:, offset:end])
        scores = 0.125 * jnp.einsum('hqe,hke->hqk', qb, kb, preferred_element_type=F32)
        scores = jnp.where(allowed, scores, -1e+30)
        soft = jnp.exp(scores - lses[index])
        probs = soft.astype(BF16)
        dp = jnp.einsum('hqe,hke->hqk', dob, vb, preferred_element_type=F32)
        dot = jnp.sum(soft * dp, axis=-1, keepdims=True)
        ds = (soft * (dp - dot)).astype(BF16)
        dq.append(0.125 * jnp.einsum('hqk,hke->hqe', ds, kb, preferred_element_type=F32))
        pad = ((0, 0), (0, seq_len - end), (0, 0))
        dk = dk + jnp.pad(0.125 * jnp.einsum('hqk,hqe->hke', ds, qb, preferred_element_type=F32), pad)
        dv = dv + jnp.pad(jnp.einsum('hqk,hqe->hke', probs, dob, preferred_element_type=F32), pad)
    return (jnp.concatenate(dq, axis=1), dk, dv)

def gather_both(shard):
    mine = lax.all_gather(shard, CHIPS, axis=0, tiled=False)
    return jnp.stack([mine, lax.ppermute(mine, 'c', SWAP)])

def scatter_both(partial, sizes):
    ny, nz, nx = sizes
    shard_shape = partial.shape[2:]
    low = partial.astype(BF16)
    got = lax.ppermute(low[1], 'c', SWAP)
    mine = (low[0].astype(F32) + got.astype(F32)).astype(BF16)
    mine = mine.reshape((ny, nz, nx) + shard_shape)
    mine = mine.transpose((0, 2, 1) + tuple(range(3, mine.ndim)))
    mine = mine.reshape((ny * nx, nz) + shard_shape)
    mine = lax.psum_scatter(mine, ('y', 'x'), scatter_dimension=0, tiled=False)
    return lax.psum_scatter(mine, 'z', scatter_dimension=0, tiled=False).astype(F32)

def shards(inputs, doc_starts, w_qkv, w_out, w_up, w_down, norm_gains, norm_biases, cotangent):
    ny, nz, nx = (lax.axis_size(name) for name in CHIPS)
    core = lax.axis_index('c')
    sizes = (ny, nz, nx)
    parts = nz * nx
    micro, _, shard_len, width = inputs.shape
    tokens = micro * shard_len
    seq_len = shard_len * parts
    dpart = width // (2 * ny)
    hcols = w_out.shape[0]
    heads = hcols // HD
    units = w_up.shape[1]

    def to_own(values):
        pieces = values.reshape(values.shape[:-1] + (ny, 2, dpart))
        pieces = jnp.where(core == 0, pieces, pieces[..., ::-1, :])
        return jnp.swapaxes(pieces, -3, -2).reshape(values.shape)

    def from_own(values):
        pieces = jnp.swapaxes(values.reshape(values.shape[:-1] + (2, ny, dpart)), -3, -2)
        return jnp.where(core == 0, pieces, pieces[..., ::-1, :]).reshape(values.shape)
    qkv_all = gather_both(w_qkv).reshape(2, ny, parts, 3, dpart, hcols)
    norms = jnp.stack([norm_gains, norm_biases])
    norms = gather_dp(norms, ny, dpart)
    norms = to_own(norms.astype(F32))
    gains, shifts = (norms[0], norms[1])
    out_all = gather_both(w_out).reshape(2, ny, parts, hcols, dpart)
    up_all = gather_both(w_up).reshape(2, ny, parts, dpart, units)
    down_all = gather_both(w_down).reshape(2, ny, parts, units, dpart)
    qkv_full = qkv_all.transpose(0, 1, 4, 3, 2, 5).reshape(width, 3 * parts * hcols)
    out_full = out_all.transpose(2, 3, 0, 1, 4).reshape(parts * hcols, width)
    up_full = up_all.transpose(0, 1, 3, 2, 4).reshape(width, parts * units)
    down_full = down_all.transpose(2, 3, 0, 1, 4).reshape(parts * units, width)
    x = to_own(inputs.reshape(tokens, width)).astype(F32)
    cot = to_own(cotangent.reshape(tokens, width)).astype(F32)
    place = lax.axis_index(SEQ) * shard_len + jnp.arange(shard_len, dtype=jnp.int32)
    cos_own, sin_own, cos_row, sin_row, segments = ([], [], [], [], [])
    for index in range(micro):
        starts = doc_starts[index, 0]
        c, s = angles_of(doc_layout(starts, place)[1])
        cos_own.append(c)
        sin_own.append(s)
        segment, position = doc_layout(starts, jnp.arange(seq_len, dtype=jnp.int32))
        c, s = angles_of(position)
        cos_row.append(c)
        sin_row.append(s)
        segments.append(segment)
    cos_own = jnp.concatenate(cos_own)[:, None, None]
    sin_own = jnp.concatenate(sin_own)[:, None, None]
    normed1, xhat0, scale0 = ln_forward(x, gains[0], shifts[0])
    normed1 = normed1.astype(BF16)
    projected = jnp.dot(normed1, qkv_full, preferred_element_type=F32)
    projected = projected.reshape(tokens, 3, parts * heads, HD)
    rotated = rotate(projected[:, :2], cos_own, sin_own)
    projected = jnp.concatenate([rotated, projected[:, 2:]], axis=1).astype(BF16)
    projected = projected.reshape(micro, shard_len, 3, parts, hcols).transpose(0, 3, 2, 1, 4)

    def to_heads(values):
        kinds = values.shape[1]
        got = lax.all_to_all(values, SEQ, 0, 0, tiled=True)
        got = got.reshape(parts, kinds, shard_len, heads, HD).transpose(1, 3, 0, 2, 4)
        return got.reshape(kinds, heads, seq_len, HD)

    def to_tokens(values):
        kinds = values.shape[0]
        sent = values.reshape(kinds, heads, parts, shard_len, HD).transpose(2, 0, 3, 1, 4)
        sent = sent.reshape(parts, kinds, shard_len, hcols)
        return lax.all_to_all(sent, SEQ, 0, 0, tiled=True)
    qkvs, lses, attended = ([], [], [])
    for index in range(micro):
        q, k, v = to_heads(projected[index])
        out, lse = attention_forward(q, k, v, segments[index])
        qkvs.append((q, k, v))
        lses.append(lse)
        attended.append(to_tokens(out[None])[:, 0])
    attended = jnp.stack(attended).transpose(0, 2, 1, 3).reshape(tokens, parts * hcols)
    branch1 = jnp.dot(attended, out_full, preferred_element_type=F32)
    post1, xhat1, scale1 = ln_forward(branch1, gains[1], shifts[1])
    hidden = x + post1
    normed2, xhat2, scale2 = ln_forward(hidden, gains[2], shifts[2])
    normed2 = normed2.astype(BF16)
    up_act = jnp.dot(normed2, up_full, preferred_element_type=F32)
    gated, gate_pull = jax.vjp(lambda u: jax.nn.gelu(u, approximate=True), up_act)
    activated = gated.astype(BF16)
    branch2 = jnp.dot(activated, down_full, preferred_element_type=F32)
    post2, xhat3, scale3 = ln_forward(branch2, gains[3], shifts[3])
    outputs = (hidden + post2).astype(BF16)
    grad_branch2, gain3, shift3 = ln_backward(cot, xhat3, scale3, gains[3])
    grad_branch2 = grad_branch2.astype(BF16)
    down_part = jnp.einsum('tf,td->fd', activated, grad_branch2, preferred_element_type=F32)
    down_part = down_part.astype(BF16).reshape(parts, units, 2, ny, dpart)
    down_grad = scatter_both(down_part.transpose(2, 3, 0, 1, 4).reshape(2, ny * parts, units, dpart), sizes)
    grad_act = jnp.einsum('td,fd->tf', grad_branch2, down_full, preferred_element_type=F32)
    grad_up = gate_pull(grad_act)[0].astype(BF16)
    up_part = jnp.einsum('td,tf->df', normed2, grad_up, preferred_element_type=F32)
    up_part = up_part.astype(BF16).reshape(2, ny, dpart, parts, units)
    up_grad = scatter_both(up_part.transpose(0, 1, 3, 2, 4).reshape(2, ny * parts, dpart, units), sizes)
    grad_normed2 = jnp.einsum('tf,df->td', grad_up, up_full, preferred_element_type=F32)
    extra, gain2, shift2 = ln_backward(grad_normed2, xhat2, scale2, gains[2])
    grad_hidden = cot + extra
    grad_branch1, gain1, shift1 = ln_backward(grad_hidden, xhat1, scale1, gains[1])
    grad_branch1 = grad_branch1.astype(BF16)
    grad_attended = jnp.einsum('td,fd->tf', grad_branch1, out_full, preferred_element_type=F32).astype(BF16)
    grad_attended = grad_attended.reshape(micro, shard_len, parts, 1, hcols)
    grad_attended = grad_attended.transpose(0, 2, 3, 1, 4)
    out_part = jnp.einsum('tf,td->fd', attended, grad_branch1, preferred_element_type=F32)
    out_part = out_part.astype(BF16).reshape(parts, hcols, 2, ny, dpart)
    out_grad = scatter_both(out_part.transpose(2, 3, 0, 1, 4).reshape(2, ny * parts, hcols, dpart), sizes)
    grad_projected = []
    for index in range(micro):
        do = to_heads(grad_attended[index])[0]
        q, k, v = qkvs[index]
        dq, dk, dv = attention_backward(q, k, v, do, lses[index], segments[index])
        cos, sin = (cos_row[index], -sin_row[index])
        back = jnp.stack([rotate(dq, cos, sin), rotate(dk, cos, sin), dv]).astype(BF16)
        grad_projected.append(to_tokens(back))
    grad_projected = jnp.stack(grad_projected).transpose(0, 3, 2, 1, 4)
    grad_projected = grad_projected.reshape(tokens, 3 * parts * hcols)
    qkv_part = jnp.einsum('td,te->de', normed1, grad_projected, preferred_element_type=F32)
    qkv_part = qkv_part.astype(BF16).reshape(2, ny, dpart, 3, parts, hcols)
    qkv_grad = scatter_both(qkv_part.transpose(0, 1, 4, 3, 2, 5).reshape(2, ny * parts, 3, dpart, hcols), sizes)
    grad_normed1 = jnp.einsum('te,de->td', grad_projected, qkv_full, preferred_element_type=F32)
    extra, gain0, shift0 = ln_backward(grad_normed1, xhat0, scale0, gains[0])
    inputs_grad = grad_hidden + extra
    sums = jnp.stack([gain0, gain1, gain2, gain3, shift0, shift1, shift2, shift3])
    sums = lax.psum(from_own(sums), ('y', 'c', 'z', 'x'))
    place = (lax.axis_index('y') * 2 + core) * dpart
    sums = lax.dynamic_slice_in_dim(sums, place, dpart, 1)
    return (from_own(outputs).reshape(inputs.shape), from_own(inputs_grad).reshape(inputs.shape), qkv_grad, out_grad, up_grad, down_grad, sums[:4], sums[4:])

def gather_dp(norms, ny, dpart):
    full = lax.all_gather(norms, ('y', 'c'), axis=2, tiled=True)
    return full
NT = (((1,), (1,)), ((), ()))
GELU_A = 0.7978845608
GELU_B = 0.044715
COST = 0.2

def dot(a, b):
    return jnp.dot(a, b, preferred_element_type=F32)

def dot_nt(a, b):
    return lax.dot_general(a, b, NT, preferred_element_type=F32)

def params(semantics=1):
    return pltpu.CompilerParams(dimension_semantics=('arbitrary',) * semantics, vmem_limit_bytes=60 * 1024 * 1024)

def cost(flops, size, transcendentals=0):
    return pl.CostEstimate(flops=int(flops * COST), bytes_accessed=int(size * COST), transcendentals=int(transcendentals * COST))

def whole(shape):
    return pl.BlockSpec(shape, lambda *_: (0,) * len(shape))

def swap_halves(values):
    lane = lax.broadcasted_iota(jnp.int32, values.shape, 1)
    low = lax.rem(lane, HD) < HD // 2
    return jnp.where(low, pltpu.roll(values, 96, 1), pltpu.roll(values, 32, 1))

def row_stats(values):
    average = jnp.mean(values, axis=-1, keepdims=True)
    centred = values - average
    variance = jnp.mean(centred * centred, axis=-1, keepdims=True)
    scale = lax.rsqrt(variance + EPSILON)
    return (centred * scale, scale)

def row_pull(grad, xhat, scale, gain):
    e = grad * gain
    return scale * (e - jnp.mean(e, axis=-1, keepdims=True) - xhat * jnp.mean(e * xhat, axis=-1, keepdims=True))

def column_sum(values):
    return jnp.sum(values, axis=0, keepdims=True)

def own_place(pos, q, part):
    place = lax.bitwise_xor(pos[0], q % 2) * 2 + lax.bitwise_xor(pos[1], q // 2)
    return pl.multiple_of(place * part, part)

def load_columns(ref, pos, part):
    return jnp.concatenate([ref[:, pl.ds(own_place(pos, q, part), part)] for q in range(4)], 1)

def store_columns(ref, values, pos, part):
    for q in range(4):
        ref[:, pl.ds(own_place(pos, q, part), part)] = values[:, q * part:(q + 1) * part].astype(ref.dtype)

def tables(seq_len):
    lane = np.arange(128)
    frequency = np.exp(lane % (HD // 2) * (-2.0 * math.log(10000.0) / HD))
    angle = np.arange(seq_len)[:, None] * frequency.astype(np.float32).astype(np.float64)
    sign = np.where(lane % HD < HD // 2, -1.0, 1.0)
    return (np.cos(angle).astype(np.float32), (np.sin(angle) * sign).astype(np.float32))

def start_tables(starts):
    lane = jnp.arange(128)
    frequency = jnp.exp((lane % (HD // 2)).astype(F32) * (-2.0 * math.log(10000.0) / HD))
    angle = starts.astype(F32)[..., None] * frequency
    return (jnp.cos(angle), jnp.sin(angle) * jnp.where(lane % HD < HD // 2, -1.0, 1.0))

def angle_rows(rows, starts, base, table, start_cos, start_sin):
    cb, sb = (start_cos[0:1], start_sin[0:1])
    for d in range(1, 4):
        inside = rows >= starts[base + d]
        cb = jnp.where(inside, start_cos[d:d + 1], cb)
        sb = jnp.where(inside, start_sin[d:d + 1], sb)
    tc, ts = table
    return (tc * cb + ts * sb, ts * cb - tc * sb)

def begin_of(rows, starts, base):
    begin = jnp.zeros(rows.shape, jnp.int32)
    for d in range(1, 4):
        begin = jnp.where(rows >= starts[base + d], starts[base + d], begin)
    return begin

def proj_kernel(pos, starts, x, gains, shifts, tcos, tsin, start_cos, start_sin, *refs):
    weights = [refs[2 * q:2 * q + 2] for q in range(4)]
    first, last, keep, send = refs[8:12]
    normed, cos, sin = refs[12:15]
    outs = [first.at[0, :, 0], first.at[0, :, 1], last.at[0, :, 0]]
    part = weights[0][0].shape[2]
    count = first.shape[4]

    @pl.when(pl.program_id(0) == 0)
    def _():
        xhat, _ = row_stats(load_columns(x, pos, part).astype(F32))
        value = (xhat * gains[0:1] + shifts[0:1]).astype(BF16)
        normed[...] = value
        keep[...] = value[:, :2 * part]
        send[...] = value[:, 2 * part:]
        rows = lax.broadcasted_iota(jnp.int32, (count, 128), 0) + (pos[2] * 2 + pos[3]) * count
        for m in range(3):
            at = slice(m * count, (m + 1) * count)
            cos[at], sin[at] = angle_rows(rows, starts, 4 * m, (tcos[...], tsin[...]), start_cos.at[m], start_sin.at[m])
    total = None
    for q in range(4):
        block = jnp.concatenate([weights[q][dx][0, kind] for dx in range(2) for kind in range(3)], 1)
        term = dot(normed[:, q * part:(q + 1) * part], block)
        total = term if total is None else total + term
    for dx in range(2):
        place = lax.bitwise_xor(pos[3], dx)
        for kind in range(3):
            at = (dx * 3 + kind) * 128
            u = total[:, at:at + 128]
            if kind < 2:
                u = u * cos[...] + swap_halves(u) * sin[...]
            u = u.astype(BF16)
            for m in range(3):
                outs[m][place, kind] = u[m * count:(m + 1) * count]

def ring_place(pos, i, nz):
    return lax.rem(pos[2] + i, nz)

def head_index(nz):
    return lambda i, pos, *_: (ring_place(pos, i, nz), 0, 0, 0, 0, 0)

def call_proj(pos, starts, x, gains, shifts, table, start_table, pieces, shard_len):
    tokens, width = x.shape
    nz, _, part, cols = pieces[0][0].shape
    piece = pl.BlockSpec((1, 3, part, cols), lambda i, *_: (i, 0, 0, 0))
    outs = [pl.BlockSpec((1, 2, n, 3, shard_len, cols), head_index(nz)) for n in (2, 1)]
    shapes = [jax.ShapeDtypeStruct((nz, 2, n, 3, shard_len, cols), BF16) for n in (2, 1)]
    half = (tokens, width // 2)
    rows = pl.BlockSpec((shard_len, 128), lambda i, pos, _: (pos[2] * 2 + pos[3], 0))
    return pl.pallas_call(proj_kernel, grid_spec=pltpu.PrefetchScalarGridSpec(num_scalar_prefetch=2, grid=(nz,), in_specs=[whole(a.shape) for a in (x, gains, shifts)] + [rows] * 2 + [whole(a.shape) for a in start_table] + [piece] * 8, out_specs=outs + [whole(half)] * 2, scratch_shapes=[pltpu.VMEM((tokens, width), BF16), pltpu.VMEM((tokens, 128), F32), pltpu.VMEM((tokens, 128), F32)]), out_shape=shapes + [jax.ShapeDtypeStruct(half, BF16)] * 2, compiler_params=params(), cost_estimate=cost(2 * tokens * width * 3 * nz * 2 * cols, 12000000.0), name='project')(pos, starts, x, gains, shifts, *table, *start_table, *[p for pair in pieces for p in pair])

def head_mask(shape, head):
    lane = lax.broadcasted_iota(jnp.int32, shape, 1)
    return lane < HD if head == 0 else lane >= HD

def attend_kernel(first, starts, got, out, lse_out):
    micro = first + pl.program_id(0)
    shards_n, _, count, lanes = got.shape
    seq_len = shards_n * count
    block = min(256, seq_len)
    q_all = (got[:, 0] * 0.125).reshape(seq_len, lanes)
    k_all = got[:, 1].reshape(seq_len, lanes)
    v_all = got[:, 2].reshape(seq_len, lanes)
    per = block // count
    for start in range(0, seq_len, block):
        end = start + block
        qb = q_all[start:end]
        key = lax.broadcasted_iota(jnp.int32, (block, end), 1)
        query = start + lax.broadcasted_iota(jnp.int32, (block, end), 0)
        begin = begin_of(start + lax.broadcasted_iota(jnp.int32, (block, 1), 0), starts, 4 * micro)
        allowed = (key <= query) & (key >= begin)
        results = []
        for head in range(2):
            mask = head_mask(qb.shape, head)
            scores = dot_nt(jnp.where(mask, qb, 0), k_all[:end])
            scores = jnp.where(allowed, scores, -1e+30)
            peak = jnp.max(scores, axis=-1, keepdims=True)
            e = jnp.exp(scores - peak)
            total = jnp.sum(e, axis=-1, keepdims=True)
            results.append(dot(e.astype(BF16), v_all[:end]) / total)
            lse = jnp.broadcast_to(peak + jnp.log(total), (block, 128))
            lse_out[head:head + 1, start:end] = jnp.transpose(lse)[0:1]
        mixed = jnp.where(head_mask(results[0].shape, 0), results[0], results[1]).astype(BF16)
        out[start // count:end // count] = mixed.reshape(per, count, lanes)

def call_attend(first, starts, got):
    parts, number, _, count, lanes = got.shape
    seq_len = parts * count
    return pl.pallas_call(functools.partial(attend_kernel, first), grid_spec=pltpu.PrefetchScalarGridSpec(num_scalar_prefetch=1, grid=(number,), in_specs=[pl.BlockSpec((parts, None, 3, count, lanes), lambda i, _: (0, i, 0, 0, 0))], out_specs=[pl.BlockSpec((parts, None, count, lanes), lambda i, _: (0, i, 0, 0)), pl.BlockSpec((None, 8, seq_len), lambda i, _: (i, 0, 0))]), out_shape=[jax.ShapeDtypeStruct((parts, number, count, lanes), BF16), jax.ShapeDtypeStruct((number, 8, seq_len), F32)], compiler_params=params(), cost_estimate=cost(number * 8 * seq_len * seq_len * lanes, number * 2000000.0, number * 2 * seq_len * seq_len), name='attend')(starts, got)

def attend_back_kernel(first, starts, tcos, tsin, start_cos, start_sin, got, grad, att, lse, out, dq_ref, dk_ref, dv_ref):
    micro = first + pl.program_id(0)
    shards_n, _, count, lanes = got.shape
    seq_len = shards_n * count
    block = min(256, seq_len)
    q_all = (got[:, 0] * 0.125).reshape(seq_len, lanes)
    k_all = got[:, 1].reshape(seq_len, lanes)
    v_all = got[:, 2].reshape(seq_len, lanes)
    do_all = grad[...].reshape(seq_len, lanes)
    prod = do_all.astype(F32) * att[...].reshape(seq_len, lanes).astype(F32)
    prod = jnp.transpose(prod)
    deltas = [jnp.sum(prod[:HD], axis=0, keepdims=True), jnp.sum(prod[HD:], axis=0, keepdims=True)]
    begins = begin_of(lax.broadcasted_iota(jnp.int32, (1, seq_len), 1), starts, 4 * micro)
    for start in range(0, seq_len, block):
        end = start + block
        kb, vb = (k_all[start:end], v_all[start:end])
        qs, dos = (q_all[start:], do_all[start:])
        span = seq_len - start
        key = start + lax.broadcasted_iota(jnp.int32, (block, span), 0)
        query = start + lax.broadcasted_iota(jnp.int32, (block, span), 1)
        allowed = (key <= query) & (key >= begins[:, start:])
        dks, dvs, dqs = ([], [], [])
        for head in range(2):
            mask = head_mask(kb.shape, head)
            scores = dot_nt(jnp.where(mask, kb, 0), qs)
            soft = jnp.exp(jnp.where(allowed, scores, -1e+30) - lse[head:head + 1, start:])
            pull = dot_nt(jnp.where(mask, vb, 0), dos)
            ds = (soft * (pull - deltas[head][:, start:])).astype(BF16)
            dvs.append(dot(soft.astype(BF16), dos))
            dks.append(dot(ds, qs))
            dqs.append(lax.dot_general(ds, kb, (((0,), (0,)), ((), ())), preferred_element_type=F32))
        low = head_mask(kb.shape, 0)
        dk_ref[start:end] = jnp.where(low, dks[0], dks[1])
        dv_ref[start:end] = jnp.where(low, dvs[0], dvs[1])
        dq = jnp.where(head_mask(dqs[0].shape, 0), dqs[0], dqs[1])
        if start == 0:
            dq_ref[...] = dq
        else:
            dq_ref[start:] += dq
    rows = lax.broadcasted_iota(jnp.int32, (seq_len, lanes), 0)
    cos, sin = angle_rows(rows, starts, 4 * micro, (tcos[...], tsin[...]), start_cos.at[micro], start_sin.at[micro])
    for kind, ref in enumerate((dq_ref, dk_ref, dv_ref)):
        u = ref[...]
        if kind == 0:
            u = u * 0.125
        if kind < 2:
            u = u * cos - swap_halves(u) * sin
        out[:, kind] = u.astype(BF16).reshape(shards_n, count, lanes)

def call_attend_back(first, starts, table, start_table, got, grads, att, lse):
    parts, number, _, count, lanes = got.shape
    seq_len = parts * count
    return pl.pallas_call(functools.partial(attend_back_kernel, first), grid_spec=pltpu.PrefetchScalarGridSpec(num_scalar_prefetch=1, grid=(number,), in_specs=[whole(a.shape) for a in (*table, *start_table)] + [pl.BlockSpec((parts, None, 3, count, lanes), lambda i, _: (0, i, 0, 0, 0)), pl.BlockSpec((parts, None, count, lanes), lambda i, _: (0, first + i, 0, 0)), pl.BlockSpec((parts, None, count, lanes), lambda i, _: (0, i, 0, 0)), pl.BlockSpec((None, 8, seq_len), lambda i, _: (i, 0, 0))], out_specs=pl.BlockSpec((parts, None, 3, count, lanes), lambda i, _: (0, i, 0, 0, 0)), scratch_shapes=[pltpu.VMEM((seq_len, lanes), F32)] * 3), out_shape=jax.ShapeDtypeStruct((parts, number, 3, count, lanes), BF16), compiler_params=params(), cost_estimate=cost(number * 20 * seq_len * seq_len * lanes, number * 4000000.0, number * 2 * seq_len * seq_len), name='attend_back')(starts, *table, *start_table, got, grads, att, lse)

def mix_block(mixes, q, k):
    return jnp.concatenate([mixes[q][0][k], mixes[q][1][k]], 0)

def add_into(ref, cols, first, value):

    @pl.when(first)
    def _():
        ref[:, cols] = value

    @pl.when(jnp.logical_not(first))
    def _():
        ref[:, cols] += value

def layer_kernel(pos, *refs):
    att = [refs[0].at[:, 0], refs[0].at[:, 1], refs[1].at[:, 0]]
    x, cot, gains, shifts = refs[2:6]
    ups = [refs[6 + 2 * q:8 + 2 * q] for q in range(4)]
    downs = [refs[14 + 2 * q:16 + 2 * q] for q in range(4)]
    mixes = [refs[22 + 2 * q:24 + 2 * q] for q in range(4)]
    outputs, att_all, act, slope, keep, send, xhat1, scale1, xhat2, scale2, sums = refs[30:41]
    normed, hidden, total = refs[41:44]
    nz = mixes[0][0].shape[0]
    count = refs[0].shape[2]
    part = downs[0][0].shape[2]
    step = pl.program_id(0)

    def hand_out(index, value):
        keep[index] = value[:, :2 * part]
        send[index] = value[:, 2 * part:]

    @pl.when(step == 0)
    def _():
        for k in range(nz):
            for dx in range(2):
                place = ring_place(pos, k, nz) * 2 + lax.bitwise_xor(pos[3], dx)
                for m in range(3):
                    at = (k * 2 + dx) * 128
                    att_all[m * count:(m + 1) * count, at:at + 128] = att[m][place]
        for q in range(4):
            acc = None
            for k in range(nz):
                term = dot(att_all[:, k * 256:(k + 1) * 256], mix_block(mixes, q, k))
                acc = term if acc is None else acc + term
            total[:, q * part:(q + 1) * part] = acc
        xhat, scale = row_stats(total[...])
        xhat1[...] = xhat
        scale1[...] = jnp.broadcast_to(scale, scale1.shape)
        value = load_columns(x, pos, part).astype(F32) + xhat * gains[1:2] + shifts[1:2]
        hidden[...] = value
        xhat, scale = row_stats(value)
        xhat2[...] = xhat
        scale2[...] = jnp.broadcast_to(scale, scale2.shape)
        value = (xhat * gains[2:3] + shifts[2:3]).astype(BF16)
        normed[...] = value
        hand_out(0, value)
    for dx in range(2):
        u = None
        for q in range(4):
            term = dot(normed[:, q * part:(q + 1) * part], ups[q][dx][...])
            u = term if u is None else u + term
        square = u * u
        t = jnp.tanh(GELU_A * (u * (1.0 + GELU_B * square)))
        half = 0.5 * (1.0 + t)
        act[0, dx] = (u * half).astype(BF16)
        bend = half + 0.5 * GELU_A * u * (1.0 - t * t) * (1.0 + 3.0 * GELU_B * square)
        slope[0, dx] = bend.astype(BF16)
    for q in range(4):
        term = dot(act[0, 0], downs[q][0][0]) + dot(act[0, 1], downs[q][1][0])
        add_into(total, slice(q * part, (q + 1) * part), step == 0, term)

    @pl.when(step == nz - 1)
    def _():
        xhat, scale = row_stats(total[...])
        value = hidden[...] + xhat * gains[3:4] + shifts[3:4]
        store_columns(outputs, value, pos, part)
        grad = load_columns(cot, pos, part).astype(F32)
        sums[0:1] = column_sum(grad * xhat)
        sums[1:2] = column_sum(grad)
        hand_out(1, row_pull(grad, xhat, scale, gains[3:4]).astype(BF16))

def layer_specs(units, part, rows, nz, order):

    def up_spec(dy, dx):

        def index(i, pos):
            place = lax.bitwise_xor(pos[0], dy) * 2 + lax.bitwise_xor(pos[3], dx)
            return (place, ring_place(pos, order(i), nz), 0, 0)
        return pl.BlockSpec((None, None, part, units), index)
    ups = [up_spec(dy, dx) for _ in range(2) for dy in range(2) for dx in range(2)]
    down = pl.BlockSpec((1, units, part), lambda i, pos: (order(i), 0, 0))
    mix = pl.BlockSpec((nz, rows, part), lambda i, pos: (0, units // rows, 0))
    return ups + [down] * 8 + [mix] * 8

def layer_weights(ups, mixes):
    mixes_flat = [p for pair in mixes for p in pair]
    return [ups[0]] * 4 + [ups[1]] * 4 + mixes_flat * 2

def call_layer(pos, att, x, cot, gains, shifts, ups, mixes):
    tokens, width = x.shape
    _, nz, part, units = ups[0].shape
    rows = mixes[0][0].shape[1] - units
    act = pl.BlockSpec((1, 2, tokens, units), lambda i, pos: (i, 0, 0, 0))
    flat, column = ((tokens, width), (tokens, 128))
    side = (2, tokens, width // 2)
    ffn = jax.ShapeDtypeStruct((nz, 2, tokens, units), BF16)
    low = jax.ShapeDtypeStruct(flat, BF16)
    return pl.pallas_call(layer_kernel, grid_spec=pltpu.PrefetchScalarGridSpec(num_scalar_prefetch=1, grid=(nz,), in_specs=[whole(a.shape) for a in (*att, x, cot, gains, shifts)] + layer_specs(units, part, rows, nz, lambda i: i), out_specs=[whole(flat)] * 2 + [act] * 2 + [whole(side)] * 2 + [whole(flat), whole(column)] * 2 + [whole((8, width))], scratch_shapes=[pltpu.VMEM(flat, BF16), pltpu.VMEM(flat, F32), pltpu.VMEM(flat, F32)]), out_shape=[low, low, ffn, ffn] + [jax.ShapeDtypeStruct(side, BF16)] * 2 + [jax.ShapeDtypeStruct(flat, F32), jax.ShapeDtypeStruct(column, F32)] * 2 + [jax.ShapeDtypeStruct((8, width), F32)], compiler_params=params(), cost_estimate=cost(2 * tokens * width * (2 * nz * 2 * units + width), 40000000.0, tokens * nz * 2 * units), name='layer')(pos, *att, x, cot, gains, shifts, *layer_weights(ups, mixes))

def layer_back_kernel(pos, *refs):
    cot, gains, xhat1, scale1, xhat2, scale2, slope, keep, send = refs[0:9]
    ups = [refs[9 + 2 * q:11 + 2 * q] for q in range(4)]
    downs = [refs[17 + 2 * q:19 + 2 * q] for q in range(4)]
    mixes = [refs[25 + 2 * q:27 + 2 * q] for q in range(4)]
    g_up, keep_out, send_out, g_hidden, g_att, sums, total = refs[33:40]
    nz = mixes[0][0].shape[0]
    count = g_att.shape[2]
    part = downs[0][0].shape[2]
    step = pl.program_id(0)
    g_b2 = [keep[1, :, :part], keep[1, :, part:], send[1, :, :part], send[1, :, part:]]
    for dx in range(2):
        g = None
        for q in range(4):
            term = dot_nt(g_b2[q], downs[q][dx][0])
            g = term if g is None else g + term
        g_up[0, dx] = (g * slope[0, dx].astype(F32)).astype(BF16)
    for q in range(4):
        term = dot_nt(g_up[0, 0], ups[q][0][...]) + dot_nt(g_up[0, 1], ups[q][1][...])
        add_into(total, slice(q * part, (q + 1) * part), step == 0, term)

    @pl.when(step == nz - 1)
    def _():
        grad = total[...]
        xhat = xhat2[...]
        sums[1:2] = column_sum(grad * xhat)
        sums[3:4] = column_sum(grad)
        grad = load_columns(cot, pos, part).astype(F32) + row_pull(grad, xhat, scale2[:, 0:1], gains[2:3])
        g_hidden[...] = grad
        xhat = xhat1[...]
        sums[0:1] = column_sum(grad * xhat)
        sums[2:3] = column_sum(grad)
        g_b1 = row_pull(grad, xhat, scale1[:, 0:1], gains[1:2]).astype(BF16)
        keep_out[...] = g_b1[:, :2 * part]
        send_out[...] = g_b1[:, 2 * part:]
        for k in range(nz):
            acc = None
            for q in range(4):
                term = dot_nt(g_b1[:, q * part:(q + 1) * part], mix_block(mixes, q, k))
                acc = term if acc is None else acc + term
            acc = acc.astype(BF16)
            for dx in range(2):
                place = ring_place(pos, k, nz) * 2 + lax.bitwise_xor(pos[3], dx)
                for m in range(3):
                    g_att[place, m] = acc[m * count:(m + 1) * count, dx * 128:(dx + 1) * 128]

def call_layer_back(pos, cot, gains, kept, slope, keep, send, ups, mixes, count):
    tokens, width = cot.shape
    _, nz, part, units = ups[0].shape
    rows = mixes[0][0].shape[1] - units
    turn = nz - 1
    act = pl.BlockSpec((1, 2, tokens, units), lambda i, pos: (turn - i, 0, 0, 0))
    flat, half = ((tokens, width), (tokens, width // 2))
    heads = (2 * nz, tokens // count, count, rows)
    return pl.pallas_call(layer_back_kernel, grid_spec=pltpu.PrefetchScalarGridSpec(num_scalar_prefetch=1, grid=(nz,), in_specs=[whole(a.shape) for a in (cot, gains, *kept)] + [act, whole(keep.shape), whole(send.shape)] + layer_specs(units, part, rows, nz, lambda i: turn - i), out_specs=[act] + [whole(v) for v in (half, half, flat, heads, (8, width))], scratch_shapes=[pltpu.VMEM(flat, F32)]), out_shape=[jax.ShapeDtypeStruct(slope.shape, BF16), jax.ShapeDtypeStruct(half, BF16), jax.ShapeDtypeStruct(half, BF16), jax.ShapeDtypeStruct(flat, F32), jax.ShapeDtypeStruct(heads, BF16), jax.ShapeDtypeStruct((8, width), F32)], compiler_params=params(), cost_estimate=cost(2 * tokens * width * (2 * nz * 2 * units + width), 40000000.0), name='layer_back')(pos, cot, gains, *kept, slope, keep, send, *layer_weights(ups, mixes))

def place_piece(outs, dy, dx, cut, index, value):
    if dy == 0 and dx == 0:
        outs[0][index] = value
        return
    if cut is None:
        outs[2 * dy + dx][index] = value
        return
    low, high = outs[1 + 2 * (2 * dy + dx - 1):][:2]
    step = pl.program_id(0)

    @pl.when(step < cut)
    def _():
        low[index] = value

    @pl.when(step >= cut)
    def _():
        high[index] = value

def piece_specs(block, nz, cut):
    zeros = (0,) * (len(block) - 1)
    if cut is None:
        spec = pl.BlockSpec(block, lambda i, *_: (i,) + zeros)
        return ([spec] * 4, [jax.ShapeDtypeStruct((nz,) + block[1:], BF16)] * 4)
    low = pl.BlockSpec(block, lambda i, *_: (jnp.minimum(i, cut - 1),) + zeros)
    high = pl.BlockSpec(block, lambda i, *_: (jnp.maximum(i - cut, 0),) + zeros)
    specs = [pl.BlockSpec(block, lambda i, *_: (i,) + zeros)] + [low, high] * 3
    shapes = [nz] + [cut, nz - cut] * 3
    return (specs, [jax.ShapeDtypeStruct((n,) + block[1:], BF16) for n in shapes])

def down_grad_kernel(pos, act, act2, keep, recv, out):
    part = out.shape[3]
    for dx in range(2):
        side = jnp.concatenate([jnp.transpose(act[0, dx]), jnp.transpose(act2[0, dx])], 1)
        for dy in range(2):
            cols = slice(dy * part, (dy + 1) * part)
            grad = jnp.concatenate([keep[0, :, cols], recv[0, :, cols]], 0)
            place = lax.bitwise_xor(pos[0], dy) * 2 + lax.bitwise_xor(pos[3], dx)
            out[place, 0] = dot(side, grad).astype(BF16)

def call_down_grad(pos, act, act2, keep, recv):
    nz, _, tokens, units = act.shape
    half = keep.shape[2]
    part = half // 2
    ffn = pl.BlockSpec((1, 2, tokens, units), lambda i, pos: (i, 0, 0, 0))
    side = pl.BlockSpec((1, tokens, half), lambda i, pos: (1, 0, 0))
    return pl.pallas_call(down_grad_kernel, grid_spec=pltpu.PrefetchScalarGridSpec(num_scalar_prefetch=1, grid=(nz,), in_specs=[ffn, ffn, side, side], out_specs=pl.BlockSpec((4, 1, units, part), lambda i, pos: (0, ring_place(pos, i, nz), 0, 0))), out_shape=jax.ShapeDtypeStruct((4, nz, units, part), BF16), compiler_params=params(), cost_estimate=cost(2 * tokens * 2 * half * nz * 2 * units, 16000000.0), name='down_grad')(pos, act, act2, keep, recv)

def up_grad_kernel(cut, g_up, g_up2, keep, recv, keep1, recv1, att, att2, *refs):
    outs, flipped = (refs[:-1], refs[-1])
    part, units = (g_up.shape[3] // 2, g_up.shape[3])
    tokens = g_up.shape[2]

    @pl.when(pl.program_id(0) == 0)
    def _():
        flipped[:, :tokens] = jnp.transpose(keep[0])
        flipped[:, tokens:] = jnp.transpose(recv[0])
    side = jnp.concatenate([jnp.transpose(att[...]), jnp.transpose(att2[...])], 1)
    for dy in range(2):
        cols = slice(dy * part, (dy + 1) * part)
        both = dot(side, jnp.concatenate([keep1[:, cols], recv1[:, cols]], 0)).astype(BF16)
        for dx in range(2):
            grad = jnp.concatenate([g_up[0, dx], g_up2[0, dx]], 0)
            value = dot(flipped[cols], grad).astype(BF16)
            rows = both[dx * 128:(dx + 1) * 128]
            rows = jnp.concatenate([rows[:64], rows[64:]], 1)
            place_piece(outs, dy, dx, cut, 0, jnp.concatenate([value, rows], 0))

def call_up_grad(cut, g_up, g_up2, keep, recv, keep1, recv1, att, att2):
    nz, _, tokens, units = g_up.shape
    half = keep.shape[2]
    part = half // 2
    heads = att.shape[1] // nz
    ffn = pl.BlockSpec((1, 2, tokens, units), lambda i: (i, 0, 0, 0))
    side = pl.BlockSpec((1, tokens, half), lambda i: (0, 0, 0))
    head = pl.BlockSpec((tokens, heads), lambda i: (0, i))
    specs, shapes = piece_specs((1, part + heads // 4, units), nz, cut)
    return pl.pallas_call(functools.partial(up_grad_kernel, cut), grid=(nz,), in_specs=[ffn, ffn, side, side, whole(keep1.shape), whole(keep1.shape), head, head], out_specs=specs, out_shape=shapes, scratch_shapes=[pltpu.VMEM((half, 2 * tokens), BF16)], compiler_params=params(), cost_estimate=cost(2 * tokens * 2 * half * nz * 2 * units, 16000000.0), name='up_grad')(g_up, g_up2, keep, recv, keep1, recv1, att, att2)

def load_grads(pos, grads):
    columns = []
    for dx in range(2):
        place = lax.bitwise_xor(pos[3], dx)
        for kind in range(3):
            rows = [g[0, place, m, kind] for g in grads for m in range(g.shape[2])]
            columns.append(jnp.concatenate(rows, 0))
    return jnp.concatenate(columns, 1)

def qkv_grad_kernel(cut, pos, *refs):
    grads, keep, recv = (refs[0:4], refs[4], refs[5])
    outs, flipped = (refs[6:-1], refs[-1])
    part = outs[0].shape[2]
    tokens = keep.shape[0]

    @pl.when(pl.program_id(0) == 0)
    def _():
        flipped[:, :tokens] = jnp.transpose(keep[...])
        flipped[:, tokens:] = jnp.transpose(recv[...])
    block = load_grads(pos, grads)
    for dy in range(2):
        res = dot(flipped[dy * part:(dy + 1) * part], block).astype(BF16)
        for dx in range(2):
            for kind in range(3):
                at = (dx * 3 + kind) * 128
                place_piece(outs, dy, dx, cut, (0, kind), res[:, at:at + 128])

def call_qkv_grad(cut, pos, grads, grads2, keep, recv):
    nz, _, _, _, count, cols = grads[0].shape
    tokens, half = keep.shape
    part = half // 2
    grad_specs = [pl.BlockSpec((1,) + g.shape[1:], head_index(nz)) for g in grads]
    specs, shapes = piece_specs((1, 3, part, cols), nz, cut)
    return pl.pallas_call(functools.partial(qkv_grad_kernel, cut), grid_spec=pltpu.PrefetchScalarGridSpec(num_scalar_prefetch=1, grid=(nz,), in_specs=grad_specs * 2 + [whole(keep.shape)] * 2, out_specs=specs, scratch_shapes=[pltpu.VMEM((half, 2 * tokens), BF16)]), out_shape=shapes, compiler_params=params(), cost_estimate=cost(2 * tokens * 2 * half * 3 * nz * 2 * cols, 12000000.0), name='qkv_grad')(pos, *grads, *grads2, keep, recv)

def input_grad_kernel(pos, *refs):
    grads, x, gains, g_hidden = (refs[0:2], refs[2], refs[3], refs[4])
    weights = [refs[5 + 2 * q:7 + 2 * q] for q in range(4)]
    out, sums, total = refs[13:16]
    part = weights[0][0].shape[2]
    step = pl.program_id(0)
    block = load_grads(pos, grads)
    for q in range(4):
        side = jnp.concatenate([weights[q][dx][0, kind] for dx in range(2) for kind in range(3)], 1)
        term = dot_nt(block, side)

        @pl.when(step == 0)
        def _():
            total[:, q * part:(q + 1) * part] = term

        @pl.when(step > 0)
        def _():
            total[:, q * part:(q + 1) * part] += term

    @pl.when(step == pl.num_programs(0) - 1)
    def _():
        grad = total[...]
        xhat, scale = row_stats(load_columns(x, pos, part).astype(F32))
        sums[0:1] = column_sum(grad * xhat)
        sums[1:2] = column_sum(grad)
        value = g_hidden[...] + row_pull(grad, xhat, scale, gains[0:1])
        store_columns(out, value, pos, part)

def call_input_grad(pos, grads, x, gains, g_hidden, pieces):
    nz, _, _, _, count, cols = grads[0].shape
    tokens, width = x.shape
    part = width // 4
    grad_specs = [pl.BlockSpec((1,) + g.shape[1:], head_index(nz)) for g in grads]
    piece = pl.BlockSpec((1, 3, part, cols), lambda i, pos: (i, 0, 0, 0))
    return pl.pallas_call(input_grad_kernel, grid_spec=pltpu.PrefetchScalarGridSpec(num_scalar_prefetch=1, grid=(nz,), in_specs=grad_specs + [whole(a.shape) for a in (x, gains, g_hidden)] + [piece] * 8, out_specs=[whole((tokens, width)), whole((8, width))], scratch_shapes=[pltpu.VMEM((tokens, width), F32)]), out_shape=[jax.ShapeDtypeStruct((tokens, width), F32), jax.ShapeDtypeStruct((8, width), F32)], compiler_params=params(), cost_estimate=cost(2 * tokens * width * 3 * nz * 2 * cols, 16000000.0), name='input_grad')(pos, *grads, x, gains, g_hidden, *[p for pair in pieces for p in pair])

def sum_kernel(*refs):
    total = refs[0][...].astype(F32)
    for ref in refs[1:-1]:
        total = total + ref[...].astype(F32)
    refs[-1][...] = total.astype(BF16)

def add(*values):
    shape = values[0].shape
    block = pl.BlockSpec((1,) + shape[1:], lambda i: (i,) + (0,) * (len(shape) - 1))
    return pl.pallas_call(sum_kernel, grid=(shape[0],), in_specs=[block] * len(values), out_specs=block, out_shape=jax.ShapeDtypeStruct(shape, BF16), compiler_params=params(), cost_estimate=cost(values[0].size * len(values), 2 * values[0].size * (len(values) + 1)), name='add')(*values)

def sum_cut_kernel(cut, pos, mine, low_x, high_x, low_y, high_y, out):
    step = pl.program_id(0)

    @pl.when(step < cut)
    def _():
        total = mine[...].astype(F32) + low_x[...].astype(F32) + low_y[...].astype(F32)
        out[...] = total.astype(BF16)

    @pl.when(step >= cut)
    def _():
        total = mine[...].astype(F32) + high_x[...].astype(F32) + high_y[...].astype(F32)
        out[...] = total.astype(BF16)

def sum_ring_kernel(pos, *refs):
    sum_kernel(*refs)

def send_direct(parts):
    corner = lax.ppermute(parts[3], ('y', 'x'), [(i, 3 - i) for i in range(4)])
    return (corner, swap(parts[1], 'x'), swap(parts[2], 'y'))

def add_direct(pos, values):
    shape = values[0].shape
    nz = shape[0]
    block = (1,) + shape[1:]
    zeros = (0,) * (len(block) - 1)
    return pl.pallas_call(sum_ring_kernel, grid_spec=pltpu.PrefetchScalarGridSpec(num_scalar_prefetch=1, grid=(nz,), in_specs=[pl.BlockSpec(block, lambda i, pos: (i,) + zeros)] * len(values), out_specs=pl.BlockSpec(block, lambda i, pos: (ring_place(pos, i, nz),) + zeros)), out_shape=jax.ShapeDtypeStruct(shape, BF16), compiler_params=params(), cost_estimate=cost(values[0].size * 4, 10 * values[0].size), name='add_direct')(pos, *values)

def add_sides(cut, pos, mine, sides, ordered=True):
    nz = mine.shape[0]
    block = (1,) + mine.shape[1:]
    specs, _ = piece_specs(block, nz, cut)
    zeros = (0,) * (len(block) - 1)
    return pl.pallas_call(functools.partial(sum_cut_kernel, cut), grid_spec=pltpu.PrefetchScalarGridSpec(num_scalar_prefetch=1, grid=(nz,), in_specs=specs[:5], out_specs=pl.BlockSpec(block, lambda i, pos: (ring_place(pos, i, nz) if ordered else i,) + zeros)), out_shape=jax.ShapeDtypeStruct(mine.shape, BF16), compiler_params=params(), cost_estimate=cost(mine.size * 2, 8 * mine.size), name='add_sides')(pos, mine, *sides)

def after(values, *others):
    return lax.optimization_barrier((values, others))[0]

def swap(values, axis):
    return lax.ppermute(values, axis, SWAP)

def ring(values, step, size):
    return lax.ppermute(values, 'z', [(i, (i + step) % size) for i in range(size)])

def gather_sides(mine):
    return (swap(mine, 'x'), swap(mine, 'y'))

def gather_corner(over_x, over_y, cut):
    return jnp.concatenate([swap(over_x[:cut], 'y'), swap(over_y[cut:], 'x')])

def pair_up(mine, over_x, over_y, corner):
    return [[mine, over_x], [over_y, corner]]

def send_corner(parts):
    return (swap(parts[5], 'y'), swap(parts[6], 'x'))

def add_pair_kernel(a, b, c, d, first, second):
    first[...] = (a[...].astype(F32) + b[...].astype(F32)).astype(BF16)
    second[...] = (c[...].astype(F32) + d[...].astype(F32)).astype(BF16)

def corner_sums(parts, corner):
    if parts[1].shape != parts[4].shape:
        return (add(parts[1], corner[0]), add(parts[4], corner[1]))
    shape = parts[1].shape
    block = pl.BlockSpec((1,) + shape[1:], lambda i: (i,) + (0,) * (len(shape) - 1))
    return pl.pallas_call(add_pair_kernel, grid=(shape[0],), in_specs=[block] * 4, out_specs=[block] * 2, out_shape=[jax.ShapeDtypeStruct(shape, BF16)] * 2, compiler_params=params(), cost_estimate=cost(parts[1].size * 4, parts[1].size * 12), name='add_pair')(parts[1], corner[0], parts[4], corner[1])

def send_sides(parts, sums):
    high_x, low_y = after((parts[2], parts[3]), sums)
    return (swap(sums[0], 'x'), swap(high_x, 'x'), swap(low_y, 'y'), swap(sums[1], 'y'))

def plane_norms(sums, part):
    pieces = [sums[:, q * part:(q + 1) * part] for q in range(4)]
    low, high = (pieces[dy] + swap(pieces[2 + dy], 'c') for dy in range(2))
    mine = low + swap(high, 'y')
    return mine + swap(mine, 'x')

def line_norms(mine):
    mine = mine + lax.ppermute(mine, 'z', [(i, i ^ 1) for i in range(4)])
    return mine + lax.ppermute(mine, 'z', [(i, i ^ 2) for i in range(4)])

def fast_shards(inputs, doc_starts, w_qkv, w_out, w_up, w_down, norm_gains, norm_biases, cotangent):
    pos = jnp.stack([lax.axis_index(name) for name in ('y', 'c', 'z', 'x')]).astype(jnp.int32)
    nz = lax.axis_size('z')
    parts = nz * 2
    micro, _, shard_len, width = inputs.shape
    tokens = micro * shard_len
    seq_len = shard_len * parts
    part = width // 4
    cols = w_qkv.shape[2]
    half = nz // 2
    starts = doc_starts.reshape(-1)
    x = inputs.reshape(tokens, width)
    cot = cotangent.reshape(tokens, width)

    def exchange(values):
        return lax.all_to_all(values, SEQ, 0, 0, tiled=True)
    rings = [ring(w_qkv, nz - k, nz) for k in range(1, nz)]
    norms = jnp.concatenate([norm_gains, norm_biases])
    norms_y, norms_c = (swap(norms, 'y'), swap(norms, 'c'))
    norms = jnp.concatenate([norms, norms_y, norms_c, swap(norms_y, 'c')], 1).astype(F32)
    gains, shifts = (norms[:4], norms[4:])
    start_table = start_tables(doc_starts[:, 0])
    table = tables(seq_len)
    mix = jnp.concatenate([w_down, w_out])
    qkv_mine, mix = after((jnp.stack([w_qkv] + rings), mix), norms, start_table)
    mix1, mix3 = (ring(after(mix, qkv_mine), k, nz) for k in (nz - 1, 1))
    qkv_sides = after(gather_sides(qkv_mine), mix1, mix3)
    mix2 = ring(after(mix, qkv_sides), nz - 2, nz)
    qkv_corner = gather_corner(*qkv_sides, half)
    qkv_other = [swap(p, 'c') for p in (qkv_mine, *qkv_sides)]
    qkv_corner = after(qkv_corner, qkv_other)
    up_mine = lax.all_gather(after(w_up, qkv_corner), 'z', axis=0, tiled=False)
    mix_mine = jnp.stack([mix, mix1, mix2, mix3])
    qkv_other.append(swap(qkv_corner, 'c'))
    qkv = pair_up(qkv_mine, *qkv_sides, qkv_corner) + pair_up(*qkv_other)
    first, last, keep0, send1 = call_proj(pos, starts, x, gains, shifts, table, start_table, qkv, shard_len)
    mix_mine = after(mix_mine, first)
    mix_sides = gather_sides(mix_mine)
    got = [None, None]
    got[0] = exchange(first.reshape(parts, 2, 3, shard_len, cols))
    got[1] = exchange(after(last.reshape(parts, 1, 3, shard_len, cols), got[0]))
    mix_corner = gather_corner(*mix_sides, 2)
    mix_other = [swap(p, 'c') for p in (mix_mine, *mix_sides)]
    att_local, lses, att = ([None, None], [None, None], [None, None])
    got[0] = after(got[0], mix_other, mix_corner)
    up_own = lax.all_gather(after(up_mine, got[0]), ('y', 'x'), axis=0, tiled=False)
    mix_other.append(swap(mix_corner, 'c'))
    att_local[0], lses[0] = call_attend(0, starts, got[0])
    got[1] = after(got[1], att_local[0], mix_corner)
    att[0] = exchange(att_local[0])
    att_local[1], lses[1] = call_attend(2, starts, got[1])
    att[0] = after(att[0], att_local[1], mix_other)
    att[1] = exchange(after(att_local[1], att[0]))
    mixes = pair_up(mix_mine, *mix_sides, mix_corner) + pair_up(*mix_other)
    up_own = after(up_own, att[1])
    ups = [up_own, swap(up_own, 'c')]
    res = call_layer(pos, att, x, cot, gains, shifts, ups, mixes)
    outputs, att_all, act, slope, keep, send = res[:6]
    kept, sums3 = (res[6:10], res[10])
    recv, act2, att_all2, recv0 = (swap(v, 'c') for v in (send, act, att_all, send1))
    res = call_layer_back(pos, cot, gains, kept, slope, keep, send, ups, mixes, shard_len)
    g_up, keep1, send1, g_hidden, g_att, sums = res
    back, back2 = ([None, None], [None, None])
    recv1, g_up2 = (swap(send1, 'c'), swap(g_up, 'c'))
    act2 = after(act2, g_up)
    down_parts = call_down_grad(pos, act, act2, keep, recv)
    down_sum = lax.psum_scatter(down_parts, ('y', 'x'), scatter_dimension=0, tiled=True)
    down_sum = down_sum.reshape(down_parts.shape[1:])
    g_up = after(g_up, down_parts)
    grad = exchange(g_att)
    grad = after(grad, down_parts)
    res2 = call_attend_back(2, starts, table, start_table, got[1], grad, att_local[1], lses[1])
    back[1] = exchange(res2)
    grad = after(grad, res2)
    res = call_attend_back(0, starts, table, start_table, got[0], grad, att_local[0], lses[0])
    up_parts = call_up_grad(None, after(g_up, res), g_up2, keep, recv, keep1, recv1, att_all, att_all2)
    up_sent = send_direct(up_parts)
    back[1] = after(back[1], res)
    back[0] = exchange(after(res, back[1]))
    back2[1] = swap(back[1].reshape((nz, 2) + back[1].shape[1:]), 'c')
    back[0] = after(back[0], down_sum)
    down_sum = lax.psum_scatter(down_sum, 'z', scatter_dimension=0, tiled=False)
    back[0] = after(back[0], back2[1], up_parts)
    back[0] = after(back[0], up_sent[1], up_sent[2])
    back = [b.reshape((nz, 2) + b.shape[1:]) for b in back]
    back2[0] = swap(back[0], 'c')
    qkv_cut = half
    qkv_parts = call_qkv_grad(qkv_cut, pos, back, back2, keep0, recv0)
    back = after(back, qkv_parts)
    up_sent = after(up_sent, qkv_parts)
    qkv_corner = send_corner(qkv_parts)
    qkv_sums = corner_sums(qkv_parts, qkv_corner)
    qkv_sent = send_sides(qkv_parts, qkv_sums)
    inputs_grad, sums0 = call_input_grad(pos, after(back, qkv_sums), x, gains, g_hidden, qkv)
    up_sum = add_direct(pos, (up_parts[0], *up_sent))
    qkv_sent = after(qkv_sent, up_sum)
    up_sum = lax.psum_scatter(up_sum, 'z', scatter_dimension=0, tiled=False)
    norm_sums = [sums0[:1], sums[:2], sums3[:1], sums0[1:2], sums[2:4], sums3[1:2]]
    norm_sums = jnp.concatenate(norm_sums)
    qkv_sent, norm_sums = after((qkv_sent, norm_sums), norm_sums, down_sum)
    qkv_sum = add_sides(half, pos, qkv_parts[0], qkv_sent, True)
    norm_sums = line_norms(plane_norms(after(norm_sums, qkv_sum), part))
    qkv_sum = lax.psum_scatter(qkv_sum, 'z', scatter_dimension=0, tiled=False)
    down_sum = down_sum.astype(F32)
    up_sum, out_sum = (up_sum[:part].astype(F32), up_sum[part:].astype(F32))
    out_sum = jnp.concatenate([out_sum[:, :part], out_sum[:, part:]], 0)
    qkv_sum = after(qkv_sum, norm_sums, down_sum, out_sum, up_sum)
    return (outputs.reshape(inputs.shape), inputs_grad.reshape(inputs.shape), qkv_sum.astype(F32), out_sum, up_sum, down_sum, norm_sums[:4], norm_sums[4:])

def fits_fast(mesh, inputs, w_qkv, w_up):
    dp, tensor = (mesh.shape['dp'], mesh.shape['tensor'])
    return dp == 4 and tensor == 8 and (inputs.shape[0] == 3) and (inputs.shape[1] == dp) and (inputs.shape[2] == 1024) and (w_qkv.shape[1:] == (1024, 1024)) and (w_up.shape[1] == 4096)

def solution(mesh):
    dp, tensor = (mesh.shape['dp'], mesh.shape['tensor'])
    names = ('y', 'c', 'z', 'x')
    fine = Mesh(mesh.devices.reshape(dp // 2, 2, 4, tensor // 4), names)
    rows, seq = (('y', 'c'), ('z', 'x'))
    tokens = P(None, rows, seq, None)
    weights = (P(None, rows, seq), P(seq, rows), P(rows, seq), P(seq, rows))
    norm = P(None, rows)

    def run(*arrays):
        fast = fits_fast(mesh, arrays[0], arrays[2], arrays[4])
        return jax.shard_map(fast_shards if fast else shards, mesh=fine, in_specs=(tokens, P(None, rows, None)) + weights + (norm, norm, tokens), out_specs=(tokens, tokens) + weights + (norm, norm), check_vma=False)(*arrays)
    return run
```

```python
import functools
import math
import jax
import jax.numpy as jnp
import numpy as np
from jax import lax
from jax.experimental import pallas as pl
from jax.experimental.pallas import tpu as pltpu
from jax.sharding import Mesh, PartitionSpec as P
HD = 64
EPSILON = 1e-05
F32 = jnp.float32
BF16 = jnp.bfloat16
CHIPS = ('y', 'z', 'x')
SEQ = ('z', 'x')
SWAP = [(0, 1), (1, 0)]

def ln_forward(values, gain, shift):
    average = jnp.mean(values, axis=-1, keepdims=True)
    centred = values - average
    variance = jnp.mean(centred * centred, axis=-1, keepdims=True)
    scale = lax.rsqrt(variance + EPSILON)
    xhat = centred * scale
    return (xhat * gain + shift, xhat, scale)

def ln_backward(grad, xhat, scale, gain):
    e = grad * gain
    dv = scale * (e - jnp.mean(e, axis=-1, keepdims=True) - xhat * jnp.mean(e * xhat, axis=-1, keepdims=True))
    return (dv, jnp.sum(grad * xhat, axis=0), jnp.sum(grad, axis=0))

def rotate(values, cosines, sines):
    half_dim = values.shape[-1] // 2
    lower = values[..., :half_dim]
    upper = values[..., half_dim:]
    return jnp.concatenate([lower * cosines - upper * sines, upper * cosines + lower * sines], axis=-1)

def doc_layout(starts, token_index):
    inside = token_index[:, None] >= starts[None, :]
    segment = jnp.sum(inside.astype(jnp.int32), axis=1)
    begins = jnp.max(jnp.where(inside, starts[None, :], 0), axis=1)
    return (segment, token_index - begins)

def angles_of(position):
    frequency = jnp.exp(jnp.arange(HD // 2, dtype=F32) * (-2.0 * math.log(10000.0) / HD))
    angles = position.astype(F32)[..., None] * frequency
    return (jnp.cos(angles), jnp.sin(angles))

def block_mask(segment, offset, block_len, key_len):
    query_pos = jnp.arange(offset, offset + block_len, dtype=jnp.int32)
    key_pos = jnp.arange(key_len, dtype=jnp.int32)
    causal = key_pos[None, :] <= query_pos[:, None]
    return causal & (segment[offset:offset + block_len, None] == segment[None, :key_len])

def attention_forward(q, k, v, segment):
    seq_len = q.shape[1]
    block_len = min(512, seq_len)
    pieces, lses = ([], [])
    for offset in range(0, seq_len, block_len):
        end = offset + block_len
        allowed = block_mask(segment, offset, block_len, end)[None]
        scores = 0.125 * jnp.einsum('hqe,hke->hqk', q[:, offset:end], k[:, :end], preferred_element_type=F32)
        scores = jnp.where(allowed, scores, -1e+30)
        peak = jnp.max(scores, axis=-1, keepdims=True)
        lse = peak + jnp.log(jnp.sum(jnp.exp(scores - peak), axis=-1, keepdims=True))
        probs = jnp.exp(scores - lse).astype(BF16)
        pieces.append(jnp.einsum('hqk,hke->hqe', probs, v[:, :end], preferred_element_type=F32).astype(BF16))
        lses.append(lse)
    return (jnp.concatenate(pieces, axis=1), lses)

def attention_backward(q, k, v, do, lses, segment):
    seq_len = q.shape[1]
    block_len = min(512, seq_len)
    dq = []
    dk = jnp.zeros(k.shape, F32)
    dv = jnp.zeros(v.shape, F32)
    for index, offset in enumerate(range(0, seq_len, block_len)):
        end = offset + block_len
        allowed = block_mask(segment, offset, block_len, end)[None]
        qb, kb, vb, dob = (q[:, offset:end], k[:, :end], v[:, :end], do[:, offset:end])
        scores = 0.125 * jnp.einsum('hqe,hke->hqk', qb, kb, preferred_element_type=F32)
        scores = jnp.where(allowed, scores, -1e+30)
        soft = jnp.exp(scores - lses[index])
        probs = soft.astype(BF16)
        dp = jnp.einsum('hqe,hke->hqk', dob, vb, preferred_element_type=F32)
        dot = jnp.sum(soft * dp, axis=-1, keepdims=True)
        ds = (soft * (dp - dot)).astype(BF16)
        dq.append(0.125 * jnp.einsum('hqk,hke->hqe', ds, kb, preferred_element_type=F32))
        pad = ((0, 0), (0, seq_len - end), (0, 0))
        dk = dk + jnp.pad(0.125 * jnp.einsum('hqk,hqe->hke', ds, qb, preferred_element_type=F32), pad)
        dv = dv + jnp.pad(jnp.einsum('hqk,hqe->hke', probs, dob, preferred_element_type=F32), pad)
    return (jnp.concatenate(dq, axis=1), dk, dv)

def gather_both(shard):
    mine = lax.all_gather(shard, CHIPS, axis=0, tiled=False)
    return jnp.stack([mine, lax.ppermute(mine, 'c', SWAP)])

def scatter_both(partial, sizes):
    ny, nz, nx = sizes
    shard_shape = partial.shape[2:]
    low = partial.astype(BF16)
    got = lax.ppermute(low[1], 'c', SWAP)
    mine = (low[0].astype(F32) + got.astype(F32)).astype(BF16)
    mine = mine.reshape((ny, nz, nx) + shard_shape)
    mine = mine.transpose((0, 2, 1) + tuple(range(3, mine.ndim)))
    mine = mine.reshape((ny * nx, nz) + shard_shape)
    mine = lax.psum_scatter(mine, ('y', 'x'), scatter_dimension=0, tiled=False)
    return lax.psum_scatter(mine, 'z', scatter_dimension=0, tiled=False).astype(F32)

def shards(inputs, doc_starts, w_qkv, w_out, w_up, w_down, norm_gains, norm_biases, cotangent):
    ny, nz, nx = (lax.axis_size(name) for name in CHIPS)
    core = lax.axis_index('c')
    sizes = (ny, nz, nx)
    parts = nz * nx
    micro, _, shard_len, width = inputs.shape
    tokens = micro * shard_len
    seq_len = shard_len * parts
    dpart = width // (2 * ny)
    hcols = w_out.shape[0]
    heads = hcols // HD
    units = w_up.shape[1]

    def to_own(values):
        pieces = values.reshape(values.shape[:-1] + (ny, 2, dpart))
        pieces = jnp.where(core == 0, pieces, pieces[..., ::-1, :])
        return jnp.swapaxes(pieces, -3, -2).reshape(values.shape)

    def from_own(values):
        pieces = jnp.swapaxes(values.reshape(values.shape[:-1] + (2, ny, dpart)), -3, -2)
        return jnp.where(core == 0, pieces, pieces[..., ::-1, :]).reshape(values.shape)
    qkv_all = gather_both(w_qkv).reshape(2, ny, parts, 3, dpart, hcols)
    norms = jnp.stack([norm_gains, norm_biases])
    norms = gather_dp(norms, ny, dpart)
    norms = to_own(norms.astype(F32))
    gains, shifts = (norms[0], norms[1])
    out_all = gather_both(w_out).reshape(2, ny, parts, hcols, dpart)
    up_all = gather_both(w_up).reshape(2, ny, parts, dpart, units)
    down_all = gather_both(w_down).reshape(2, ny, parts, units, dpart)
    qkv_full = qkv_all.transpose(0, 1, 4, 3, 2, 5).reshape(width, 3 * parts * hcols)
    out_full = out_all.transpose(2, 3, 0, 1, 4).reshape(parts * hcols, width)
    up_full = up_all.transpose(0, 1, 3, 2, 4).reshape(width, parts * units)
    down_full = down_all.transpose(2, 3, 0, 1, 4).reshape(parts * units, width)
    x = to_own(inputs.reshape(tokens, width)).astype(F32)
    cot = to_own(cotangent.reshape(tokens, width)).astype(F32)
    place = lax.axis_index(SEQ) * shard_len + jnp.arange(shard_len, dtype=jnp.int32)
    cos_own, sin_own, cos_row, sin_row, segments = ([], [], [], [], [])
    for index in range(micro):
        starts = doc_starts[index, 0]
        c, s = angles_of(doc_layout(starts, place)[1])
        cos_own.append(c)
        sin_own.append(s)
        segment, position = doc_layout(starts, jnp.arange(seq_len, dtype=jnp.int32))
        c, s = angles_of(position)
        cos_row.append(c)
        sin_row.append(s)
        segments.append(segment)
    cos_own = jnp.concatenate(cos_own)[:, None, None]
    sin_own = jnp.concatenate(sin_own)[:, None, None]
    normed1, xhat0, scale0 = ln_forward(x, gains[0], shifts[0])
    normed1 = normed1.astype(BF16)
    projected = jnp.dot(normed1, qkv_full, preferred_element_type=F32)
    projected = projected.reshape(tokens, 3, parts * heads, HD)
    rotated = rotate(projected[:, :2], cos_own, sin_own)
    projected = jnp.concatenate([rotated, projected[:, 2:]], axis=1).astype(BF16)
    projected = projected.reshape(micro, shard_len, 3, parts, hcols).transpose(0, 3, 2, 1, 4)

    def to_heads(values):
        kinds = values.shape[1]
        got = lax.all_to_all(values, SEQ, 0, 0, tiled=True)
        got = got.reshape(parts, kinds, shard_len, heads, HD).transpose(1, 3, 0, 2, 4)
        return got.reshape(kinds, heads, seq_len, HD)

    def to_tokens(values):
        kinds = values.shape[0]
        sent = values.reshape(kinds, heads, parts, shard_len, HD).transpose(2, 0, 3, 1, 4)
        sent = sent.reshape(parts, kinds, shard_len, hcols)
        return lax.all_to_all(sent, SEQ, 0, 0, tiled=True)
    qkvs, lses, attended = ([], [], [])
    for index in range(micro):
        q, k, v = to_heads(projected[index])
        out, lse = attention_forward(q, k, v, segments[index])
        qkvs.append((q, k, v))
        lses.append(lse)
        attended.append(to_tokens(out[None])[:, 0])
    attended = jnp.stack(attended).transpose(0, 2, 1, 3).reshape(tokens, parts * hcols)
    branch1 = jnp.dot(attended, out_full, preferred_element_type=F32)
    post1, xhat1, scale1 = ln_forward(branch1, gains[1], shifts[1])
    hidden = x + post1
    normed2, xhat2, scale2 = ln_forward(hidden, gains[2], shifts[2])
    normed2 = normed2.astype(BF16)
    up_act = jnp.dot(normed2, up_full, preferred_element_type=F32)
    gated, gate_pull = jax.vjp(lambda u: jax.nn.gelu(u, approximate=True), up_act)
    activated = gated.astype(BF16)
    branch2 = jnp.dot(activated, down_full, preferred_element_type=F32)
    post2, xhat3, scale3 = ln_forward(branch2, gains[3], shifts[3])
    outputs = (hidden + post2).astype(BF16)
    grad_branch2, gain3, shift3 = ln_backward(cot, xhat3, scale3, gains[3])
    grad_branch2 = grad_branch2.astype(BF16)
    down_part = jnp.einsum('tf,td->fd', activated, grad_branch2, preferred_element_type=F32)
    down_part = down_part.astype(BF16).reshape(parts, units, 2, ny, dpart)
    down_grad = scatter_both(down_part.transpose(2, 3, 0, 1, 4).reshape(2, ny * parts, units, dpart), sizes)
    grad_act = jnp.einsum('td,fd->tf', grad_branch2, down_full, preferred_element_type=F32)
    grad_up = gate_pull(grad_act)[0].astype(BF16)
    up_part = jnp.einsum('td,tf->df', normed2, grad_up, preferred_element_type=F32)
    up_part = up_part.astype(BF16).reshape(2, ny, dpart, parts, units)
    up_grad = scatter_both(up_part.transpose(0, 1, 3, 2, 4).reshape(2, ny * parts, dpart, units), sizes)
    grad_normed2 = jnp.einsum('tf,df->td', grad_up, up_full, preferred_element_type=F32)
    extra, gain2, shift2 = ln_backward(grad_normed2, xhat2, scale2, gains[2])
    grad_hidden = cot + extra
    grad_branch1, gain1, shift1 = ln_backward(grad_hidden, xhat1, scale1, gains[1])
    grad_branch1 = grad_branch1.astype(BF16)
    grad_attended = jnp.einsum('td,fd->tf', grad_branch1, out_full, preferred_element_type=F32).astype(BF16)
    grad_attended = grad_attended.reshape(micro, shard_len, parts, 1, hcols)
    grad_attended = grad_attended.transpose(0, 2, 3, 1, 4)
    out_part = jnp.einsum('tf,td->fd', attended, grad_branch1, preferred_element_type=F32)
    out_part = out_part.astype(BF16).reshape(parts, hcols, 2, ny, dpart)
    out_grad = scatter_both(out_part.transpose(2, 3, 0, 1, 4).reshape(2, ny * parts, hcols, dpart), sizes)
    grad_projected = []
    for index in range(micro):
        do = to_heads(grad_attended[index])[0]
        q, k, v = qkvs[index]
        dq, dk, dv = attention_backward(q, k, v, do, lses[index], segments[index])
        cos, sin = (cos_row[index], -sin_row[index])
        back = jnp.stack([rotate(dq, cos, sin), rotate(dk, cos, sin), dv]).astype(BF16)
        grad_projected.append(to_tokens(back))
    grad_projected = jnp.stack(grad_projected).transpose(0, 3, 2, 1, 4)
    grad_projected = grad_projected.reshape(tokens, 3 * parts * hcols)
    qkv_part = jnp.einsum('td,te->de', normed1, grad_projected, preferred_element_type=F32)
    qkv_part = qkv_part.astype(BF16).reshape(2, ny, dpart, 3, parts, hcols)
    qkv_grad = scatter_both(qkv_part.transpose(0, 1, 4, 3, 2, 5).reshape(2, ny * parts, 3, dpart, hcols), sizes)
    grad_normed1 = jnp.einsum('te,de->td', grad_projected, qkv_full, preferred_element_type=F32)
    extra, gain0, shift0 = ln_backward(grad_normed1, xhat0, scale0, gains[0])
    inputs_grad = grad_hidden + extra
    sums = jnp.stack([gain0, gain1, gain2, gain3, shift0, shift1, shift2, shift3])
    sums = lax.psum(from_own(sums), ('y', 'c', 'z', 'x'))
    place = (lax.axis_index('y') * 2 + core) * dpart
    sums = lax.dynamic_slice_in_dim(sums, place, dpart, 1)
    return (from_own(outputs).reshape(inputs.shape), from_own(inputs_grad).reshape(inputs.shape), qkv_grad, out_grad, up_grad, down_grad, sums[:4], sums[4:])

def gather_dp(norms, ny, dpart):
    full = lax.all_gather(norms, ('y', 'c'), axis=2, tiled=True)
    return full
NT = (((1,), (1,)), ((), ()))
GELU_A = 0.7978845608
GELU_B = 0.044715
COST = 0.2

def dot(a, b):
    return jnp.dot(a, b, preferred_element_type=F32)

def dot_nt(a, b):
    return lax.dot_general(a, b, NT, preferred_element_type=F32)

def params(semantics=1):
    return pltpu.CompilerParams(dimension_semantics=('arbitrary',) * semantics, vmem_limit_bytes=60 * 1024 * 1024)

def cost(flops, size, transcendentals=0):
    return pl.CostEstimate(flops=int(flops * COST), bytes_accessed=int(size * COST), transcendentals=int(transcendentals * COST))

def whole(shape):
    return pl.BlockSpec(shape, lambda *_: (0,) * len(shape))

def swap_halves(values):
    lane = lax.broadcasted_iota(jnp.int32, values.shape, 1)
    low = lax.rem(lane, HD) < HD // 2
    return jnp.where(low, pltpu.roll(values, 96, 1), pltpu.roll(values, 32, 1))

def row_stats(values):
    average = jnp.mean(values, axis=-1, keepdims=True)
    centred = values - average
    variance = jnp.mean(centred * centred, axis=-1, keepdims=True)
    scale = lax.rsqrt(variance + EPSILON)
    return (centred * scale, scale)

def row_pull(grad, xhat, scale, gain):
    e = grad * gain
    return scale * (e - jnp.mean(e, axis=-1, keepdims=True) - xhat * jnp.mean(e * xhat, axis=-1, keepdims=True))

def column_sum(values):
    return jnp.sum(values, axis=0, keepdims=True)

def own_place(pos, q, part):
    place = lax.bitwise_xor(pos[0], q % 2) * 2 + lax.bitwise_xor(pos[1], q // 2)
    return pl.multiple_of(place * part, part)

def load_columns(ref, pos, part):
    return jnp.concatenate([ref[:, pl.ds(own_place(pos, q, part), part)] for q in range(4)], 1)

def store_columns(ref, values, pos, part):
    for q in range(4):
        ref[:, pl.ds(own_place(pos, q, part), part)] = values[:, q * part:(q + 1) * part].astype(ref.dtype)

def tables(seq_len):
    lane = np.arange(128)
    frequency = np.exp(lane % (HD // 2) * (-2.0 * math.log(10000.0) / HD))
    angle = np.arange(seq_len)[:, None] * frequency.astype(np.float32).astype(np.float64)
    sign = np.where(lane % HD < HD // 2, -1.0, 1.0)
    return (np.cos(angle).astype(np.float32), (np.sin(angle) * sign).astype(np.float32))

def start_tables(starts):
    lane = jnp.arange(128)
    frequency = jnp.exp((lane % (HD // 2)).astype(F32) * (-2.0 * math.log(10000.0) / HD))
    angle = starts.astype(F32)[..., None] * frequency
    return (jnp.cos(angle), jnp.sin(angle) * jnp.where(lane % HD < HD // 2, -1.0, 1.0))

def angle_rows(rows, starts, base, table, start_cos, start_sin):
    cb, sb = (start_cos[0:1], start_sin[0:1])
    for d in range(1, 4):
        inside = rows >= starts[base + d]
        cb = jnp.where(inside, start_cos[d:d + 1], cb)
        sb = jnp.where(inside, start_sin[d:d + 1], sb)
    tc, ts = table
    return (tc * cb + ts * sb, ts * cb - tc * sb)

def begin_of(rows, starts, base):
    begin = jnp.zeros(rows.shape, jnp.int32)
    for d in range(1, 4):
        begin = jnp.where(rows >= starts[base + d], starts[base + d], begin)
    return begin

def proj_kernel(pos, starts, x, gains, shifts, tcos, tsin, start_cos, start_sin, *refs):
    weights = [refs[2 * q:2 * q + 2] for q in range(4)]
    first, last, keep, send = refs[8:12]
    normed, cos, sin = refs[12:15]
    outs = [first.at[0, :, 0], first.at[0, :, 1], last.at[0, :, 0]]
    part = weights[0][0].shape[2]
    count = first.shape[4]

    @pl.when(pl.program_id(0) == 0)
    def _():
        xhat, _ = row_stats(load_columns(x, pos, part).astype(F32))
        value = (xhat * gains[0:1] + shifts[0:1]).astype(BF16)
        normed[...] = value
        keep[...] = value[:, :2 * part]
        send[...] = value[:, 2 * part:]
        rows = lax.broadcasted_iota(jnp.int32, (count, 128), 0) + (pos[2] * 2 + pos[3]) * count
        for m in range(3):
            at = slice(m * count, (m + 1) * count)
            cos[at], sin[at] = angle_rows(rows, starts, 4 * m, (tcos[...], tsin[...]), start_cos.at[m], start_sin.at[m])
    total = None
    for q in range(4):
        block = jnp.concatenate([weights[q][dx][0, kind] for dx in range(2) for kind in range(3)], 1)
        term = dot(normed[:, q * part:(q + 1) * part], block)
        total = term if total is None else total + term
    for dx in range(2):
        place = lax.bitwise_xor(pos[3], dx)
        for kind in range(3):
            at = (dx * 3 + kind) * 128
            u = total[:, at:at + 128]
            if kind < 2:
                u = u * cos[...] + swap_halves(u) * sin[...]
            u = u.astype(BF16)
            for m in range(3):
                outs[m][place, kind] = u[m * count:(m + 1) * count]

def ring_place(pos, i, nz):
    return lax.rem(pos[2] + i, nz)

def head_index(nz):
    return lambda i, pos, *_: (ring_place(pos, i, nz), 0, 0, 0, 0, 0)

def call_proj(pos, starts, x, gains, shifts, table, start_table, pieces, shard_len):
    tokens, width = x.shape
    nz, _, part, cols = pieces[0][0].shape
    piece = pl.BlockSpec((1, 3, part, cols), lambda i, *_: (i, 0, 0, 0))
    outs = [pl.BlockSpec((1, 2, n, 3, shard_len, cols), head_index(nz)) for n in (2, 1)]
    shapes = [jax.ShapeDtypeStruct((nz, 2, n, 3, shard_len, cols), BF16) for n in (2, 1)]
    half = (tokens, width // 2)
    rows = pl.BlockSpec((shard_len, 128), lambda i, pos, _: (pos[2] * 2 + pos[3], 0))
    return pl.pallas_call(proj_kernel, grid_spec=pltpu.PrefetchScalarGridSpec(num_scalar_prefetch=2, grid=(nz,), in_specs=[whole(a.shape) for a in (x, gains, shifts)] + [rows] * 2 + [whole(a.shape) for a in start_table] + [piece] * 8, out_specs=outs + [whole(half)] * 2, scratch_shapes=[pltpu.VMEM((tokens, width), BF16), pltpu.VMEM((tokens, 128), F32), pltpu.VMEM((tokens, 128), F32)]), out_shape=shapes + [jax.ShapeDtypeStruct(half, BF16)] * 2, compiler_params=params(), cost_estimate=cost(2 * tokens * width * 3 * nz * 2 * cols, 12000000.0), name='project')(pos, starts, x, gains, shifts, *table, *start_table, *[p for pair in pieces for p in pair])

def head_mask(shape, head):
    lane = lax.broadcasted_iota(jnp.int32, shape, 1)
    return lane < HD if head == 0 else lane >= HD

def attend_kernel(first, starts, got, out, lse_out):
    micro = first + pl.program_id(0)
    shards_n, _, count, lanes = got.shape
    seq_len = shards_n * count
    block = min(256, seq_len)
    q_all = (got[:, 0] * 0.125).reshape(seq_len, lanes)
    k_all = got[:, 1].reshape(seq_len, lanes)
    v_all = got[:, 2].reshape(seq_len, lanes)
    per = block // count
    for start in range(0, seq_len, block):
        end = start + block
        qb = q_all[start:end]
        key = lax.broadcasted_iota(jnp.int32, (block, end), 1)
        query = start + lax.broadcasted_iota(jnp.int32, (block, end), 0)
        begin = begin_of(start + lax.broadcasted_iota(jnp.int32, (block, 1), 0), starts, 4 * micro)
        allowed = (key <= query) & (key >= begin)
        results = []
        for head in range(2):
            mask = head_mask(qb.shape, head)
            scores = dot_nt(jnp.where(mask, qb, 0), k_all[:end])
            scores = jnp.where(allowed, scores, -1e+30)
            peak = jnp.max(scores, axis=-1, keepdims=True)
            e = jnp.exp(scores - peak)
            total = jnp.sum(e, axis=-1, keepdims=True)
            results.append(dot(e.astype(BF16), v_all[:end]) / total)
            lse = jnp.broadcast_to(peak + jnp.log(total), (block, 128))
            lse_out[head:head + 1, start:end] = jnp.transpose(lse)[0:1]
        mixed = jnp.where(head_mask(results[0].shape, 0), results[0], results[1]).astype(BF16)
        out[start // count:end // count] = mixed.reshape(per, count, lanes)

def call_attend(first, starts, got):
    parts, number, _, count, lanes = got.shape
    seq_len = parts * count
    return pl.pallas_call(functools.partial(attend_kernel, first), grid_spec=pltpu.PrefetchScalarGridSpec(num_scalar_prefetch=1, grid=(number,), in_specs=[pl.BlockSpec((parts, None, 3, count, lanes), lambda i, _: (0, i, 0, 0, 0))], out_specs=[pl.BlockSpec((parts, None, count, lanes), lambda i, _: (0, i, 0, 0)), pl.BlockSpec((None, 8, seq_len), lambda i, _: (i, 0, 0))]), out_shape=[jax.ShapeDtypeStruct((parts, number, count, lanes), BF16), jax.ShapeDtypeStruct((number, 8, seq_len), F32)], compiler_params=params(), cost_estimate=cost(number * 8 * seq_len * seq_len * lanes, number * 2000000.0, number * 2 * seq_len * seq_len), name='attend')(starts, got)

def attend_back_kernel(first, starts, tcos, tsin, start_cos, start_sin, got, grad, att, lse, out, dq_ref, dk_ref, dv_ref):
    micro = first + pl.program_id(0)
    shards_n, _, count, lanes = got.shape
    seq_len = shards_n * count
    block = min(256, seq_len)
    q_all = (got[:, 0] * 0.125).reshape(seq_len, lanes)
    k_all = got[:, 1].reshape(seq_len, lanes)
    v_all = got[:, 2].reshape(seq_len, lanes)
    do_all = grad[...].reshape(seq_len, lanes)
    prod = do_all.astype(F32) * att[...].reshape(seq_len, lanes).astype(F32)
    prod = jnp.transpose(prod)
    deltas = [jnp.sum(prod[:HD], axis=0, keepdims=True), jnp.sum(prod[HD:], axis=0, keepdims=True)]
    begins = begin_of(lax.broadcasted_iota(jnp.int32, (1, seq_len), 1), starts, 4 * micro)
    for start in range(0, seq_len, block):
        end = start + block
        kb, vb = (k_all[start:end], v_all[start:end])
        qs, dos = (q_all[start:], do_all[start:])
        span = seq_len - start
        key = start + lax.broadcasted_iota(jnp.int32, (block, span), 0)
        query = start + lax.broadcasted_iota(jnp.int32, (block, span), 1)
        allowed = (key <= query) & (key >= begins[:, start:])
        dks, dvs, dqs = ([], [], [])
        for head in range(2):
            mask = head_mask(kb.shape, head)
            scores = dot_nt(jnp.where(mask, kb, 0), qs)
            soft = jnp.exp(jnp.where(allowed, scores, -1e+30) - lse[head:head + 1, start:])
            pull = dot_nt(jnp.where(mask, vb, 0), dos)
            ds = (soft * (pull - deltas[head][:, start:])).astype(BF16)
            dvs.append(dot(soft.astype(BF16), dos))
            dks.append(dot(ds, qs))
            dqs.append(lax.dot_general(ds, kb, (((0,), (0,)), ((), ())), preferred_element_type=F32))
        low = head_mask(kb.shape, 0)
        dk_ref[start:end] = jnp.where(low, dks[0], dks[1])
        dv_ref[start:end] = jnp.where(low, dvs[0], dvs[1])
        dq = jnp.where(head_mask(dqs[0].shape, 0), dqs[0], dqs[1])
        if start == 0:
            dq_ref[...] = dq
        else:
            dq_ref[start:] += dq
    rows = lax.broadcasted_iota(jnp.int32, (seq_len, lanes), 0)
    cos, sin = angle_rows(rows, starts, 4 * micro, (tcos[...], tsin[...]), start_cos.at[micro], start_sin.at[micro])
    for kind, ref in enumerate((dq_ref, dk_ref, dv_ref)):
        u = ref[...]
        if kind == 0:
            u = u * 0.125
        if kind < 2:
            u = u * cos - swap_halves(u) * sin
        out[:, kind] = u.astype(BF16).reshape(shards_n, count, lanes)

def call_attend_back(first, starts, table, start_table, got, grads, att, lse):
    parts, number, _, count, lanes = got.shape
    seq_len = parts * count
    return pl.pallas_call(functools.partial(attend_back_kernel, first), grid_spec=pltpu.PrefetchScalarGridSpec(num_scalar_prefetch=1, grid=(number,), in_specs=[whole(a.shape) for a in (*table, *start_table)] + [pl.BlockSpec((parts, None, 3, count, lanes), lambda i, _: (0, i, 0, 0, 0)), pl.BlockSpec((parts, None, count, lanes), lambda i, _: (0, first + i, 0, 0)), pl.BlockSpec((parts, None, count, lanes), lambda i, _: (0, i, 0, 0)), pl.BlockSpec((None, 8, seq_len), lambda i, _: (i, 0, 0))], out_specs=pl.BlockSpec((parts, None, 3, count, lanes), lambda i, _: (0, i, 0, 0, 0)), scratch_shapes=[pltpu.VMEM((seq_len, lanes), F32)] * 3), out_shape=jax.ShapeDtypeStruct((parts, number, 3, count, lanes), BF16), compiler_params=params(), cost_estimate=cost(number * 20 * seq_len * seq_len * lanes, number * 4000000.0, number * 2 * seq_len * seq_len), name='attend_back')(starts, *table, *start_table, got, grads, att, lse)

def mix_block(mixes, q, k):
    return jnp.concatenate([mixes[q][0][k], mixes[q][1][k]], 0)

def add_into(ref, cols, first, value):

    @pl.when(first)
    def _():
        ref[:, cols] = value

    @pl.when(jnp.logical_not(first))
    def _():
        ref[:, cols] += value

def layer_kernel(pos, *refs):
    att = [refs[0].at[:, 0], refs[0].at[:, 1], refs[1].at[:, 0]]
    x, cot, gains, shifts = refs[2:6]
    ups = [refs[6 + 2 * q:8 + 2 * q] for q in range(4)]
    downs = [refs[14 + 2 * q:16 + 2 * q] for q in range(4)]
    mixes = [refs[22 + 2 * q:24 + 2 * q] for q in range(4)]
    outputs, att_all, act, slope, keep, send, xhat1, scale1, xhat2, scale2, sums = refs[30:41]
    normed, hidden, total = refs[41:44]
    nz = mixes[0][0].shape[0]
    count = refs[0].shape[2]
    part = downs[0][0].shape[2]
    step = pl.program_id(0)

    def hand_out(index, value):
        keep[index] = value[:, :2 * part]
        send[index] = value[:, 2 * part:]

    @pl.when(step == 0)
    def _():
        for k in range(nz):
            for dx in range(2):
                place = ring_place(pos, k, nz) * 2 + lax.bitwise_xor(pos[3], dx)
                for m in range(3):
                    at = (k * 2 + dx) * 128
                    att_all[m * count:(m + 1) * count, at:at + 128] = att[m][place]
        for q in range(4):
            acc = None
            for k in range(nz):
                term = dot(att_all[:, k * 256:(k + 1) * 256], mix_block(mixes, q, k))
                acc = term if acc is None else acc + term
            total[:, q * part:(q + 1) * part] = acc
        xhat, scale = row_stats(total[...])
        xhat1[...] = xhat.astype(xhat1.dtype)
        scale1[...] = jnp.broadcast_to(scale, scale1.shape)
        value = load_columns(x, pos, part).astype(F32) + xhat * gains[1:2] + shifts[1:2]
        hidden[...] = value
        xhat, scale = row_stats(value)
        xhat2[...] = xhat.astype(xhat2.dtype)
        scale2[...] = jnp.broadcast_to(scale, scale2.shape)
        value = (xhat * gains[2:3] + shifts[2:3]).astype(BF16)
        normed[...] = value
        hand_out(0, value)
    for dx in range(2):
        u = None
        for q in range(4):
            term = dot(normed[:, q * part:(q + 1) * part], ups[q][dx][...])
            u = term if u is None else u + term
        square = u * u
        t = jnp.tanh(GELU_A * (u * (1.0 + GELU_B * square)))
        half = 0.5 * (1.0 + t)
        act[0, dx] = (u * half).astype(BF16)
        bend = half + 0.5 * GELU_A * u * (1.0 - t * t) * (1.0 + 3.0 * GELU_B * square)
        slope[0, dx] = bend.astype(BF16)
    for q in range(4):
        term = dot(act[0, 0], downs[q][0][0]) + dot(act[0, 1], downs[q][1][0])
        add_into(total, slice(q * part, (q + 1) * part), step == 0, term)

    @pl.when(step == nz - 1)
    def _():
        xhat, scale = row_stats(total[...])
        value = hidden[...] + xhat * gains[3:4] + shifts[3:4]
        store_columns(outputs, value, pos, part)
        grad = load_columns(cot, pos, part).astype(F32)
        sums[0:1] = column_sum(grad * xhat)
        sums[1:2] = column_sum(grad)
        hand_out(1, row_pull(grad, xhat, scale, gains[3:4]).astype(BF16))

def layer_specs(units, part, rows, nz, order):

    def up_spec(dy, dx):

        def index(i, pos):
            place = lax.bitwise_xor(pos[0], dy) * 2 + lax.bitwise_xor(pos[3], dx)
            return (place, ring_place(pos, order(i), nz), 0, 0)
        return pl.BlockSpec((None, None, part, units), index)
    ups = [up_spec(dy, dx) for _ in range(2) for dy in range(2) for dx in range(2)]
    down = pl.BlockSpec((1, units, part), lambda i, pos: (order(i), 0, 0))
    mix = pl.BlockSpec((nz, rows, part), lambda i, pos: (0, units // rows, 0))
    return ups + [down] * 8 + [mix] * 8

def layer_weights(ups, mixes):
    mixes_flat = [p for pair in mixes for p in pair]
    return [ups[0]] * 4 + [ups[1]] * 4 + mixes_flat * 2

def call_layer(pos, att, x, cot, gains, shifts, ups, mixes):
    tokens, width = x.shape
    _, nz, part, units = ups[0].shape
    rows = mixes[0][0].shape[1] - units
    act = pl.BlockSpec((1, 2, tokens, units), lambda i, pos: (i, 0, 0, 0))
    flat, column = ((tokens, width), (tokens, 128))
    side = (2, tokens, width // 2)
    ffn = jax.ShapeDtypeStruct((nz, 2, tokens, units), BF16)
    low = jax.ShapeDtypeStruct(flat, BF16)
    return pl.pallas_call(layer_kernel, grid_spec=pltpu.PrefetchScalarGridSpec(num_scalar_prefetch=1, grid=(nz,), in_specs=[whole(a.shape) for a in (*att, x, cot, gains, shifts)] + layer_specs(units, part, rows, nz, lambda i: i), out_specs=[whole(flat)] * 2 + [act] * 2 + [whole(side)] * 2 + [whole(flat), whole(column)] * 2 + [whole((8, width))], scratch_shapes=[pltpu.VMEM(flat, BF16), pltpu.VMEM(flat, F32), pltpu.VMEM(flat, F32)]), out_shape=[low, low, ffn, ffn] + [jax.ShapeDtypeStruct(side, BF16)] * 2 + [jax.ShapeDtypeStruct(flat, BF16), jax.ShapeDtypeStruct(column, F32)] * 2 + [jax.ShapeDtypeStruct((8, width), F32)], compiler_params=params(), cost_estimate=cost(2 * tokens * width * (2 * nz * 2 * units + width), 40000000.0, tokens * nz * 2 * units), name='layer')(pos, *att, x, cot, gains, shifts, *layer_weights(ups, mixes))

def layer_back_kernel(pos, *refs):
    cot, gains, xhat1, scale1, xhat2, scale2, slope, keep, send = refs[0:9]
    ups = [refs[9 + 2 * q:11 + 2 * q] for q in range(4)]
    downs = [refs[17 + 2 * q:19 + 2 * q] for q in range(4)]
    mixes = [refs[25 + 2 * q:27 + 2 * q] for q in range(4)]
    g_up, keep_out, send_out, g_hidden, g_att, sums, total = refs[33:40]
    nz = mixes[0][0].shape[0]
    count = g_att.shape[2]
    part = downs[0][0].shape[2]
    step = pl.program_id(0)
    g_b2 = [keep[1, :, :part], keep[1, :, part:], send[1, :, :part], send[1, :, part:]]
    for dx in range(2):
        g = None
        for q in range(4):
            term = dot_nt(g_b2[q], downs[q][dx][0])
            g = term if g is None else g + term
        g_up[0, dx] = (g * slope[0, dx].astype(F32)).astype(BF16)
    for q in range(4):
        term = dot_nt(g_up[0, 0], ups[q][0][...]) + dot_nt(g_up[0, 1], ups[q][1][...])
        add_into(total, slice(q * part, (q + 1) * part), step == 0, term)

    @pl.when(step == nz - 1)
    def _():
        grad = total[...]
        xhat = xhat2[...].astype(F32)
        sums[1:2] = column_sum(grad * xhat)
        sums[3:4] = column_sum(grad)
        grad = load_columns(cot, pos, part).astype(F32) + row_pull(grad, xhat, scale2[:, 0:1], gains[2:3])
        g_hidden[...] = grad
        xhat = xhat1[...].astype(F32)
        sums[0:1] = column_sum(grad * xhat)
        sums[2:3] = column_sum(grad)
        g_b1 = row_pull(grad, xhat, scale1[:, 0:1], gains[1:2]).astype(BF16)
        keep_out[...] = g_b1[:, :2 * part]
        send_out[...] = g_b1[:, 2 * part:]
        for k in range(nz):
            acc = None
            for q in range(4):
                term = dot_nt(g_b1[:, q * part:(q + 1) * part], mix_block(mixes, q, k))
                acc = term if acc is None else acc + term
            acc = acc.astype(BF16)
            for dx in range(2):
                place = ring_place(pos, k, nz) * 2 + lax.bitwise_xor(pos[3], dx)
                for m in range(3):
                    g_att[place, m] = acc[m * count:(m + 1) * count, dx * 128:(dx + 1) * 128]

def call_layer_back(pos, cot, gains, kept, slope, keep, send, ups, mixes, count):
    tokens, width = cot.shape
    _, nz, part, units = ups[0].shape
    rows = mixes[0][0].shape[1] - units
    turn = nz - 1
    act = pl.BlockSpec((1, 2, tokens, units), lambda i, pos: (turn - i, 0, 0, 0))
    flat, half = ((tokens, width), (tokens, width // 2))
    heads = (2 * nz, tokens // count, count, rows)
    return pl.pallas_call(layer_back_kernel, grid_spec=pltpu.PrefetchScalarGridSpec(num_scalar_prefetch=1, grid=(nz,), in_specs=[whole(a.shape) for a in (cot, gains, *kept)] + [act, whole(keep.shape), whole(send.shape)] + layer_specs(units, part, rows, nz, lambda i: turn - i), out_specs=[act] + [whole(v) for v in (half, half, flat, heads, (8, width))], scratch_shapes=[pltpu.VMEM(flat, F32)]), out_shape=[jax.ShapeDtypeStruct(slope.shape, BF16), jax.ShapeDtypeStruct(half, BF16), jax.ShapeDtypeStruct(half, BF16), jax.ShapeDtypeStruct(flat, F32), jax.ShapeDtypeStruct(heads, BF16), jax.ShapeDtypeStruct((8, width), F32)], compiler_params=params(), cost_estimate=cost(2 * tokens * width * (2 * nz * 2 * units + width), 40000000.0), name='layer_back')(pos, cot, gains, *kept, slope, keep, send, *layer_weights(ups, mixes))

def place_piece(outs, dy, dx, cut, index, value):
    if dy == 0 and dx == 0:
        outs[0][index] = value
        return
    if cut is None:
        outs[2 * dy + dx][index] = value
        return
    low, high = outs[1 + 2 * (2 * dy + dx - 1):][:2]
    step = pl.program_id(0)

    @pl.when(step < cut)
    def _():
        low[index] = value

    @pl.when(step >= cut)
    def _():
        high[index] = value

def piece_specs(block, nz, cut):
    zeros = (0,) * (len(block) - 1)
    if cut is None:
        spec = pl.BlockSpec(block, lambda i, *_: (i,) + zeros)
        return ([spec] * 4, [jax.ShapeDtypeStruct((nz,) + block[1:], BF16)] * 4)
    low = pl.BlockSpec(block, lambda i, *_: (jnp.minimum(i, cut - 1),) + zeros)
    high = pl.BlockSpec(block, lambda i, *_: (jnp.maximum(i - cut, 0),) + zeros)
    specs = [pl.BlockSpec(block, lambda i, *_: (i,) + zeros)] + [low, high] * 3
    shapes = [nz] + [cut, nz - cut] * 3
    return (specs, [jax.ShapeDtypeStruct((n,) + block[1:], BF16) for n in shapes])

def down_grad_kernel(pos, act, act2, keep, recv, out):
    part = out.shape[3]
    for dx in range(2):
        side = jnp.concatenate([jnp.transpose(act[0, dx]), jnp.transpose(act2[0, dx])], 1)
        for dy in range(2):
            cols = slice(dy * part, (dy + 1) * part)
            grad = jnp.concatenate([keep[0, :, cols], recv[0, :, cols]], 0)
            place = lax.bitwise_xor(pos[0], dy) * 2 + lax.bitwise_xor(pos[3], dx)
            out[place, 0] = dot(side, grad).astype(BF16)

def call_down_grad(pos, act, act2, keep, recv):
    nz, _, tokens, units = act.shape
    half = keep.shape[2]
    part = half // 2
    ffn = pl.BlockSpec((1, 2, tokens, units), lambda i, pos: (i, 0, 0, 0))
    side = pl.BlockSpec((1, tokens, half), lambda i, pos: (1, 0, 0))
    return pl.pallas_call(down_grad_kernel, grid_spec=pltpu.PrefetchScalarGridSpec(num_scalar_prefetch=1, grid=(nz,), in_specs=[ffn, ffn, side, side], out_specs=pl.BlockSpec((4, 1, units, part), lambda i, pos: (0, ring_place(pos, i, nz), 0, 0))), out_shape=jax.ShapeDtypeStruct((4, nz, units, part), BF16), compiler_params=params(), cost_estimate=cost(2 * tokens * 2 * half * nz * 2 * units, 16000000.0), name='down_grad')(pos, act, act2, keep, recv)

def up_grad_kernel(cut, g_up, g_up2, keep, recv, keep1, recv1, att, att2, *refs):
    outs, flipped = (refs[:-1], refs[-1])
    part, units = (g_up.shape[3] // 2, g_up.shape[3])
    tokens = g_up.shape[2]

    @pl.when(pl.program_id(0) == 0)
    def _():
        flipped[:, :tokens] = jnp.transpose(keep[0])
        flipped[:, tokens:] = jnp.transpose(recv[0])
    side = jnp.concatenate([jnp.transpose(att[...]), jnp.transpose(att2[...])], 1)
    for dy in range(2):
        cols = slice(dy * part, (dy + 1) * part)
        both = dot(side, jnp.concatenate([keep1[:, cols], recv1[:, cols]], 0)).astype(BF16)
        for dx in range(2):
            grad = jnp.concatenate([g_up[0, dx], g_up2[0, dx]], 0)
            value = dot(flipped[cols], grad).astype(BF16)
            rows = both[dx * 128:(dx + 1) * 128]
            rows = jnp.concatenate([rows[:64], rows[64:]], 1)
            place_piece(outs, dy, dx, cut, 0, jnp.concatenate([value, rows], 0))

def call_up_grad(cut, g_up, g_up2, keep, recv, keep1, recv1, att, att2):
    nz, _, tokens, units = g_up.shape
    half = keep.shape[2]
    part = half // 2
    heads = att.shape[1] // nz
    ffn = pl.BlockSpec((1, 2, tokens, units), lambda i: (i, 0, 0, 0))
    side = pl.BlockSpec((1, tokens, half), lambda i: (0, 0, 0))
    head = pl.BlockSpec((tokens, heads), lambda i: (0, i))
    specs, shapes = piece_specs((1, part + heads // 4, units), nz, cut)
    return pl.pallas_call(functools.partial(up_grad_kernel, cut), grid=(nz,), in_specs=[ffn, ffn, side, side, whole(keep1.shape), whole(keep1.shape), head, head], out_specs=specs, out_shape=shapes, scratch_shapes=[pltpu.VMEM((half, 2 * tokens), BF16)], compiler_params=params(), cost_estimate=cost(2 * tokens * 2 * half * nz * 2 * units, 16000000.0), name='up_grad')(g_up, g_up2, keep, recv, keep1, recv1, att, att2)

def load_grads(pos, grads):
    columns = []
    for dx in range(2):
        place = lax.bitwise_xor(pos[3], dx)
        for kind in range(3):
            rows = [g[0, place, m, kind] for g in grads for m in range(g.shape[2])]
            columns.append(jnp.concatenate(rows, 0))
    return jnp.concatenate(columns, 1)

def qkv_grad_kernel(cut, pos, *refs):
    grads, keep, recv = (refs[0:4], refs[4], refs[5])
    outs, flipped = (refs[6:-1], refs[-1])
    part = outs[0].shape[2]
    tokens = keep.shape[0]

    @pl.when(pl.program_id(0) == 0)
    def _():
        flipped[:, :tokens] = jnp.transpose(keep[...])
        flipped[:, tokens:] = jnp.transpose(recv[...])
    block = load_grads(pos, grads)
    for dy in range(2):
        res = dot(flipped[dy * part:(dy + 1) * part], block).astype(BF16)
        for dx in range(2):
            for kind in range(3):
                at = (dx * 3 + kind) * 128
                place_piece(outs, dy, dx, cut, (0, kind), res[:, at:at + 128])

def call_qkv_grad(cut, pos, grads, grads2, keep, recv):
    nz, _, _, _, count, cols = grads[0].shape
    tokens, half = keep.shape
    part = half // 2
    grad_specs = [pl.BlockSpec((1,) + g.shape[1:], head_index(nz)) for g in grads]
    specs, shapes = piece_specs((1, 3, part, cols), nz, cut)
    return pl.pallas_call(functools.partial(qkv_grad_kernel, cut), grid_spec=pltpu.PrefetchScalarGridSpec(num_scalar_prefetch=1, grid=(nz,), in_specs=grad_specs * 2 + [whole(keep.shape)] * 2, out_specs=specs, scratch_shapes=[pltpu.VMEM((half, 2 * tokens), BF16)]), out_shape=shapes, compiler_params=params(), cost_estimate=cost(2 * tokens * 2 * half * 3 * nz * 2 * cols, 12000000.0), name='qkv_grad')(pos, *grads, *grads2, keep, recv)

def input_grad_kernel(pos, *refs):
    grads, x, gains, g_hidden = (refs[0:2], refs[2], refs[3], refs[4])
    weights = [refs[5 + 2 * q:7 + 2 * q] for q in range(4)]
    out, sums, total = refs[13:16]
    part = weights[0][0].shape[2]
    step = pl.program_id(0)
    block = load_grads(pos, grads)
    for q in range(4):
        side = jnp.concatenate([weights[q][dx][0, kind] for dx in range(2) for kind in range(3)], 1)
        term = dot_nt(block, side)

        @pl.when(step == 0)
        def _():
            total[:, q * part:(q + 1) * part] = term

        @pl.when(step > 0)
        def _():
            total[:, q * part:(q + 1) * part] += term

    @pl.when(step == pl.num_programs(0) - 1)
    def _():
        grad = total[...]
        xhat, scale = row_stats(load_columns(x, pos, part).astype(F32))
        sums[0:1] = column_sum(grad * xhat)
        sums[1:2] = column_sum(grad)
        value = g_hidden[...] + row_pull(grad, xhat, scale, gains[0:1])
        store_columns(out, value, pos, part)

def call_input_grad(pos, grads, x, gains, g_hidden, pieces):
    nz, _, _, _, count, cols = grads[0].shape
    tokens, width = x.shape
    part = width // 4
    grad_specs = [pl.BlockSpec((1,) + g.shape[1:], head_index(nz)) for g in grads]
    piece = pl.BlockSpec((1, 3, part, cols), lambda i, pos: (i, 0, 0, 0))
    return pl.pallas_call(input_grad_kernel, grid_spec=pltpu.PrefetchScalarGridSpec(num_scalar_prefetch=1, grid=(nz,), in_specs=grad_specs + [whole(a.shape) for a in (x, gains, g_hidden)] + [piece] * 8, out_specs=[whole((tokens, width)), whole((8, width))], scratch_shapes=[pltpu.VMEM((tokens, width), F32)]), out_shape=[jax.ShapeDtypeStruct((tokens, width), F32), jax.ShapeDtypeStruct((8, width), F32)], compiler_params=params(), cost_estimate=cost(2 * tokens * width * 3 * nz * 2 * cols, 16000000.0), name='input_grad')(pos, *grads, x, gains, g_hidden, *[p for pair in pieces for p in pair])

def sum_kernel(*refs):
    total = refs[0][...].astype(F32)
    for ref in refs[1:-1]:
        total = total + ref[...].astype(F32)
    refs[-1][...] = total.astype(BF16)

def add(*values):
    shape = values[0].shape
    block = pl.BlockSpec((1,) + shape[1:], lambda i: (i,) + (0,) * (len(shape) - 1))
    return pl.pallas_call(sum_kernel, grid=(shape[0],), in_specs=[block] * len(values), out_specs=block, out_shape=jax.ShapeDtypeStruct(shape, BF16), compiler_params=params(), cost_estimate=cost(values[0].size * len(values), 2 * values[0].size * (len(values) + 1)), name='add')(*values)

def sum_cut_kernel(cut, pos, mine, low_x, high_x, low_y, high_y, out):
    step = pl.program_id(0)

    @pl.when(step < cut)
    def _():
        total = mine[...].astype(F32) + low_x[...].astype(F32) + low_y[...].astype(F32)
        out[...] = total.astype(BF16)

    @pl.when(step >= cut)
    def _():
        total = mine[...].astype(F32) + high_x[...].astype(F32) + high_y[...].astype(F32)
        out[...] = total.astype(BF16)

def sum_ring_kernel(pos, *refs):
    sum_kernel(*refs)

def send_direct(parts):
    corner = lax.ppermute(parts[3], ('y', 'x'), [(i, 3 - i) for i in range(4)])
    return (corner, swap(parts[1], 'x'), swap(parts[2], 'y'))

def add_direct(pos, values):
    shape = values[0].shape
    nz = shape[0]
    block = (1,) + shape[1:]
    zeros = (0,) * (len(block) - 1)
    return pl.pallas_call(sum_ring_kernel, grid_spec=pltpu.PrefetchScalarGridSpec(num_scalar_prefetch=1, grid=(nz,), in_specs=[pl.BlockSpec(block, lambda i, pos: (i,) + zeros)] * len(values), out_specs=pl.BlockSpec(block, lambda i, pos: (ring_place(pos, i, nz),) + zeros)), out_shape=jax.ShapeDtypeStruct(shape, BF16), compiler_params=params(), cost_estimate=cost(values[0].size * 4, 10 * values[0].size), name='add_direct')(pos, *values)

def add_sides(cut, pos, mine, sides, ordered=True):
    nz = mine.shape[0]
    block = (1,) + mine.shape[1:]
    specs, _ = piece_specs(block, nz, cut)
    zeros = (0,) * (len(block) - 1)
    return pl.pallas_call(functools.partial(sum_cut_kernel, cut), grid_spec=pltpu.PrefetchScalarGridSpec(num_scalar_prefetch=1, grid=(nz,), in_specs=specs[:5], out_specs=pl.BlockSpec(block, lambda i, pos: (ring_place(pos, i, nz) if ordered else i,) + zeros)), out_shape=jax.ShapeDtypeStruct(mine.shape, BF16), compiler_params=params(), cost_estimate=cost(mine.size * 2, 8 * mine.size), name='add_sides')(pos, mine, *sides)

def after(values, *others):
    return lax.optimization_barrier((values, others))[0]

def swap(values, axis):
    return lax.ppermute(values, axis, SWAP)

def ring(values, step, size):
    return lax.ppermute(values, 'z', [(i, (i + step) % size) for i in range(size)])

def gather_sides(mine):
    return (swap(mine, 'x'), swap(mine, 'y'))

def gather_corner(over_x, over_y, cut):
    return jnp.concatenate([swap(over_x[:cut], 'y'), swap(over_y[cut:], 'x')])

def pair_up(mine, over_x, over_y, corner):
    return [[mine, over_x], [over_y, corner]]

def send_corner(parts):
    return (swap(parts[5], 'y'), swap(parts[6], 'x'))

def add_pair_kernel(a, b, c, d, first, second):
    first[...] = (a[...].astype(F32) + b[...].astype(F32)).astype(BF16)
    second[...] = (c[...].astype(F32) + d[...].astype(F32)).astype(BF16)

def corner_sums(parts, corner):
    if parts[1].shape != parts[4].shape:
        return (add(parts[1], corner[0]), add(parts[4], corner[1]))
    shape = parts[1].shape
    block = pl.BlockSpec((1,) + shape[1:], lambda i: (i,) + (0,) * (len(shape) - 1))
    return pl.pallas_call(add_pair_kernel, grid=(shape[0],), in_specs=[block] * 4, out_specs=[block] * 2, out_shape=[jax.ShapeDtypeStruct(shape, BF16)] * 2, compiler_params=params(), cost_estimate=cost(parts[1].size * 4, parts[1].size * 12), name='add_pair')(parts[1], corner[0], parts[4], corner[1])

def send_sides(parts, sums):
    high_x, low_y = after((parts[2], parts[3]), sums)
    return (swap(sums[0], 'x'), swap(high_x, 'x'), swap(low_y, 'y'), swap(sums[1], 'y'))

def plane_norms(sums, part):
    pieces = [sums[:, q * part:(q + 1) * part] for q in range(4)]
    low, high = (pieces[dy] + swap(pieces[2 + dy], 'c') for dy in range(2))
    mine = low + swap(high, 'y')
    return mine + swap(mine, 'x')

def line_norms(mine):
    mine = mine + lax.ppermute(mine, 'z', [(i, i ^ 1) for i in range(4)])
    return mine + lax.ppermute(mine, 'z', [(i, i ^ 2) for i in range(4)])

def fast_shards(inputs, doc_starts, w_qkv, w_out, w_up, w_down, norm_gains, norm_biases, cotangent):
    pos = jnp.stack([lax.axis_index(name) for name in ('y', 'c', 'z', 'x')]).astype(jnp.int32)
    nz = lax.axis_size('z')
    parts = nz * 2
    micro, _, shard_len, width = inputs.shape
    tokens = micro * shard_len
    seq_len = shard_len * parts
    part = width // 4
    cols = w_qkv.shape[2]
    half = nz // 2
    starts = doc_starts.reshape(-1)
    x = inputs.reshape(tokens, width)
    cot = cotangent.reshape(tokens, width)

    def exchange(values):
        return lax.all_to_all(values, SEQ, 0, 0, tiled=True)
    rings = [ring(w_qkv, nz - k, nz) for k in range(1, nz)]
    norms = jnp.concatenate([norm_gains, norm_biases])
    norms_y, norms_c = (swap(norms, 'y'), swap(norms, 'c'))
    norms = jnp.concatenate([norms, norms_y, norms_c, swap(norms_y, 'c')], 1).astype(F32)
    gains, shifts = (norms[:4], norms[4:])
    start_table = start_tables(doc_starts[:, 0])
    table = tables(seq_len)
    mix = jnp.concatenate([w_down, w_out])
    qkv_mine, mix = after((jnp.stack([w_qkv] + rings), mix), norms, start_table)
    mix1, mix3 = (ring(after(mix, qkv_mine), k, nz) for k in (nz - 1, 1))
    qkv_sides = after(gather_sides(qkv_mine), mix1, mix3)
    mix2 = ring(after(mix, qkv_sides), nz - 2, nz)
    qkv_corner = gather_corner(*qkv_sides, half)
    qkv_other = [swap(p, 'c') for p in (qkv_mine, *qkv_sides)]
    qkv_corner = after(qkv_corner, qkv_other)
    up_mine = lax.all_gather(after(w_up, qkv_corner), 'z', axis=0, tiled=False)
    mix_mine = jnp.stack([mix, mix1, mix2, mix3])
    qkv_other.append(swap(qkv_corner, 'c'))
    qkv = pair_up(qkv_mine, *qkv_sides, qkv_corner) + pair_up(*qkv_other)
    first, last, keep0, send1 = call_proj(pos, starts, x, gains, shifts, table, start_table, qkv, shard_len)
    mix_mine = after(mix_mine, first)
    mix_sides = gather_sides(mix_mine)
    got = [None, None]
    got[0] = exchange(first.reshape(parts, 2, 3, shard_len, cols))
    got[1] = exchange(after(last.reshape(parts, 1, 3, shard_len, cols), got[0]))
    mix_corner = gather_corner(*mix_sides, 2)
    mix_other = [swap(p, 'c') for p in (mix_mine, *mix_sides)]
    att_local, lses, att = ([None, None], [None, None], [None, None])
    got[0] = after(got[0], mix_other, mix_corner)
    up_own = lax.all_gather(after(up_mine, got[0]), ('y', 'x'), axis=0, tiled=False)
    mix_other.append(swap(mix_corner, 'c'))
    att_local[0], lses[0] = call_attend(0, starts, got[0])
    got[1] = after(got[1], att_local[0], mix_corner)
    att[0] = exchange(att_local[0])
    att_local[1], lses[1] = call_attend(2, starts, got[1])
    att[0] = after(att[0], att_local[1], mix_other)
    att[1] = exchange(after(att_local[1], att[0]))
    mixes = pair_up(mix_mine, *mix_sides, mix_corner) + pair_up(*mix_other)
    up_own = after(up_own, att[1])
    ups = [up_own, swap(up_own, 'c')]
    res = call_layer(pos, att, x, cot, gains, shifts, ups, mixes)
    outputs, att_all, act, slope, keep, send = res[:6]
    kept, sums3 = (res[6:10], res[10])
    recv, act2, att_all2, recv0 = (swap(v, 'c') for v in (send, act, att_all, send1))
    res = call_layer_back(pos, cot, gains, kept, slope, keep, send, ups, mixes, shard_len)
    g_up, keep1, send1, g_hidden, g_att, sums = res
    back, back2 = ([None, None], [None, None])
    recv1, g_up2 = (swap(send1, 'c'), swap(g_up, 'c'))
    act2 = after(act2, g_up)
    down_parts = call_down_grad(pos, act, act2, keep, recv)
    down_sum = lax.psum_scatter(down_parts, ('y', 'x'), scatter_dimension=0, tiled=True)
    down_sum = down_sum.reshape(down_parts.shape[1:])
    g_up = after(g_up, down_parts)
    grad = exchange(g_att)
    grad = after(grad, down_parts)
    res2 = call_attend_back(2, starts, table, start_table, got[1], grad, att_local[1], lses[1])
    back[1] = exchange(res2)
    grad = after(grad, res2)
    res = call_attend_back(0, starts, table, start_table, got[0], grad, att_local[0], lses[0])
    up_parts = call_up_grad(None, after(g_up, res), g_up2, keep, recv, keep1, recv1, att_all, att_all2)
    up_sent = send_direct(up_parts)
    back[1] = after(back[1], res)
    back[0] = exchange(after(res, back[1]))
    back2[1] = swap(back[1].reshape((nz, 2) + back[1].shape[1:]), 'c')
    back[0] = after(back[0], down_sum)
    down_sum = lax.psum_scatter(down_sum, 'z', scatter_dimension=0, tiled=False)
    back[0] = after(back[0], back2[1], up_parts)
    back[0] = after(back[0], up_sent[1], up_sent[2])
    back = [b.reshape((nz, 2) + b.shape[1:]) for b in back]
    back2[0] = swap(back[0], 'c')
    qkv_cut = half
    qkv_parts = call_qkv_grad(qkv_cut, pos, back, back2, keep0, recv0)
    back = after(back, qkv_parts)
    up_sent = after(up_sent, qkv_parts)
    qkv_corner = send_corner(qkv_parts)
    qkv_sums = corner_sums(qkv_parts, qkv_corner)
    qkv_sent = send_sides(qkv_parts, qkv_sums)
    inputs_grad, sums0 = call_input_grad(pos, after(back, qkv_sums), x, gains, g_hidden, qkv)
    up_sum = add_direct(pos, (up_parts[0], *up_sent))
    qkv_sent = after(qkv_sent, up_sum)
    up_sum = lax.psum_scatter(up_sum, 'z', scatter_dimension=0, tiled=False)
    norm_sums = [sums0[:1], sums[:2], sums3[:1], sums0[1:2], sums[2:4], sums3[1:2]]
    norm_sums = jnp.concatenate(norm_sums)
    qkv_sent, norm_sums = after((qkv_sent, norm_sums), norm_sums, down_sum)
    qkv_sum = add_sides(half, pos, qkv_parts[0], qkv_sent, True)
    norm_sums = line_norms(plane_norms(after(norm_sums, qkv_sum), part))
    qkv_sum = lax.psum_scatter(qkv_sum, 'z', scatter_dimension=0, tiled=False)
    down_sum = down_sum.astype(F32)
    up_sum, out_sum = (up_sum[:part].astype(F32), up_sum[part:].astype(F32))
    out_sum = jnp.concatenate([out_sum[:, :part], out_sum[:, part:]], 0)
    qkv_sum = after(qkv_sum, norm_sums, down_sum, out_sum, up_sum)
    return (outputs.reshape(inputs.shape), inputs_grad.reshape(inputs.shape), qkv_sum.astype(F32), out_sum, up_sum, down_sum, norm_sums[:4], norm_sums[4:])

def fits_fast(mesh, inputs, w_qkv, w_up):
    dp, tensor = (mesh.shape['dp'], mesh.shape['tensor'])
    return dp == 4 and tensor == 8 and (inputs.shape[0] == 3) and (inputs.shape[1] == dp) and (inputs.shape[2] == 1024) and (w_qkv.shape[1:] == (1024, 1024)) and (w_up.shape[1] == 4096)

def solution(mesh):
    dp, tensor = (mesh.shape['dp'], mesh.shape['tensor'])
    names = ('y', 'c', 'z', 'x')
    fine = Mesh(mesh.devices.reshape(dp // 2, 2, 4, tensor // 4), names)
    rows, seq = (('y', 'c'), ('z', 'x'))
    tokens = P(None, rows, seq, None)
    weights = (P(None, rows, seq), P(seq, rows), P(rows, seq), P(seq, rows))
    norm = P(None, rows)

    def run(*arrays):
        fast = fits_fast(mesh, arrays[0], arrays[2], arrays[4])
        return jax.shard_map(fast_shards if fast else shards, mesh=fine, in_specs=(tokens, P(None, rows, None)) + weights + (norm, norm, tokens), out_specs=(tokens, tokens) + weights + (norm, norm), check_vma=False)(*arrays)
    return run
```
